512 devices in a mesh: az: 64 (over z, x, y_hi), rad: 8 (over y_lo, core).
Axes of the slice: x: 4, y: 8 (y_hi: 2, y_lo: 4; y = y_hi * 4 + y_lo), z: 8, core: 2. Of those that a mesh axis runs over, the one named last changes fastest.
Arguments:
- fields: float32 [5, 2, 768, 16384], P(None, None, 'rad', 'az'), as said below
- shifts: int32 [768], P('rad'), may hold values from 0 to 16383, as said below
- cycle_area: float32 [768], P('rad'), may hold values from 0.5 to 2
- gravity: float32 [768], P('rad'), may hold values from 0.00013020834 to 0.0013020834
- kappa_az: float32 [768], P('rad'), may hold values from 0.05 to 0.24
- kappa_rad: float32 [768], P('rad'), may hold values from 0.05 to 0.24
Outputs:
- updated: float32 [5, 2, 768, 16384], P(None, None, 'rad', 'az')
- enclosed: float32 [768], P('rad')
The draws below stay inside these ranges and needn't reach their ends.
Inputs may be any that keep to these rules, and one draw needn't show every extreme that they name: shifts[r] is the whole number of cells by which row r moves toward higher azimuth. fields[0] is positive.
All inputs are finite; a program needn't handle non-finite values.
Results may differ from the reference program's by a relative error of at most 0.00002.
Values sent between devices are 32-bit elements; how exact they have to be, the bound alone decides.
No kernel may reach another device: no remote copies, remote signals or barrier semaphores. Data moves between devices by JAX's collectives and lax.ppermute only.
A program may use at most 64 MiB of HBM per device.

```python
import math
import jax
import jax.numpy as jnp
from jax import lax

FIELDS = 5
LAYERS = 2
NR = 768
NA = 16384


def draw_fields(key, part):
    key = jax.random.fold_in(key, 7)
    key_rough, key_other = jax.random.split(key, 2)
    ramp = 1.0 + 2.0 * jnp.arange(NA, dtype=jnp.float32) / NA
    density = ramp * jax.random.uniform(key_rough, (LAYERS, NR, NA), jnp.float32, 0.5, 1.5)
    others = jax.random.normal(key_other, (FIELDS - 1, LAYERS, NR, NA), jnp.float32)
    return jnp.concatenate([density[None], others], axis=0)


def draw_shifts(key, part):
    key = jax.random.fold_in(key, 11)
    values = jax.random.randint(key, (NR,), 0, NA, jnp.int32)
    return values.at[0].set(NA - 1).at[1].set(0)


def block_scale(rng, dims, cuts, least, largest):
    def one(position, parts):
        draws = jax.random.uniform(jax.random.fold_in(jax.random.fold_in(rng, 6), position), (parts,), jnp.float32, least / len(cuts), largest / len(cuts))
        return jnp.repeat(jnp.exp(draws), dims[position] // parts).reshape((-1,) + (1,) * (len(dims) - position - 1))

    factor_of = one(*cuts[0])
    for cut in cuts[1:]:
        factor_of = factor_of * one(*cut)
    return factor_of


def setup_inputs(seed: int = 0) -> dict:
    splits = jax.random.split(jax.random.key(seed), 7)
    return {
        "fields": draw_fields(jax.random.fold_in(splits[6], 71), 0),
        "shifts": draw_shifts(jax.random.fold_in(splits[6], 71), 0),
        "cycle_area": jnp.clip(jnp.exp(math.log(2.0) - 1.3862944 * jax.random.uniform(splits[2], (NR,), jnp.float32) ** block_scale(splits[2], (NR,), ((0, 8),), -0.2, 0.2)), 0.5, 2.0),
        "gravity": jnp.clip(jnp.exp(math.log(0.0013020834) - 2.3025851 * jax.random.uniform(splits[3], (NR,), jnp.float32) ** block_scale(splits[3], (NR,), ((0, 8),), -0.2, 0.2)), 0.00013020834, 0.0013020834),
        "kappa_az": jnp.clip(0.05 + 0.19 * jax.random.uniform(splits[4], (NR,), jnp.float32) ** block_scale(splits[4], (NR,), ((0, 8),), -0.2, 0.2), 0.05, 0.24),
        "kappa_rad": jnp.clip(0.05 + 0.19 * jax.random.uniform(splits[5], (NR,), jnp.float32) ** block_scale(splits[5], (NR,), ((0, 8),), -0.2, 0.2), 0.05, 0.24),
    }


star_mass = 1.0


def shift_field(field, shifts):
    cell_index = (jnp.arange(NA, dtype=jnp.int32)[None, :] - shifts[:, None]) % NA
    cell_index = jnp.broadcast_to(cell_index[None], field.shape)
    return jnp.take_along_axis(field, cell_index, axis=2)


def reference(fields, shifts, cycle_area, gravity, kappa_az, kappa_rad):
    density = fields[0]
    row_mass = cycle_area * jnp.sum(density, axis=(0, 2)) / (2.0 * NA)
    before = jnp.cumsum(row_mass) - row_mass
    enclosed = star_mass + before + 0.5 * row_mass
    pull_rate = (gravity * enclosed)[None, :, None]
    momentum = fields[1] - pull_rate * density
    energy = fields[3] - pull_rate * fields[1]
    sourced = jnp.stack([density, momentum, fields[2], energy, fields[4]])
    advected = lax.map(lambda field: shift_field(field, shifts), sourced)
    beside_all = jnp.roll(advected, 1, axis=3) + jnp.roll(advected, -1, axis=3) - 2.0 * advected
    padded = jnp.pad(advected, ((0, 0), (0, 0), (1, 1), (0, 0)))
    across = padded[:, :, 2:] + padded[:, :, :-2] - 2.0 * advected
    updated = advected + kappa_az[None, None, :, None] * beside_all + kappa_rad[None, None, :, None] * across
    return updated, enclosed
```

```python
import jax
import jax.numpy as jnp
from jax import lax
from jax.experimental import pallas as pl
from jax.experimental.pallas import tpu as pltpu
from jax.sharding import PartitionSpec as P

star_mass = 1.0

ORDER = (0, 1, 3, 2, 4)
RING = 64
GROUPS = 3
ROWS = 96
SPAN = ROWS // GROUPS
HALF = 16
BLOCK = 2 * HALF
PIECES = 2 * RING
VMEM_LIMIT = 24 * 1024 * 1024

TILES = ((0, 1, 5), (1, 2, 2))


def iotas():
    lane = lax.broadcasted_iota(jnp.int32, (8, 128), 1)
    line = lax.broadcasted_iota(jnp.int32, (8, 128), 0)
    return lane, line


def pack_kernel(fields, packed):
    for place, field in enumerate(ORDER):
        for layer in range(2):
            for group in range(GROUPS):
                for half in range(2):
                    first = BLOCK * layer + HALF * half + 5 * group + place
                    packed[pl.ds(first, SPAN, stride=2 * BLOCK), :] = fields[
                        field, layer, pl.ds(SPAN * group, SPAN), pl.ds(128 * half, 128)
                    ]
    cells = [fields[0, z, :, pl.ds(128 * h, 128)] for z in range(2) for h in range(2)]
    total = (cells[0] + cells[1]) + (cells[2] + cells[3])
    square = jnp.concatenate([total, jnp.zeros((128 - ROWS, 128), jnp.float32)], axis=0)
    mass = jnp.sum(square.T, axis=0, keepdims=True)
    packed[pl.ds(15, RING, stride=BLOCK), :] = jnp.broadcast_to(mass, (RING, 128))
    packed[pl.ds(31, RING, stride=BLOCK), :] = jnp.zeros((RING, 128), jnp.float32)


def shift_kernel(place, shifts, lines, moved, mass):
    lane, line = iotas()
    row = place[0] >> 1
    whole, part, early = [], [], []
    for group in range(GROUPS):
        shift = shifts[SPAN * group + row]
        whole.append(shift >> 7)
        part.append(shift & 127)
        early.append(lane < part[group])

    def turned(piece, tile, group):
        at = pl.multiple_of(((piece - whole[group]) & (PIECES - 1)) * HALF + 8 * tile, 8)
        return pltpu.roll(lines[pl.ds(at, 8), :], part[group], 1)

    def one(ring, state):
        before, edges = state
        for half in range(2):
            piece = 2 * ring + half
            now, kept = [], []
            for tile, (first, second, split) in enumerate(TILES):
                a, b = turned(piece, tile, first), turned(piece, tile, second)
                pa, pb = before[tile]
                value = jnp.where(
                    line < split, jnp.where(early[first], pa, a), jnp.where(early[second], pb, b)
                )
                at = pl.multiple_of(piece * HALF + 8 * tile, 8)
                moved[pl.ds(at, 8), :] = value
                now.append((a, b))
                if half == 0:
                    owner = (ring + RING - 1) & (RING - 1)
                    slot = RING + owner
                    kept.append(jnp.where(lane == slot, pltpu.roll(value, slot, 1), edges[tile]))
                else:
                    owner = (ring + 1) & (RING - 1)
                    kept.append(jnp.where(lane == owner, pltpu.roll(value, owner + 1, 1), edges[tile]))
            before, edges = tuple(now), tuple(kept)
        return before, edges

    before = tuple(
        (turned(PIECES - 1, tile, first), turned(PIECES - 1, tile, second))
        for tile, (first, second, _) in enumerate(TILES)
    )
    zero = jnp.zeros((8, 128), jnp.float32)
    _, edges = lax.fori_loop(0, RING, one, (before, (zero, zero)), unroll=4)
    square = jnp.concatenate([edges[0], edges[1], jnp.zeros((112, 128), jnp.float32)], axis=0).T
    moved[pl.ds(15, RING, stride=BLOCK), :] = square[:RING]
    moved[pl.ds(31, RING, stride=BLOCK), :] = square[RING:]
    parts = lines[pl.ds(15, RING, stride=BLOCK), :]
    mass[...] = jnp.broadcast_to(jnp.sum(parts, axis=0, keepdims=True), (8, 128))


def spread_kernel(kappa_az, kappa_rad, pull, lines, below, above, updated, sourced, partial):
    lane, line = iotas()
    square = jnp.concatenate(
        [lines[pl.ds(15, RING, stride=BLOCK), :], lines[pl.ds(31, RING, stride=BLOCK), :]], axis=0
    ).T
    edges = (square[0:8], square[8:16])
    takes = (((line == 1) | (line == 2), (line == 6) | (line == 7)), (line < 0, (line == 3) | (line == 4)))

    def spread(values, row, tile):
        first, second, split = TILES[tile]
        return jnp.where(line < split, values[SPAN * first + row], values[SPAN * second + row])

    def source(value, rate):
        return value - rate * pltpu.roll(value, 1, 0)

    def one(row, carry):
        for tile, (first, second, _) in enumerate(TILES):
            az = spread(kappa_az, row, tile)
            rad = spread(kappa_rad, row, tile)
            rate = jnp.where(
                takes[tile][0],
                pull[SPAN * first + row + 1],
                jnp.where(takes[tile][1], pull[SPAN * second + row + 1], 0.0),
            )
            for layer in range(2):
                ring = 2 * row + layer
                base = pl.multiple_of(ring * BLOCK + 8 * tile, 8)
                low = lines[pl.ds(base, 8), :]
                high = lines[pl.ds(base + HALF, 8), :]
                low_up, high_up = pltpu.roll(low, 1, 1), pltpu.roll(high, 1, 1)
                low_down, high_down = pltpu.roll(low, 127, 1), pltpu.roll(high, 127, 1)
                left = pltpu.roll(edges[tile], (128 - ring) & 127, 1)
                right = pltpu.roll(edges[tile], 63 - ring, 1)
                sides = (
                    jnp.where(lane == 0, left, low_up) + jnp.where(lane == 127, high_down, low_down),
                    jnp.where(lane == 0, low_up, high_up) + jnp.where(lane == 127, right, high_down),
                )
                for half, value in enumerate((low, high)):
                    closed = value + az * (sides[half] - 2.0 * value)
                    full = source(value, rate)
                    sourced[pl.ds(base + 2 * BLOCK + HALF * half, 8), :] = full
                    partial[pl.ds(base + HALF * half, 8), :] = source(closed, rate) - 2.0 * rad * full
        return carry

    lax.fori_loop(0, SPAN, one, 0, unroll=2)

    for layer in range(2):
        for half in range(2):
            at = BLOCK * layer + HALF * half
            under = source(below[pl.ds(at + 8, 8), :], jnp.where(takes[1][1], pull[0], 0.0))
            over = source(above[pl.ds(at, 8), :], jnp.where(takes[0][0], pull[ROWS + 1], 0.0))
            sourced[pl.ds(at, 5), :] = under[2:7]
            sourced[pl.ds(at + 5, 10), :] = sourced[pl.ds(RING * BLOCK + at, 10), :]
            top = (RING + 2) * BLOCK + at
            sourced[pl.ds(top, 10), :] = sourced[pl.ds(2 * BLOCK + at + 5, 10), :]
            sourced[pl.ds(top + 10, 5), :] = over[0:5]

    def two(row, carry):
        for tile in range(2):
            rad = spread(kappa_rad, row, tile)
            for layer in range(2):
                for half in range(2):
                    base = pl.multiple_of((2 * row + layer) * BLOCK + HALF * half + 8 * tile, 8)
                    beside = sourced[pl.ds(base, 8), :] + sourced[pl.ds(base + 4 * BLOCK, 8), :]
                    partial[pl.ds(base, 8), :] = partial[pl.ds(base, 8), :] + rad * beside
        return carry

    lax.fori_loop(0, SPAN, two, 0, unroll=4)

    for place, field in enumerate(ORDER):
        for layer in range(2):
            for group in range(GROUPS):
                for half in range(2):
                    first = BLOCK * layer + HALF * half + 5 * group + place
                    updated[field, layer, pl.ds(SPAN * group, SPAN), pl.ds(128 * half, 128)] = partial[
                        pl.ds(first, SPAN, stride=2 * BLOCK), :
                    ]


def specs(*kinds):
    return [pl.BlockSpec(memory_space=kind) for kind in kinds]


def shards(fields, shifts, cycle_area, gravity, kappa_az, kappa_rad):
    vmem, smem = pltpu.VMEM, pltpu.SMEM
    params = pltpu.CompilerParams(vmem_limit_bytes=VMEM_LIMIT)
    blocks = jax.ShapeDtypeStruct((RING * BLOCK, 128), jnp.float32)

    def dealt(lines):
        lines = lines.reshape(RING, BLOCK, 128)
        return lax.all_to_all(lines, "az", 0, 0, tiled=True).reshape(RING * BLOCK, 128)

    packed = pl.pallas_call(
        pack_kernel,
        out_shape=blocks,
        in_specs=specs(vmem),
        out_specs=specs(vmem)[0],
        compiler_params=params,
        name="pack",
    )(fields)
    whole = dealt(packed)
    place = lax.axis_index("az").astype(jnp.int32)[None]
    moved, mass = pl.pallas_call(
        shift_kernel,
        out_shape=(blocks, jax.ShapeDtypeStruct((8, 128), jnp.float32)),
        in_specs=specs(smem, smem, vmem),
        out_specs=specs(vmem, vmem),
        compiler_params=params,
        name="shift",
    )(place, shifts, whole)
    lines = dealt(moved)

    row_mass = cycle_area * mass[0, :ROWS] / (2.0 * RING * 256)
    mine = jnp.stack([row_mass, gravity])
    everyone = lax.all_gather(mine, "rad")
    ranks = everyone.shape[0]
    masses = everyone[:, 0, :]
    totals = jnp.sum(masses, axis=1)
    rank = jnp.arange(ranks)
    offset = jnp.sum(jnp.where(rank[None, :] < rank[:, None], totals[None, :], 0.0), axis=1)
    row = jnp.arange(ROWS)
    before = jnp.sum(jnp.where(row[None, None, :] < row[None, :, None], masses[:, None, :], 0.0), axis=2)
    reach = star_mass + offset[:, None] + before + 0.5 * masses
    pulls = (everyone[:, 1, :] * reach).reshape(ranks * ROWS)
    me = lax.axis_index("rad")
    pull = lax.dynamic_slice(jnp.pad(pulls, (1, 1)), (me * ROWS,), (ROWS + 2,))
    enclosed = lax.dynamic_slice(reach.reshape(ranks * ROWS), (me * ROWS,), (ROWS,))

    up = [(i, i + 1) for i in range(ranks - 1)]
    down = [(i + 1, i) for i in range(ranks - 1)]
    below = lax.ppermute(lines[(RING - 2) * BLOCK :], "rad", up)
    above = lax.ppermute(lines[: 2 * BLOCK], "rad", down)
    updated = pl.pallas_call(
        spread_kernel,
        out_shape=jax.ShapeDtypeStruct(fields.shape, jnp.float32),
        in_specs=specs(smem, smem, smem, vmem, vmem, vmem),
        out_specs=specs(vmem)[0],
        scratch_shapes=[
            pltpu.VMEM(((RING + 4) * BLOCK, 128), jnp.float32),
            pltpu.VMEM((RING * BLOCK, 128), jnp.float32),
        ],
        compiler_params=params,
        name="spread",
    )(kappa_az, kappa_rad, pull, lines, below, above)
    return updated, enclosed


def solution(mesh):
    placed = (P(None, None, "rad", "az"), P("rad"), P("rad"), P("rad"), P("rad"), P("rad"))
    return jax.shard_map(
        shards,
        mesh=mesh,
        in_specs=placed,
        out_specs=(P(None, None, "rad", "az"), P("rad")),
        check_vma=False,
    )
```

```python
import jax
import jax.numpy as jnp
from jax import lax
from jax.experimental import pallas as pl
from jax.experimental.pallas import tpu as pltpu
from jax.sharding import PartitionSpec as P

star_mass = 1.0

ORDER = (0, 1, 3, 2, 4)
RING = 64
GROUPS = 3
ROWS = 96
SPAN = ROWS // GROUPS
HALF = 16
BLOCK = 2 * HALF
PIECES = 2 * RING
VMEM_LIMIT = 24 * 1024 * 1024

TILES = ((0, 1, 5), (1, 2, 2))


def iotas():
    lane = lax.broadcasted_iota(jnp.int32, (8, 128), 1)
    line = lax.broadcasted_iota(jnp.int32, (8, 128), 0)
    return lane, line


def windows():
    for side in range(2):
        for layer in range(2):
            for half in range(2):
                yield side, layer, half, BLOCK * (32 * side + 16 * layer + 8 * half) + 31


def pack_kernel(fields, below, above, packed):
    lane, line = iotas()
    for place, field in enumerate(ORDER):
        for layer in range(2):
            for group in range(GROUPS):
                for half in range(2):
                    first = BLOCK * layer + HALF * half + 5 * group + place
                    packed[pl.ds(first, SPAN, stride=2 * BLOCK), :] = fields[
                        field, layer, pl.ds(SPAN * group, SPAN), pl.ds(128 * half, 128)
                    ]
    cells = [fields[0, z, :, pl.ds(128 * h, 128)] for z in range(2) for h in range(2)]
    total = (cells[0] + cells[1]) + (cells[2] + cells[3])
    square = jnp.concatenate([total, jnp.zeros((128 - ROWS, 128), jnp.float32)], axis=0)
    mass = jnp.sum(square.T, axis=0, keepdims=True)
    packed[pl.ds(15, RING, stride=BLOCK), :] = jnp.broadcast_to(mass, (RING, 128))
    for side, layer, half, first in windows():
        tile = jnp.zeros((8, 128), jnp.float32)
        for place, field in enumerate(ORDER):
            cells = (below, above)[side][pl.ds(2 * field + layer, 1), pl.ds(128 * half, 128)]
            turned = pltpu.roll(jnp.broadcast_to(cells, (8, 128)), 16 * (place + 1), 1)
            for bit in (1, 2, 4):
                turned = jnp.where(line & bit == 0, turned, pltpu.roll(turned, 128 - 16 * bit, 1))
            tile = jnp.where(lane >> 4 == place + 1, turned, tile)
        packed[pl.ds(first, 8, stride=BLOCK), :] = tile


def shift_kernel(place, shifts, near, lines, moved, mass, twice):
    lane, line = iotas()
    row = place[0] >> 1
    whole, part, early = [], [], []
    for group in range(GROUPS):
        shift = shifts[SPAN * group + row]
        whole.append(shift >> 7)
        part.append(shift & 127)
        early.append(lane < part[group])

    def turned(piece, tile, group):
        at = pl.multiple_of(((piece - whole[group]) & (PIECES - 1)) * HALF + 8 * tile, 8)
        return pltpu.roll(lines[pl.ds(at, 8), :], part[group], 1)

    def one(ring, state):
        before, edges = state
        for half in range(2):
            piece = 2 * ring + half
            now, kept = [], []
            for tile, (first, second, split) in enumerate(TILES):
                a, b = turned(piece, tile, first), turned(piece, tile, second)
                pa, pb = before[tile]
                value = jnp.where(
                    line < split, jnp.where(early[first], pa, a), jnp.where(early[second], pb, b)
                )
                at = pl.multiple_of(piece * HALF + 8 * tile, 8)
                moved[pl.ds(at, 8), :] = value
                now.append((a, b))
                if half == 0:
                    owner = (ring + RING - 1) & (RING - 1)
                    slot = RING + owner
                    kept.append(jnp.where(lane == slot, pltpu.roll(value, slot, 1), edges[tile]))
                else:
                    owner = (ring + 1) & (RING - 1)
                    kept.append(jnp.where(lane == owner, pltpu.roll(value, owner + 1, 1), edges[tile]))
            before, edges = tuple(now), tuple(kept)
        return before, edges

    before = tuple(
        (turned(PIECES - 1, tile, first), turned(PIECES - 1, tile, second))
        for tile, (first, second, _) in enumerate(TILES)
    )
    zero = jnp.zeros((8, 128), jnp.float32)
    _, edges = lax.fori_loop(0, RING, one, (before, (zero, zero)), unroll=4)
    square = jnp.concatenate([edges[0], edges[1], jnp.zeros((112, 128), jnp.float32)], axis=0).T
    moved[pl.ds(15, RING, stride=BLOCK), :] = square[:RING]
    ends = lines[pl.ds(31, RING, stride=BLOCK), :]
    twice[pl.ds(0, RING), :] = ends
    twice[pl.ds(RING, RING), :] = ends
    shift = near[place[0] >> 5]
    wide = lax.broadcasted_iota(jnp.int32, (RING, 128), 1)
    crosses = (wide & 15) + 16 * (place[0] & 15) + (shift & 255) >= 256
    blocks = shift >> 8
    ends = jnp.where(crosses, twice[pl.ds(RING - 1 - blocks, RING), :], twice[pl.ds(RING - blocks, RING), :])
    moved[pl.ds(31, RING, stride=BLOCK), :] = jnp.where(wide < 16, square[RING:], ends)
    parts = lines[pl.ds(15, RING, stride=BLOCK), :]
    mass[...] = jnp.broadcast_to(jnp.sum(parts, axis=0, keepdims=True), (8, 128))


def spread_kernel(near, kappa_az, kappa_rad, pull, lines, updated, sourced, partial, ends):
    lane, line = iotas()
    square = jnp.concatenate(
        [lines[pl.ds(15, RING, stride=BLOCK), :], lines[pl.ds(31, RING, stride=BLOCK), :]], axis=0
    ).T
    edges = (square[0:8], square[8:16])
    takes = (((line == 1) | (line == 2), (line == 6) | (line == 7)), (line < 0, (line == 3) | (line == 4)))

    def spread(values, row, tile):
        first, second, split = TILES[tile]
        return jnp.where(line < split, values[SPAN * first + row], values[SPAN * second + row])

    def source(value, rate):
        return value - rate * pltpu.roll(value, 1, 0)

    def one(row, carry):
        for tile, (first, second, _) in enumerate(TILES):
            az = spread(kappa_az, row, tile)
            rad = spread(kappa_rad, row, tile)
            rate = jnp.where(
                takes[tile][0],
                pull[SPAN * first + row + 1],
                jnp.where(takes[tile][1], pull[SPAN * second + row + 1], 0.0),
            )
            for layer in range(2):
                ring = 2 * row + layer
                base = pl.multiple_of(ring * BLOCK + 8 * tile, 8)
                low = lines[pl.ds(base, 8), :]
                high = lines[pl.ds(base + HALF, 8), :]
                low_up, high_up = pltpu.roll(low, 1, 1), pltpu.roll(high, 1, 1)
                low_down, high_down = pltpu.roll(low, 127, 1), pltpu.roll(high, 127, 1)
                left = pltpu.roll(edges[tile], (128 - ring) & 127, 1)
                right = pltpu.roll(edges[tile], 63 - ring, 1)
                sides = (
                    jnp.where(lane == 0, left, low_up) + jnp.where(lane == 127, high_down, low_down),
                    jnp.where(lane == 0, low_up, high_up) + jnp.where(lane == 127, right, high_down),
                )
                for half, value in enumerate((low, high)):
                    closed = value + az * (sides[half] - 2.0 * value)
                    full = source(value, rate)
                    sourced[pl.ds(base + 2 * BLOCK + HALF * half, 8), :] = full
                    partial[pl.ds(base + HALF * half, 8), :] = source(closed, rate) - 2.0 * rad * full
        return carry

    lax.fori_loop(0, SPAN, one, 0, unroll=2)

    ends[...] = jnp.zeros(ends.shape, jnp.float32)
    for side, layer, half, first in windows():
        tile = lines[pl.ds(first, 8, stride=BLOCK), :]
        for place in range(5):
            turned = pltpu.roll(pltpu.roll(tile, 112 - 16 * place, 1), 0, 1, stride=16, stride_axis=0)
            cells = jnp.sum(jnp.where(lane >> 4 == line, turned, 0.0), axis=0, keepdims=True)
            ends[pl.ds(8 * (4 * side + 2 * layer + half) + place, 1), :] = cells
    for side in range(2):
        part, odd = near[side] & 127, near[side] & 128
        rate = jnp.where(takes[0][0], pull[(ROWS + 1) * side], 0.0)
        for layer in range(2):
            at = 8 * (4 * side + 2 * layer)
            low = pltpu.roll(ends[pl.ds(at, 8), :], part, 1)
            high = pltpu.roll(ends[pl.ds(at + 8, 8), :], part, 1)
            even = jnp.where(lane < part, high, low), jnp.where(lane < part, low, high)
            for half in range(2):
                row = BLOCK * layer + HALF * half
                full = source(jnp.where(odd == 0, even[half], even[1 - half]), rate)
                if side == 0:
                    sourced[pl.ds(row, 5), :] = full[0:5]
                    sourced[pl.ds(row + 5, 10), :] = sourced[pl.ds(RING * BLOCK + row, 10), :]
                else:
                    top = (RING + 2) * BLOCK + row
                    sourced[pl.ds(top, 10), :] = sourced[pl.ds(2 * BLOCK + row + 5, 10), :]
                    sourced[pl.ds(top + 10, 5), :] = full[0:5]

    def two(row, carry):
        for tile in range(2):
            rad = spread(kappa_rad, row, tile)
            for layer in range(2):
                for half in range(2):
                    base = pl.multiple_of((2 * row + layer) * BLOCK + HALF * half + 8 * tile, 8)
                    beside = sourced[pl.ds(base, 8), :] + sourced[pl.ds(base + 4 * BLOCK, 8), :]
                    partial[pl.ds(base, 8), :] = partial[pl.ds(base, 8), :] + rad * beside
        return carry

    lax.fori_loop(0, SPAN, two, 0, unroll=4)

    for place, field in enumerate(ORDER):
        for layer in range(2):
            for group in range(GROUPS):
                for half in range(2):
                    first = BLOCK * layer + HALF * half + 5 * group + place
                    updated[field, layer, pl.ds(SPAN * group, SPAN), pl.ds(128 * half, 128)] = partial[
                        pl.ds(first, SPAN, stride=2 * BLOCK), :
                    ]


def specs(*kinds):
    return [pl.BlockSpec(memory_space=kind) for kind in kinds]


def shards(fields, shifts, cycle_area, gravity, kappa_az, kappa_rad):
    vmem, smem = pltpu.VMEM, pltpu.SMEM
    params = pltpu.CompilerParams(vmem_limit_bytes=VMEM_LIMIT)
    blocks = jax.ShapeDtypeStruct((RING * BLOCK, 128), jnp.float32)

    def dealt(lines):
        lines = lines.reshape(RING, BLOCK, 128)
        return lax.all_to_all(lines, "az", 0, 0, tiled=True).reshape(RING * BLOCK, 128)

    ranks = lax.axis_size("rad")
    up = [(i, i + 1) for i in range(ranks - 1)]
    down = [(i + 1, i) for i in range(ranks - 1)]
    below = lax.ppermute(fields[:, :, ROWS - 1, :].reshape(10, 256), "rad", up)
    above = lax.ppermute(fields[:, :, 0, :].reshape(10, 256), "rad", down)
    packed = pl.pallas_call(
        pack_kernel,
        out_shape=blocks,
        in_specs=specs(vmem, vmem, vmem),
        out_specs=specs(vmem)[0],
        compiler_params=params,
        name="pack",
    )(fields, below, above)
    near = jnp.concatenate([lax.ppermute(shifts[ROWS - 1 :], "rad", up), lax.ppermute(shifts[:1], "rad", down)])
    whole = dealt(packed)
    place = lax.axis_index("az").astype(jnp.int32)[None]
    moved, mass = pl.pallas_call(
        shift_kernel,
        out_shape=(blocks, jax.ShapeDtypeStruct((8, 128), jnp.float32)),
        in_specs=specs(smem, smem, smem, vmem),
        out_specs=specs(vmem, vmem),
        scratch_shapes=[pltpu.VMEM((2 * RING, 128), jnp.float32)],
        compiler_params=params,
        name="shift",
    )(place, shifts, near, whole)
    lines = dealt(moved)

    row_mass = cycle_area * mass[0, :ROWS] / (2.0 * RING * 256)
    mine = jnp.stack([row_mass, gravity])
    everyone = lax.all_gather(mine, "rad")
    masses = everyone[:, 0, :]
    totals = jnp.sum(masses, axis=1)
    rank = jnp.arange(ranks)
    offset = jnp.sum(jnp.where(rank[None, :] < rank[:, None], totals[None, :], 0.0), axis=1)
    row = jnp.arange(ROWS)
    before = jnp.sum(jnp.where(row[None, None, :] < row[None, :, None], masses[:, None, :], 0.0), axis=2)
    reach = star_mass + offset[:, None] + before + 0.5 * masses
    pulls = (everyone[:, 1, :] * reach).reshape(ranks * ROWS)
    me = lax.axis_index("rad")
    pull = lax.dynamic_slice(jnp.pad(pulls, (1, 1)), (me * ROWS,), (ROWS + 2,))
    enclosed = lax.dynamic_slice(reach.reshape(ranks * ROWS), (me * ROWS,), (ROWS,))

    updated = pl.pallas_call(
        spread_kernel,
        out_shape=jax.ShapeDtypeStruct(fields.shape, jnp.float32),
        in_specs=specs(smem, smem, smem, smem, vmem),
        out_specs=specs(vmem)[0],
        scratch_shapes=[
            pltpu.VMEM(((RING + 4) * BLOCK, 128), jnp.float32),
            pltpu.VMEM((RING * BLOCK, 128), jnp.float32),
            pltpu.VMEM((64, 128), jnp.float32),
        ],
        compiler_params=params,
        name="spread",
    )(near, kappa_az, kappa_rad, pull, lines)
    return updated, enclosed


def solution(mesh):
    placed = (P(None, None, "rad", "az"), P("rad"), P("rad"), P("rad"), P("rad"), P("rad"))
    return jax.shard_map(
        shards,
        mesh=mesh,
        in_specs=placed,
        out_specs=(P(None, None, "rad", "az"), P("rad")),
        check_vma=False,
    )
```

```python
import jax
import jax.numpy as jnp
from jax import lax
from jax.experimental import pallas as pl
from jax.experimental.pallas import tpu as pltpu
from jax.sharding import Mesh, PartitionSpec as P

star_mass = 1.0
RAD = ("chip", "core")

ORDER = (0, 1, 3, 2, 4)
RING = 64
GROUPS = 3
ROWS = 96
SPAN = ROWS // GROUPS
HALF = 16
BLOCK = 2 * HALF
PIECES = 2 * RING
VMEM_LIMIT = 24 * 1024 * 1024

TILES = ((0, 1, 5), (1, 2, 2))


def iotas():
    lane = lax.broadcasted_iota(jnp.int32, (8, 128), 1)
    line = lax.broadcasted_iota(jnp.int32, (8, 128), 0)
    return lane, line


def windows():
    for side in range(2):
        for layer in range(2):
            for half in range(2):
                yield side, layer, half, BLOCK * (32 * side + 16 * layer + 8 * half) + 31


def late(half, line):
    return half == 1 and line >= 8


def pack_kernel(fields, packed):
    for place, field in enumerate(ORDER):
        for layer in range(2):
            for group in range(GROUPS):
                for half in range(2):
                    if late(half, 5 * group + place):
                        continue
                    first = BLOCK * layer + HALF * half + 5 * group + place
                    packed[pl.ds(first, SPAN, stride=2 * BLOCK), :] = fields[
                        field, layer, pl.ds(SPAN * group, SPAN), pl.ds(128 * half, 128)
                    ]
    cells = [fields[0, z, :, pl.ds(128 * h, 128)] for z in range(2) for h in range(2)]
    total = (cells[0] + cells[1]) + (cells[2] + cells[3])
    square = jnp.concatenate([total, jnp.zeros((128 - ROWS, 128), jnp.float32)], axis=0)
    mass = jnp.sum(square.T, axis=0, keepdims=True)
    packed[pl.ds(15, RING, stride=BLOCK), :] = jnp.broadcast_to(mass, (RING, 128))


def finish_kernel(fields, below, above, begun, packed, rows, sem):
    lane, line = iotas()
    for place, field in enumerate(ORDER):
        for layer in range(2):
            for group in range(GROUPS):
                if late(1, 5 * group + place):
                    rows[pl.ds(8 * layer + 5 * group + place - 8, SPAN, stride=16), :] = fields[
                        field, layer, pl.ds(SPAN * group, SPAN), pl.ds(128, 128)
                    ]
    for side, layer, half, first in windows():
        tile = jnp.zeros((8, 128), jnp.float32)
        for place, field in enumerate(ORDER):
            cells = (below, above)[side][pl.ds(2 * field + layer, 1), pl.ds(128 * half, 128)]
            turned = pltpu.roll(jnp.broadcast_to(cells, (8, 128)), 16 * (place + 1), 1)
            for bit in (1, 2, 4):
                turned = jnp.where(line & bit == 0, turned, pltpu.roll(turned, 128 - 16 * bit, 1))
            tile = jnp.where(lane >> 4 == place + 1, turned, tile)
        rows[pl.ds(first // BLOCK * 8 + 7, 8, stride=8), :] = tile
    copy = pltpu.make_async_copy(rows.reshape(RING, 8, 128), packed.at[:, pl.ds(24, 8), :], sem)
    copy.start()
    copy.wait()


def shift_kernel(place, shifts, near, lines, moved, mass, twice):
    lane, line = iotas()
    row = place[0] >> 1
    whole, part, early = [], [], []
    for group in range(GROUPS):
        shift = shifts[SPAN * group + row]
        whole.append(shift >> 7)
        part.append(shift & 127)
        early.append(lane < part[group])

    def turned(piece, tile, group):
        at = pl.multiple_of(((piece - whole[group]) & (PIECES - 1)) * HALF + 8 * tile, 8)
        return pltpu.roll(lines[pl.ds(at, 8), :], part[group], 1)

    def one(ring, state):
        before, edges = state
        for half in range(2):
            piece = 2 * ring + half
            now, kept = [], []
            for tile, (first, second, split) in enumerate(TILES):
                a, b = turned(piece, tile, first), turned(piece, tile, second)
                pa, pb = before[tile]
                value = jnp.where(
                    line < split, jnp.where(early[first], pa, a), jnp.where(early[second], pb, b)
                )
                at = pl.multiple_of(piece * HALF + 8 * tile, 8)
                moved[pl.ds(at, 8), :] = value
                now.append((a, b))
                if half == 0:
                    owner = (ring + RING - 1) & (RING - 1)
                    slot = RING + owner
                    kept.append(jnp.where(lane == slot, pltpu.roll(value, slot, 1), edges[tile]))
                else:
                    owner = (ring + 1) & (RING - 1)
                    kept.append(jnp.where(lane == owner, pltpu.roll(value, owner + 1, 1), edges[tile]))
            before, edges = tuple(now), tuple(kept)
        return before, edges

    before = tuple(
        (turned(PIECES - 1, tile, first), turned(PIECES - 1, tile, second))
        for tile, (first, second, _) in enumerate(TILES)
    )
    zero = jnp.zeros((8, 128), jnp.float32)
    _, edges = lax.fori_loop(0, RING, one, (before, (zero, zero)), unroll=4)
    square = jnp.concatenate([edges[0], edges[1], jnp.zeros((112, 128), jnp.float32)], axis=0).T
    moved[pl.ds(15, RING, stride=BLOCK), :] = square[:RING]
    ends = lines[pl.ds(31, RING, stride=BLOCK), :]
    twice[pl.ds(0, RING), :] = ends
    twice[pl.ds(RING, RING), :] = ends
    shift = near[place[0] >> 5]
    wide = lax.broadcasted_iota(jnp.int32, (RING, 128), 1)
    crosses = (wide & 15) + 16 * (place[0] & 15) + (shift & 255) >= 256
    blocks = shift >> 8
    ends = jnp.where(crosses, twice[pl.ds(RING - 1 - blocks, RING), :], twice[pl.ds(RING - blocks, RING), :])
    moved[pl.ds(31, RING, stride=BLOCK), :] = jnp.where(wide < 16, square[RING:], ends)
    parts = lines[pl.ds(15, RING, stride=BLOCK), :]
    mass[...] = jnp.broadcast_to(jnp.sum(parts, axis=0, keepdims=True), (8, 128))


def spread_kernel(near, kappa_az, kappa_rad, pull, lines, updated, sourced, partial, ends):
    lane, line = iotas()
    square = jnp.concatenate(
        [lines[pl.ds(15, RING, stride=BLOCK), :], lines[pl.ds(31, RING, stride=BLOCK), :]], axis=0
    ).T
    edges = (square[0:8], square[8:16])
    takes = (((line == 1) | (line == 2), (line == 6) | (line == 7)), (line < 0, (line == 3) | (line == 4)))

    def spread(values, row, tile):
        first, second, split = TILES[tile]
        return jnp.where(line < split, values[SPAN * first + row], values[SPAN * second + row])

    def source(value, rate):
        return value - rate * pltpu.roll(value, 1, 0)

    def one(row, carry):
        for tile, (first, second, _) in enumerate(TILES):
            az = spread(kappa_az, row, tile)
            rad = spread(kappa_rad, row, tile)
            rate = jnp.where(
                takes[tile][0],
                pull[SPAN * first + row + 1],
                jnp.where(takes[tile][1], pull[SPAN * second + row + 1], 0.0),
            )
            for layer in range(2):
                ring = 2 * row + layer
                base = pl.multiple_of(ring * BLOCK + 8 * tile, 8)
                low = lines[pl.ds(base, 8), :]
                high = lines[pl.ds(base + HALF, 8), :]
                low_up, high_up = pltpu.roll(low, 1, 1), pltpu.roll(high, 1, 1)
                low_down, high_down = pltpu.roll(low, 127, 1), pltpu.roll(high, 127, 1)
                left = pltpu.roll(edges[tile], (128 - ring) & 127, 1)
                right = pltpu.roll(edges[tile], 63 - ring, 1)
                sides = (
                    jnp.where(lane == 0, left, low_up) + jnp.where(lane == 127, high_down, low_down),
                    jnp.where(lane == 0, low_up, high_up) + jnp.where(lane == 127, right, high_down),
                )
                for half, value in enumerate((low, high)):
                    closed = value + az * (sides[half] - 2.0 * value)
                    full = source(value, rate)
                    sourced[pl.ds(base + 2 * BLOCK + HALF * half, 8), :] = full
                    partial[pl.ds(base + HALF * half, 8), :] = source(closed, rate) - 2.0 * rad * full
        return carry

    lax.fori_loop(0, SPAN, one, 0, unroll=2)

    ends[...] = jnp.zeros(ends.shape, jnp.float32)
    for side, layer, half, first in windows():
        tile = lines[pl.ds(first, 8, stride=BLOCK), :]
        for place in range(5):
            turned = pltpu.roll(pltpu.roll(tile, 112 - 16 * place, 1), 0, 1, stride=16, stride_axis=0)
            cells = jnp.sum(jnp.where(lane >> 4 == line, turned, 0.0), axis=0, keepdims=True)
            ends[pl.ds(8 * (4 * side + 2 * layer + half) + place, 1), :] = cells
    for side in range(2):
        part, odd = near[side] & 127, near[side] & 128
        rate = jnp.where(takes[0][0], pull[(ROWS + 1) * side], 0.0)
        for layer in range(2):
            at = 8 * (4 * side + 2 * layer)
            low = pltpu.roll(ends[pl.ds(at, 8), :], part, 1)
            high = pltpu.roll(ends[pl.ds(at + 8, 8), :], part, 1)
            even = jnp.where(lane < part, high, low), jnp.where(lane < part, low, high)
            for half in range(2):
                row = BLOCK * layer + HALF * half
                full = source(jnp.where(odd == 0, even[half], even[1 - half]), rate)
                if side == 0:
                    sourced[pl.ds(row, 5), :] = full[0:5]
                    sourced[pl.ds(row + 5, 10), :] = sourced[pl.ds(RING * BLOCK + row, 10), :]
                else:
                    top = (RING + 2) * BLOCK + row
                    sourced[pl.ds(top, 10), :] = sourced[pl.ds(2 * BLOCK + row + 5, 10), :]
                    sourced[pl.ds(top + 10, 5), :] = full[0:5]

    def two(row, carry):
        for tile in range(2):
            rad = spread(kappa_rad, row, tile)
            for layer in range(2):
                for half in range(2):
                    base = pl.multiple_of((2 * row + layer) * BLOCK + HALF * half + 8 * tile, 8)
                    beside = sourced[pl.ds(base, 8), :] + sourced[pl.ds(base + 4 * BLOCK, 8), :]
                    partial[pl.ds(base, 8), :] = partial[pl.ds(base, 8), :] + rad * beside
        return carry

    lax.fori_loop(0, SPAN, two, 0, unroll=4)

    for place, field in enumerate(ORDER):
        for layer in range(2):
            for group in range(GROUPS):
                for half in range(2):
                    first = BLOCK * layer + HALF * half + 5 * group + place
                    updated[field, layer, pl.ds(SPAN * group, SPAN), pl.ds(128 * half, 128)] = partial[
                        pl.ds(first, SPAN, stride=2 * BLOCK), :
                    ]


def specs(*kinds):
    return [pl.BlockSpec(memory_space=kind) for kind in kinds]


def shards(fields, shifts, cycle_area, gravity, kappa_az, kappa_rad):
    vmem, smem = pltpu.VMEM, pltpu.SMEM
    params = pltpu.CompilerParams(vmem_limit_bytes=VMEM_LIMIT)
    blocks = jax.ShapeDtypeStruct((RING * BLOCK, 128), jnp.float32)

    def dealt(lines):
        lines = lines.reshape(RING, BLOCK, 128)
        return lax.all_to_all(lines, "az", 0, 0, tiled=True).reshape(RING * BLOCK, 128)

    ranks = lax.axis_size(RAD)

    def message(row):
        cells = fields[:, :, row, :].reshape(10, 256)
        return jnp.concatenate([cells, jnp.full((6, 256), shifts[row].astype(jnp.float32))])

    below = lax.ppermute(message(ROWS - 1), RAD, [(i, i + 1) for i in range(ranks - 1)])
    above = lax.ppermute(message(0), RAD, [(i + 1, i) for i in range(ranks - 1)])
    begun = pl.pallas_call(
        pack_kernel,
        out_shape=blocks,
        in_specs=specs(vmem),
        out_specs=specs(vmem)[0],
        compiler_params=params,
        name="pack",
    )(fields)
    packed = pl.pallas_call(
        finish_kernel,
        out_shape=jax.ShapeDtypeStruct((RING, BLOCK, 128), jnp.float32),
        in_specs=specs(vmem, vmem, vmem, pl.ANY),
        out_specs=specs(pl.ANY)[0],
        scratch_shapes=[pltpu.VMEM((RING * 8, 128), jnp.float32), pltpu.SemaphoreType.DMA],
        input_output_aliases={3: 0},
        compiler_params=params,
        name="finish",
    )(fields, below, above, begun.reshape(RING, BLOCK, 128))
    near = jnp.stack([below[10, 0], above[10, 0]]).astype(jnp.int32)
    whole = dealt(packed)
    place = lax.axis_index("az").astype(jnp.int32)[None]
    moved, mass = pl.pallas_call(
        shift_kernel,
        out_shape=(blocks, jax.ShapeDtypeStruct((8, 128), jnp.float32)),
        in_specs=specs(smem, smem, smem, vmem),
        out_specs=specs(vmem, vmem),
        scratch_shapes=[pltpu.VMEM((2 * RING, 128), jnp.float32)],
        compiler_params=params,
        name="shift",
    )(place, shifts, near, whole)
    lines = dealt(moved)

    row_mass = cycle_area * mass[0, :ROWS] / (2.0 * RING * 256)
    mine = jnp.stack([row_mass, gravity])
    everyone = lax.all_gather(lax.all_gather(mine, "core"), "chip").reshape(ranks, 2, ROWS)
    masses = everyone[:, 0, :]
    totals = jnp.sum(masses, axis=1)
    rank = jnp.arange(ranks)
    offset = jnp.sum(jnp.where(rank[None, :] < rank[:, None], totals[None, :], 0.0), axis=1)
    row = jnp.arange(ROWS)
    before = jnp.sum(jnp.where(row[None, None, :] < row[None, :, None], masses[:, None, :], 0.0), axis=2)
    reach = star_mass + offset[:, None] + before + 0.5 * masses
    pulls = (everyone[:, 1, :] * reach).reshape(ranks * ROWS)
    me = lax.axis_index(RAD)
    pull = lax.dynamic_slice(jnp.pad(pulls, (1, 1)), (me * ROWS,), (ROWS + 2,))
    enclosed = lax.dynamic_slice(reach.reshape(ranks * ROWS), (me * ROWS,), (ROWS,))

    updated = pl.pallas_call(
        spread_kernel,
        out_shape=jax.ShapeDtypeStruct(fields.shape, jnp.float32),
        in_specs=specs(smem, smem, smem, smem, vmem),
        out_specs=specs(vmem)[0],
        scratch_shapes=[
            pltpu.VMEM(((RING + 4) * BLOCK, 128), jnp.float32),
            pltpu.VMEM((RING * BLOCK, 128), jnp.float32),
            pltpu.VMEM((64, 128), jnp.float32),
        ],
        compiler_params=params,
        name="spread",
    )(near, kappa_az, kappa_rad, pull, lines)
    return updated, enclosed


def solution(mesh):
    split = Mesh(mesh.devices.reshape(mesh.shape["az"], -1, 2), ("az",) + RAD)
    placed = (P(None, None, RAD, "az"), P(RAD), P(RAD), P(RAD), P(RAD), P(RAD))
    return jax.shard_map(
        shards,
        mesh=split,
        in_specs=placed,
        out_specs=(P(None, None, RAD, "az"), P(RAD)),
        check_vma=False,
    )
```

```python
import jax
import jax.numpy as jnp
from jax import lax
from jax.experimental import pallas as pl
from jax.experimental.pallas import tpu as pltpu
from jax.sharding import Mesh, PartitionSpec as P

star_mass = 1.0
RAD = ("chip", "core")

ORDER = (0, 1, 3, 2, 4)
RING = 64
GROUPS = 3
ROWS = 96
SPAN = ROWS // GROUPS
HALF = 16
BLOCK = 2 * HALF
PIECES = 2 * RING
STEP = 8
VMEM_LIMIT = 24 * 1024 * 1024

TILES = ((0, 1, 5), (1, 2, 2))


def iotas():
    lane = lax.broadcasted_iota(jnp.int32, (8, 128), 1)
    line = lax.broadcasted_iota(jnp.int32, (8, 128), 0)
    return lane, line


def windows():
    for side in range(2):
        for layer in range(2):
            for half in range(2):
                yield side, layer, half, BLOCK * (32 * side + 16 * layer + 8 * half) + 31


def pack_kernel(given, fields, packed, cells, shifts, sems):
    lane, line = iotas()
    shift_copy = pltpu.make_async_copy(given, shifts, sems.at[5])
    shift_copy.start()
    copies = [pltpu.make_async_copy(fields.at[f], cells.at[f], sems.at[f]) for f in ORDER]
    for copy in copies:
        copy.start()
    for place, field in enumerate(ORDER):
        copies[place].wait()
        for layer in range(2):
            for group in range(GROUPS):
                for half in range(2):
                    first = BLOCK * layer + HALF * half + 5 * group + place
                    packed[pl.ds(first, SPAN, stride=2 * BLOCK), :] = cells[
                        field, layer, pl.ds(SPAN * group, SPAN), pl.ds(128 * half, 128)
                    ]
        if place == 0:
            halves = [cells[0, z, :, pl.ds(128 * h, 128)] for z in range(2) for h in range(2)]
            total = (halves[0] + halves[1]) + (halves[2] + halves[3])
            square = jnp.concatenate([total, jnp.zeros((128 - ROWS, 128), jnp.float32)], axis=0)
            mass = jnp.sum(square.T, axis=0, keepdims=True)
            packed[pl.ds(15, RING, stride=BLOCK), :] = jnp.broadcast_to(mass, (RING, 128))
    shift_copy.wait()
    for side, layer, half, first in windows():
        row = (ROWS - 1) * (1 - side)
        part, odd = shifts[row] & 127, shifts[row] & 128
        tile = jnp.zeros((8, 128), jnp.float32)
        for place, field in enumerate(ORDER):
            low, high = (
                pltpu.roll(jnp.broadcast_to(cells[field, layer, pl.ds(row, 1), pl.ds(at, 128)], (8, 128)), part, 1)
                for at in (0, 128)
            )
            chosen = jnp.where((lane < part) ^ (odd != 0) ^ (half == 1), high, low)
            turned = pltpu.roll(chosen, 16 * (place + 1), 1)
            for bit in (1, 2, 4):
                turned = jnp.where(line & bit == 0, turned, pltpu.roll(turned, 128 - 16 * bit, 1))
            tile = jnp.where(lane >> 4 == place + 1, turned, tile)
        packed[pl.ds(first, 8, stride=BLOCK), :] = tile


def ends_kernel(steps, lines, moved, twice):
    cells = lines[pl.ds(31, RING, stride=BLOCK), :]
    twice[pl.ds(0, RING), :] = cells
    twice[pl.ds(RING, RING), :] = cells
    shift = steps[3]
    lane = lax.broadcasted_iota(jnp.int32, (RING, 128), 1)
    crossed = (lane & 15) + 16 * (steps[4] & 15) < (shift & 255)
    blocks = shift >> 8
    moved[...] = jnp.where(crossed, twice[pl.ds(RING - 1 - blocks, RING), :], twice[pl.ds(RING - blocks, RING), :])


def join_kernel(tail, ends, begun, moved, rows, sem):
    rows[...] = tail[...]
    lane = lax.broadcasted_iota(jnp.int32, (RING, 128), 1)
    last = pl.ds(7, RING, stride=8)
    rows[last, :] = jnp.where(lane < 16, tail[last, :], ends[...])
    copy = pltpu.make_async_copy(rows.reshape(RING, 8, 128), moved.at[:, pl.ds(24, 8), :], sem)
    copy.start()
    copy.wait()


def shift_kernel(steps, lines, moved, tail, mass, twice):
    lane, line = iotas()
    whole, part, early = [], [], []
    for group in range(GROUPS):
        shift = steps[group]
        whole.append(shift >> 7)
        part.append(shift & 127)
        early.append(lane < part[group])

    def piece_of(piece, tile, group):
        at = pl.multiple_of(((piece - whole[group]) & (PIECES - 1)) * HALF + 8 * tile, 8)
        return lines[pl.ds(at, 8), :]

    def turned(value, group):
        return pltpu.roll(value, part[group], 1)

    def several(step, state):
        before, edges = state
        edges = list(edges)
        first_piece = step * STEP
        loaded = [
            [[piece_of(first_piece + i, tile, group) for group in TILES[tile][:2]] for tile in range(2)]
            for i in range(STEP)
        ]
        values = []
        for i in range(STEP):
            now, made = [], []
            for tile, (first, second, split) in enumerate(TILES):
                a, b = turned(loaded[i][tile][0], first), turned(loaded[i][tile][1], second)
                pa, pb = before[tile]
                made.append(
                    jnp.where(line < split, jnp.where(early[first], pa, a), jnp.where(early[second], pb, b))
                )
                now.append((a, b))
            before = tuple(now)
            values.append(made)
        for i in range(0, STEP, 2):
            ring = step * (STEP // 2) + i // 2
            for tile in range(2):
                both = jnp.where(lane == 127, values[i + 1][tile], values[i][tile])
                edges[tile] = jnp.where(lane >> 1 == ring, pltpu.roll(both, (2 * ring + 1) & 127, 1), edges[tile])
        for i in range(STEP):
            for tile in range(2):
                if i % 2 == 1 and tile == 1:
                    at = pl.multiple_of((first_piece + i) // 2 * 8, 8)
                    tail[pl.ds(at, 8), :] = values[i][tile]
                else:
                    at = pl.multiple_of((first_piece + i) * HALF + 8 * tile, 8)
                    moved[pl.ds(at, 8), :] = values[i][tile]
        return before, tuple(edges)

    before = tuple(
        tuple(turned(piece_of(PIECES - 1, tile, group), group) for group in TILES[tile][:2]) for tile in range(2)
    )
    zero = jnp.zeros((8, 128), jnp.float32)
    _, edges = lax.fori_loop(0, PIECES // STEP, several, (before, (zero, zero)))
    twice[...] = jnp.concatenate([edges[0], edges[1], jnp.zeros((112, 128), jnp.float32)], axis=0).T
    left = twice[pl.ds(0, RING, stride=2), :]
    right = twice[pl.ds(1, RING, stride=2), :]
    moved[pl.ds(BLOCK + 15, RING - 1, stride=BLOCK), :] = left[: RING - 1]
    moved[pl.ds(15, 1), :] = left[RING - 1 :]
    right = jnp.concatenate([right[1:], right[:1]], axis=0)
    tail[pl.ds(7, RING, stride=8), :] = right
    parts = lines[pl.ds(15, RING, stride=BLOCK), :]
    mass[...] = jnp.broadcast_to(jnp.sum(parts, axis=0, keepdims=True), (8, 128))


def spread_kernel(rates, lines, updated, done, ends, square):
    lane, line = iotas()
    square[pl.ds(0, RING, stride=2), :] = lines[pl.ds(15, RING, stride=BLOCK), :]
    square[pl.ds(1, RING - 1, stride=2), :] = lines[pl.ds(BLOCK + 31, RING - 1, stride=BLOCK), :]
    square[pl.ds(127, 1), :] = lines[pl.ds(31, 1), :]
    across = square[...].T
    edges = across[0:8], across[8:16]
    under_edges = tuple(pltpu.roll(value, 1, 0) for value in edges)
    takes = (((line == 1) | (line == 2), (line == 6) | (line == 7)), (None, (line == 3) | (line == 4)))

    def spread(first_rate, row, tile):
        first, second, split = TILES[tile]
        return jnp.where(
            line < split, rates[first_rate + SPAN * first + row], rates[first_rate + SPAN * second + row]
        )

    def pulls(row, tile):
        first, second, _ = TILES[tile]
        other = jnp.where(takes[tile][1], rates[2 * ROWS + 1 + SPAN * second + row], 0.0)
        if takes[tile][0] is None:
            return other
        return jnp.where(takes[tile][0], rates[2 * ROWS + 1 + SPAN * first + row], other)

    def source(value, rate):
        return value - rate * pltpu.roll(value, 1, 0)

    def spots():
        return ((tile, layer, half) for tile in range(2) for layer in range(2) for half in range(2))

    def place_of(row, tile, layer, half):
        return pl.multiple_of((2 * row + layer) * BLOCK + HALF * half + 8 * tile, 8)

    def begin(row):
        cells = {spot: lines[pl.ds(place_of(row, *spot), 8), :] for spot in spots()}
        full, partial = [], []
        for tile in range(2):
            az, rad, rate = spread(0, row, tile), spread(ROWS, row, tile), pulls(row, tile)
            keep = 1.0 - 2.0 * (az + rad)
            border = edges[tile] - rate * under_edges[tile]
            for layer in range(2):
                low, high = (source(cells[tile, layer, half], rate) for half in range(2))
                side = pltpu.roll(border, (128 - 4 * row - 2 * layer) & 127, 1)
                low_up, high_up = pltpu.roll(low, 1, 1), pltpu.roll(high, 1, 1)
                low_down, high_down = pltpu.roll(low, 127, 1), pltpu.roll(high, 127, 1)
                low_sum = jnp.where(lane == 0, side, low_up) + jnp.where(lane == 127, high_down, low_down)
                high_sum = jnp.where(lane == 0, low_up, high_up) + jnp.where(lane == 127, side, high_down)
                full += [low, high]
                partial += [keep * low + az * low_sum, keep * high + az * high_sum]
        return full, partial

    def end(row, partial, under, over):
        for tile in range(2):
            rad = spread(ROWS, row, tile)
            for layer in range(2):
                for half in range(2):
                    at = 4 * tile + 2 * layer + half
                    done[pl.ds(place_of(row, tile, layer, half), 8), :] = partial[at] + rad * (under[at] + over[at])

    ends[...] = jnp.zeros(ends.shape, jnp.float32)
    for side, layer, half, first in windows():
        tile = lines[pl.ds(first, 8, stride=BLOCK), :]
        for place in range(5):
            turned = pltpu.roll(pltpu.roll(tile, 112 - 16 * place, 1), 0, 1, stride=16, stride_axis=0)
            cells = jnp.sum(jnp.where(lane >> 4 == line, turned, 0.0), axis=0, keepdims=True)
            ends[pl.ds(8 * (4 * side + 2 * layer + half) + place, 1), :] = cells

    def outer(side):
        rate = jnp.where(takes[0][0], rates[2 * ROWS + (ROWS + 1) * side], 0.0)
        return [source(ends[pl.ds(32 * side + 8 * i, 8), :], rate) for i in range(4)]

    last, last_partial = begin(SPAN - 1)
    full, partial = begin(0)
    turned = [pltpu.roll(value, 5, 0) for value in last]
    under = [jnp.where(line < 5, value, turned[i]) for i, value in enumerate(outer(0))]
    under += [jnp.where(line < 5, turned[i], turned[4 + i]) for i in range(4)]
    turned = [pltpu.roll(value, 3, 0) for value in full]
    over = [jnp.where(line < 3, turned[i], turned[4 + i]) for i in range(4)]
    over += [jnp.where(line < 2, turned[4 + i], pltpu.roll(value, 2, 0)) for i, value in enumerate(outer(1))]
    for i in range(8):
        ends[pl.ds(64 + 8 * i, 8), :] = last[i]
        ends[pl.ds(128 + 8 * i, 8), :] = last_partial[i]
        ends[pl.ds(192 + 8 * i, 8), :] = over[i]

    def kept(first):
        return [ends[pl.ds(first + 8 * i, 8), :] for i in range(8)]

    def rows(pair, state):
        under, full, partial = state
        for row in (2 * pair + 1, 2 * pair + 2):
            over, later = begin(row)
            end(row - 1, partial, under, over)
            under, full, partial = full, over, later
        return under, full, partial

    under, full, partial = lax.fori_loop(0, SPAN // 2 - 1, rows, (under, full, partial))
    last = kept(64)
    end(SPAN - 2, partial, under, last)
    end(SPAN - 1, kept(128), full, kept(192))

    for place, field in enumerate(ORDER):
        for layer in range(2):
            for group in range(GROUPS):
                for half in range(2):
                    first = BLOCK * layer + HALF * half + 5 * group + place
                    updated[field, layer, pl.ds(SPAN * group, SPAN), pl.ds(128 * half, 128)] = done[
                        pl.ds(first, SPAN, stride=2 * BLOCK), :
                    ]


def specs(*kinds):
    return [pl.BlockSpec(memory_space=kind) for kind in kinds]


def shards(fields, shifts, cycle_area, gravity, kappa_az, kappa_rad):
    vmem, smem = pltpu.VMEM, pltpu.SMEM
    params = pltpu.CompilerParams(vmem_limit_bytes=VMEM_LIMIT)
    blocks = jax.ShapeDtypeStruct((RING * BLOCK, 128), jnp.float32)

    def dealt(lines):
        lines = lines.reshape(RING, BLOCK, 128)
        return lax.all_to_all(lines, "az", 0, 0, tiled=True).reshape(RING * BLOCK, 128)

    ranks = lax.axis_size(RAD)
    packed = pl.pallas_call(
        pack_kernel,
        out_shape=blocks,
        in_specs=specs(pltpu.HBM, pltpu.HBM),
        out_specs=specs(vmem)[0],
        scratch_shapes=[
            pltpu.VMEM(fields.shape, jnp.float32),
            pltpu.SMEM(shifts.shape, jnp.int32),
            pltpu.SemaphoreType.DMA((6,)),
        ],
        compiler_params=pltpu.CompilerParams(vmem_limit_bytes=60 * 1024 * 1024),
        name="pack",
    )(shifts, fields)
    whole = dealt(packed)
    place = lax.axis_index("az").astype(jnp.int32)
    mine = lax.dynamic_slice(shifts.reshape(GROUPS, SPAN), (0, place // 2), (GROUPS, 1))[:, 0]
    end = jnp.where(place < RING // 2, shifts[ROWS - 1 :], shifts[:1])
    steps = jnp.concatenate([mine, end, place[None]])
    ends = pl.pallas_call(
        ends_kernel,
        out_shape=jax.ShapeDtypeStruct((RING, 128), jnp.float32),
        in_specs=specs(smem, vmem),
        out_specs=specs(vmem)[0],
        scratch_shapes=[pltpu.VMEM((2 * RING, 128), jnp.float32)],
        compiler_params=params,
        name="ends",
    )(steps, whole)
    outward = [(q * ranks + i, q * ranks + i + 1) for q in range(RING // 2) for i in range(ranks - 1)]
    inward = [(q * ranks + i + 1, q * ranks + i) for q in range(RING // 2, RING) for i in range(ranks - 1)]
    ends = lax.ppermute(ends, ("az",) + RAD, outward + inward)
    begun, tail, mass = pl.pallas_call(
        shift_kernel,
        out_shape=(
            blocks,
            jax.ShapeDtypeStruct((RING * 8, 128), jnp.float32),
            jax.ShapeDtypeStruct((8, 128), jnp.float32),
        ),
        in_specs=specs(smem, vmem),
        out_specs=specs(vmem, vmem, vmem),
        scratch_shapes=[pltpu.VMEM((2 * RING, 128), jnp.float32)],
        compiler_params=params,
        name="shift",
    )(steps, whole)
    moved = pl.pallas_call(
        join_kernel,
        out_shape=jax.ShapeDtypeStruct((RING, BLOCK, 128), jnp.float32),
        in_specs=specs(vmem, vmem, pl.ANY),
        out_specs=specs(pl.ANY)[0],
        scratch_shapes=[pltpu.VMEM((RING * 8, 128), jnp.float32), pltpu.SemaphoreType.DMA],
        input_output_aliases={2: 0},
        compiler_params=params,
        name="join",
    )(tail, ends, begun.reshape(RING, BLOCK, 128))
    lines = dealt(moved)

    row_mass = cycle_area * mass[0, :ROWS] / (2.0 * RING * 256)
    mine = jnp.stack([row_mass, gravity])
    everyone = lax.all_gather(lax.all_gather(mine, "core"), "chip").reshape(ranks, 2, ROWS)
    masses = everyone[:, 0, :]
    totals = jnp.sum(masses, axis=1)
    rank = jnp.arange(ranks)
    offset = jnp.sum(jnp.where(rank[None, :] < rank[:, None], totals[None, :], 0.0), axis=1)
    row = jnp.arange(ROWS)
    before = jnp.sum(jnp.where(row[None, None, :] < row[None, :, None], masses[:, None, :], 0.0), axis=2)
    reach = star_mass + offset[:, None] + before + 0.5 * masses
    pulls = (everyone[:, 1, :] * reach).reshape(ranks * ROWS)
    me = lax.axis_index(RAD)
    pull = lax.dynamic_slice(jnp.pad(pulls, (1, 1)), (me * ROWS,), (ROWS + 2,))
    enclosed = lax.dynamic_slice(reach.reshape(ranks * ROWS), (me * ROWS,), (ROWS,))

    updated = pl.pallas_call(
        spread_kernel,
        out_shape=jax.ShapeDtypeStruct(fields.shape, jnp.float32),
        in_specs=specs(smem, vmem),
        out_specs=specs(vmem)[0],
        scratch_shapes=[
            pltpu.VMEM((RING * BLOCK, 128), jnp.float32),
            pltpu.VMEM((256, 128), jnp.float32),
            pltpu.VMEM((128, 128), jnp.float32),
        ],
        compiler_params=params,
        name="spread",
    )(jnp.concatenate([kappa_az, kappa_rad, pull]), lines)
    return updated, enclosed


def solution(mesh):
    split = Mesh(mesh.devices.reshape(mesh.shape["az"], -1, 2), ("az",) + RAD)
    placed = (P(None, None, RAD, "az"), P(RAD), P(RAD), P(RAD), P(RAD), P(RAD))
    return jax.shard_map(
        shards,
        mesh=split,
        in_specs=placed,
        out_specs=(P(None, None, RAD, "az"), P(RAD)),
        check_vma=False,
    )
```

```python
import jax
import jax.numpy as jnp
from jax import lax
from jax.experimental import pallas as pl
from jax.experimental.pallas import tpu as pltpu
from jax.sharding import Mesh, PartitionSpec as P

star_mass = 1.0
RAD = ("chip", "core")

ORDER = (0, 1, 3, 2, 4)
RING = 64
GROUPS = 3
ROWS = 96
SPAN = ROWS // GROUPS
HALF = 16
BLOCK = 2 * HALF
PIECES = 2 * RING
PARTS = SPAN // 8
STEP = 8
VMEM_LIMIT = 24 * 1024 * 1024

TILES = ((0, 1, 5), (1, 2, 2))


def iotas():
    lane = lax.broadcasted_iota(jnp.int32, (8, 128), 1)
    line = lax.broadcasted_iota(jnp.int32, (8, 128), 0)
    return lane, line


def windows():
    for side in range(2):
        for layer in range(2):
            for half in range(2):
                yield side, layer, half, BLOCK * (32 * side + 16 * layer + 8 * half) + 31


def pack_kernel(given, fields, packed, cells, lines, shifts, sems, sent):
    lane, line = iotas()
    shift_copy = pltpu.make_async_copy(given, shifts, sems.at[GROUPS * PARTS])
    shift_copy.start()
    copies = {}
    for part, group in sorted(
        ((part, group) for part in range(PARTS) for group in range(GROUPS)),
        key=lambda at: at not in ((0, 0), (PARTS - 1, GROUPS - 1)),
    ):
        rows = pl.ds(SPAN * group + 8 * part, 8)
        copies[part, group] = pltpu.make_async_copy(
            fields.at[:, :, rows, :], cells.at[:, :, rows, :], sems.at[GROUPS * part + group]
        )
        copies[part, group].start()
    arrived = [(0, 0), (PARTS - 1, GROUPS - 1)]
    for at in arrived:
        copies[at].wait()
    shift_copy.wait()
    for side, layer, half, first in windows():
        row = (ROWS - 1) * (1 - side)
        part, odd = shifts[row] & 127, shifts[row] & 128
        tile = jnp.zeros((8, 128), jnp.float32)
        for place, field in enumerate(ORDER):
            low, high = (
                pltpu.roll(jnp.broadcast_to(cells[field, layer, pl.ds(row, 1), pl.ds(at, 128)], (8, 128)), part, 1)
                for at in (0, 128)
            )
            chosen = jnp.where((lane < part) ^ (odd != 0) ^ (half == 1), high, low)
            turned = pltpu.roll(chosen, 16 * (place + 1), 1)
            for bit in (1, 2, 4):
                turned = jnp.where(line & bit == 0, turned, pltpu.roll(turned, 128 - 16 * bit, 1))
            tile = jnp.where(lane >> 4 == place + 1, turned, tile)
        lines[pl.ds(first, 8, stride=BLOCK), :] = tile
    blocks = lines.reshape(RING, BLOCK, 128)
    sending = []

    def send(first, count, low, high):
        part = pl.ds(first, count), pl.ds(low, high - low)
        copy = pltpu.make_async_copy(blocks.at[part[0], part[1], :], packed.at[part[0], part[1], :], sent.at[len(sending)])
        copy.start()
        sending.append(copy)

    for part in range(PARTS):
        for group in range(GROUPS):
            if (part, group) not in arrived:
                copies[part, group].wait()
            for place, field in enumerate(ORDER):
                for layer in range(2):
                    for half in range(2):
                        first = 16 * BLOCK * part + BLOCK * layer + HALF * half + 5 * group + place
                        lines[pl.ds(first, 8, stride=2 * BLOCK), :] = cells[
                            field, layer, pl.ds(SPAN * group + 8 * part, 8), pl.ds(128 * half, 128)
                        ]
        send(16 * part, 16, 0, 8)
        send(16 * part, 16, 16, 32)
    halves = [cells[0, z, :, pl.ds(128 * h, 128)] for z in range(2) for h in range(2)]
    total = (halves[0] + halves[1]) + (halves[2] + halves[3])
    square = jnp.concatenate([total, jnp.zeros((128 - ROWS, 128), jnp.float32)], axis=0)
    mass = jnp.sum(square.T, axis=0, keepdims=True)
    lines[pl.ds(15, RING, stride=BLOCK), :] = jnp.broadcast_to(mass, (RING, 128))
    send(0, RING, 8, 16)
    for copy in sending:
        copy.wait()


def ends_kernel(steps, lines, moved, twice):
    cells = lines[pl.ds(31, RING, stride=BLOCK), :]
    twice[pl.ds(0, RING), :] = cells
    twice[pl.ds(RING, RING), :] = cells
    shift = steps[3]
    lane = lax.broadcasted_iota(jnp.int32, (RING, 128), 1)
    crossed = (lane & 15) + 16 * (steps[4] & 15) < (shift & 255)
    blocks = shift >> 8
    moved[...] = jnp.where(crossed, twice[pl.ds(RING - 1 - blocks, RING), :], twice[pl.ds(RING - blocks, RING), :])


def join_kernel(tail, ends, begun, moved, rows, sem):
    rows[...] = tail[...]
    lane = lax.broadcasted_iota(jnp.int32, (RING, 128), 1)
    last = pl.ds(7, RING, stride=8)
    rows[last, :] = jnp.where((lane < 16) | (lane >= 96), tail[last, :], ends[...])
    copy = pltpu.make_async_copy(rows.reshape(RING, 8, 128), moved.at[:, pl.ds(24, 8), :], sem)
    copy.start()
    copy.wait()


def shift_kernel(steps, lines, begun, tail, mass, moved, square, sems):
    lane, line = iotas()
    blocks = moved.reshape(RING, BLOCK, 128)

    def copy_of(step):
        part = pl.ds(step * (STEP // 2), STEP // 2)
        return pltpu.make_async_copy(
            blocks.at[part, pl.ds(0, 24), :], begun.at[part, pl.ds(0, 24), :], sems.at[step]
        )

    whole, part, early = [], [], []
    for group in range(GROUPS):
        shift = steps[group]
        whole.append(shift >> 7)
        part.append(shift & 127)
        early.append(lane < part[group])

    def piece_of(piece, tile, group):
        at = pl.multiple_of(((piece - whole[group]) & (PIECES - 1)) * HALF + 8 * tile, 8)
        return lines[pl.ds(at, 8), :]

    def turned(value, group):
        return pltpu.roll(value, part[group], 1)

    def several(step, state):
        before, edges = state
        edges = list(edges)
        first_piece = step * STEP
        loaded = [
            [[piece_of(first_piece + i, tile, group) for group in TILES[tile][:2]] for tile in range(2)]
            for i in range(STEP)
        ]
        values = []
        for i in range(STEP):
            now, made = [], []
            for tile, (first, second, split) in enumerate(TILES):
                a, b = turned(loaded[i][tile][0], first), turned(loaded[i][tile][1], second)
                pa, pb = before[tile]
                made.append(
                    jnp.where(line < split, jnp.where(early[first], pa, a), jnp.where(early[second], pb, b))
                )
                now.append((a, b))
            before = tuple(now)
            values.append(made)
        for i in range(0, STEP, 2):
            ring = step * (STEP // 2) + i // 2
            for tile in range(2):
                both = jnp.where(lane == 127, values[i + 1][tile], values[i][tile])
                edges[tile] = jnp.where(lane >> 1 == ring, pltpu.roll(both, (2 * ring + 1) & 127, 1), edges[tile])
        for i in range(STEP):
            for tile in range(2):
                if i % 2 == 1 and tile == 1:
                    at = pl.multiple_of((first_piece + i) // 2 * 8, 8)
                    tail[pl.ds(at, 8), :] = values[i][tile]
                else:
                    at = pl.multiple_of((first_piece + i) * HALF + 8 * tile, 8)
                    moved[pl.ds(at, 8), :] = values[i][tile]
        copy_of(step).start()
        return before, tuple(edges)

    before = tuple(
        tuple(turned(piece_of(PIECES - 1, tile, group), group) for group in TILES[tile][:2]) for tile in range(2)
    )
    zero = jnp.zeros((8, 128), jnp.float32)
    _, edges = lax.fori_loop(0, PIECES // STEP, several, (before, (zero, zero)))
    square[...] = jnp.concatenate([edges[0], edges[1], jnp.zeros((112, 128), jnp.float32)], axis=0).T
    left = pltpu.roll(square[pl.ds(0, RING, stride=2), :], 96, 1)
    right = square[pl.ds(1, RING, stride=2), :]
    left = jnp.concatenate([left[RING - 1 :], left[: RING - 1]], axis=0)
    right = jnp.concatenate([right[1:], right[:1]], axis=0)
    tail[pl.ds(7, RING, stride=8), :] = left + right
    parts = lines[pl.ds(15, RING, stride=BLOCK), :]
    mass[...] = jnp.broadcast_to(jnp.sum(parts, axis=0, keepdims=True), (8, 128))

    @pl.loop(0, PIECES // STEP)
    def _(step):
        copy_of(step).wait()


def spread_kernel(rank, rates, totals, local, lines, updated, enclosed, done, out, ends, square, sems):
    lane, line = iotas()
    here = rank[0]
    base = jnp.float32(star_mass)
    for other in range(totals.shape[0] // 8):
        base = base + jnp.where(other < here, totals[8 * other], 0.0)
    below = 8 * jnp.maximum(here - 1, 0)
    above = 8 * jnp.minimum(here + 1, totals.shape[0] // 8 - 1)
    outer_pull = (
        totals[below + 4] * (base - totals[below + 3]),
        totals[above + 2] * (base + totals[8 * here] + totals[above + 1]),
    )
    enclosed[...] = local[...] + base

    borders = lines[pl.ds(31, RING, stride=BLOCK), :]
    square[pl.ds(0, RING, stride=2), :] = pltpu.roll(borders, 32, 1)
    square[pl.ds(1, RING - 1, stride=2), :] = lines[pl.ds(BLOCK + 31, RING - 1, stride=BLOCK), :]
    square[pl.ds(127, 1), :] = lines[pl.ds(31, 1), :]
    across = square[...].T
    edges = across[0:8], across[8:16]
    under_edges = tuple(pltpu.roll(value, 1, 0) for value in edges)
    takes = (((line == 1) | (line == 2), (line == 6) | (line == 7)), (None, (line == 3) | (line == 4)))

    def spread(first_rate, row, tile):
        first, second, split = TILES[tile]
        return jnp.where(
            line < split, rates[first_rate + SPAN * first + row], rates[first_rate + SPAN * second + row]
        )

    def pull(row):
        return rates[2 * ROWS + row] * (base + rates[3 * ROWS + row])

    def pulls(row, tile):
        first, second, _ = TILES[tile]
        other = jnp.where(takes[tile][1], pull(SPAN * second + row), 0.0)
        if takes[tile][0] is None:
            return other
        return jnp.where(takes[tile][0], pull(SPAN * first + row), other)

    def source(value, rate):
        return value - rate * pltpu.roll(value, 1, 0)

    def spots():
        return ((tile, layer, half) for tile in range(2) for layer in range(2) for half in range(2))

    def place_of(row, tile, layer, half):
        return pl.multiple_of((2 * row + layer) * BLOCK + HALF * half + 8 * tile, 8)

    def begin(row):
        cells = {spot: lines[pl.ds(place_of(row, *spot), 8), :] for spot in spots()}
        full, partial = [], []
        for tile in range(2):
            az, rad, rate = spread(0, row, tile), spread(ROWS, row, tile), pulls(row, tile)
            keep = 1.0 - 2.0 * (az + rad)
            border = edges[tile] - rate * under_edges[tile]
            for layer in range(2):
                low, high = (source(cells[tile, layer, half], rate) for half in range(2))
                side = pltpu.roll(border, (128 - 4 * row - 2 * layer) & 127, 1)
                low_up, high_up = pltpu.roll(low, 1, 1), pltpu.roll(high, 1, 1)
                low_down, high_down = pltpu.roll(low, 127, 1), pltpu.roll(high, 127, 1)
                low_sum = jnp.where(lane == 0, side, low_up) + jnp.where(lane == 127, high_down, low_down)
                high_sum = jnp.where(lane == 0, low_up, high_up) + jnp.where(lane == 127, side, high_down)
                full += [low, high]
                partial += [keep * low + az * low_sum, keep * high + az * high_sum]
        return full, partial

    def end(row, partial, under, over):
        for tile in range(2):
            rad = spread(ROWS, row, tile)
            for layer in range(2):
                for half in range(2):
                    at = 4 * tile + 2 * layer + half
                    done[pl.ds(place_of(row, tile, layer, half), 8), :] = partial[at] + rad * (under[at] + over[at])

    ends[...] = jnp.zeros(ends.shape, jnp.float32)
    for side, layer, half, first in windows():
        tile = lines[pl.ds(first, 8, stride=BLOCK), :]
        for place in range(5):
            turned = pltpu.roll(pltpu.roll(tile, 112 - 16 * place, 1), 0, 1, stride=16, stride_axis=0)
            cells = jnp.sum(jnp.where(lane >> 4 == line, turned, 0.0), axis=0, keepdims=True)
            ends[pl.ds(8 * (4 * side + 2 * layer + half) + place, 1), :] = cells

    def outer(side):
        rate = jnp.where(takes[0][0], outer_pull[side], 0.0)
        return [source(ends[pl.ds(32 * side + 8 * i, 8), :], rate) for i in range(4)]

    last, last_partial = begin(SPAN - 1)
    full, partial = begin(0)
    turned = [pltpu.roll(value, 5, 0) for value in last]
    under = [jnp.where(line < 5, value, turned[i]) for i, value in enumerate(outer(0))]
    under += [jnp.where(line < 5, turned[i], turned[4 + i]) for i in range(4)]
    turned = [pltpu.roll(value, 3, 0) for value in full]
    over = [jnp.where(line < 3, turned[i], turned[4 + i]) for i in range(4)]
    over += [jnp.where(line < 2, turned[4 + i], pltpu.roll(value, 2, 0)) for i, value in enumerate(outer(1))]
    for i in range(8):
        ends[pl.ds(64 + 8 * i, 8), :] = last[i]
        ends[pl.ds(128 + 8 * i, 8), :] = last_partial[i]
        ends[pl.ds(192 + 8 * i, 8), :] = over[i]

    def kept(first):
        return [ends[pl.ds(first + 8 * i, 8), :] for i in range(8)]

    def rows(pair, state):
        under, full, partial = state
        for row in (2 * pair + 1, 2 * pair + 2):
            over, later = begin(row)
            end(row - 1, partial, under, over)
            under, full, partial = full, over, later
        return under, full, partial

    def copies_of(part):
        for group in range(GROUPS):
            at = pl.ds(SPAN * group + 8 * part, 8)
            yield pltpu.make_async_copy(
                out.at[:, :, at, :], updated.at[:, :, at, :], sems.at[GROUPS * part + group]
            )

    def send(part):
        for place, field in enumerate(ORDER):
            for layer in range(2):
                for group in range(GROUPS):
                    for half in range(2):
                        first = 16 * BLOCK * part + BLOCK * layer + HALF * half + 5 * group + place
                        out[field, layer, pl.ds(SPAN * group + 8 * part, 8), pl.ds(128 * half, 128)] = done[
                            pl.ds(first, 8, stride=2 * BLOCK), :
                        ]
        for copy in copies_of(part):
            copy.start()

    state = under, full, partial
    for part in range(PARTS):
        state = lax.fori_loop(4 * part, min(4 * part + 4, SPAN // 2 - 1), rows, state)
        if part == PARTS - 1:
            under, full, partial = state
            end(SPAN - 2, partial, under, kept(64))
            end(SPAN - 1, kept(128), full, kept(192))
        send(part)
    for part in range(PARTS):
        for copy in copies_of(part):
            copy.wait()


def specs(*kinds):
    return [pl.BlockSpec(memory_space=kind) for kind in kinds]


def shards(fields, shifts, cycle_area, gravity, kappa_az, kappa_rad):
    vmem, smem = pltpu.VMEM, pltpu.SMEM
    params = pltpu.CompilerParams(vmem_limit_bytes=VMEM_LIMIT)
    blocks = jax.ShapeDtypeStruct((RING, BLOCK, 128), jnp.float32)

    def dealt(lines):
        return lax.all_to_all(lines, "az", 0, 0, tiled=True).reshape(RING * BLOCK, 128)

    ranks = lax.axis_size(RAD)
    packed = pl.pallas_call(
        pack_kernel,
        out_shape=blocks,
        in_specs=specs(pltpu.HBM, pltpu.HBM),
        out_specs=specs(pl.ANY)[0],
        scratch_shapes=[
            pltpu.VMEM(fields.shape, jnp.float32),
            pltpu.VMEM((RING * BLOCK, 128), jnp.float32),
            pltpu.SMEM(shifts.shape, jnp.int32),
            pltpu.SemaphoreType.DMA((GROUPS * PARTS + 1,)),
            pltpu.SemaphoreType.DMA((2 * PARTS + 1,)),
        ],
        compiler_params=pltpu.CompilerParams(vmem_limit_bytes=60 * 1024 * 1024),
        name="pack",
    )(shifts, fields)
    whole = dealt(packed)
    place = lax.axis_index("az").astype(jnp.int32)
    mine = lax.dynamic_slice(shifts.reshape(GROUPS, SPAN), (0, place // 2), (GROUPS, 1))[:, 0]
    end = jnp.where(place < RING // 2, shifts[ROWS - 1 :], shifts[:1])
    steps = jnp.concatenate([mine, end, place[None]])
    rates = jnp.concatenate([kappa_az, kappa_rad, gravity, cycle_area])
    steps, rates = lax.optimization_barrier((steps, rates))
    gravity, cycle_area = rates[2 * ROWS : 3 * ROWS], rates[3 * ROWS :]
    ends = pl.pallas_call(
        ends_kernel,
        out_shape=jax.ShapeDtypeStruct((RING, 128), jnp.float32),
        in_specs=specs(smem, vmem),
        out_specs=specs(vmem)[0],
        scratch_shapes=[pltpu.VMEM((2 * RING, 128), jnp.float32)],
        compiler_params=params,
        name="ends",
    )(steps, whole)
    outward = [(q * ranks + i, q * ranks + i + 1) for q in range(RING // 2) for i in range(ranks - 1)]
    inward = [(q * ranks + i + 1, q * ranks + i) for q in range(RING // 2, RING) for i in range(ranks - 1)]
    ends = lax.ppermute(ends, ("az",) + RAD, outward + inward)
    begun, tail, mass = pl.pallas_call(
        shift_kernel,
        out_shape=(
            blocks,
            jax.ShapeDtypeStruct((RING * 8, 128), jnp.float32),
            jax.ShapeDtypeStruct((8, 128), jnp.float32),
        ),
        in_specs=specs(smem, vmem),
        out_specs=specs(pl.ANY, vmem, vmem),
        scratch_shapes=[
            pltpu.VMEM((RING * BLOCK, 128), jnp.float32),
            pltpu.VMEM((128, 128), jnp.float32),
            pltpu.SemaphoreType.DMA((PIECES // STEP,)),
        ],
        compiler_params=params,
        name="shift",
    )(steps, whole)
    moved = pl.pallas_call(
        join_kernel,
        out_shape=blocks,
        in_specs=specs(vmem, vmem, pl.ANY),
        out_specs=specs(pl.ANY)[0],
        scratch_shapes=[pltpu.VMEM((RING * 8, 128), jnp.float32), pltpu.SemaphoreType.DMA],
        input_output_aliases={2: 0},
        compiler_params=params,
        name="join",
    )(tail, ends, begun)
    lines = dealt(moved)

    row_mass = cycle_area * mass[0, :ROWS] / (2.0 * RING * 256)
    row = jnp.arange(ROWS)
    inside = jnp.sum(jnp.where(row[None, :] < row[:, None], row_mass[None, :], 0.0), axis=1)
    local = inside + 0.5 * row_mass
    rates = jnp.concatenate([rates[: 3 * ROWS], local])
    kind, at = jnp.arange(8)[:, None], row[None, :]
    picked = jnp.where((kind == 1) & (at == 0) | (kind == 3) & (at == ROWS - 1), 0.5 * row_mass[None, :], 0.0)
    picked = jnp.where((kind == 2) & (at == 0) | (kind == 4) & (at == ROWS - 1), gravity[None, :], picked)
    ends = jnp.sum(jnp.where(kind == 0, row_mass[None, :], picked), axis=1)
    ends, local, rates = lax.optimization_barrier((ends, local, rates))
    totals = lax.all_gather(lax.all_gather(ends, "core"), "chip").reshape(ranks * 8)
    rank = lax.axis_index(RAD).astype(jnp.int32)[None]
    updated, enclosed = pl.pallas_call(
        spread_kernel,
        out_shape=(
            jax.ShapeDtypeStruct(fields.shape, jnp.float32),
            jax.ShapeDtypeStruct(gravity.shape, jnp.float32),
        ),
        in_specs=specs(smem, smem, smem, vmem, vmem),
        out_specs=specs(pl.ANY, vmem),
        scratch_shapes=[
            pltpu.VMEM((RING * BLOCK, 128), jnp.float32),
            pltpu.VMEM(fields.shape, jnp.float32),
            pltpu.VMEM((256, 128), jnp.float32),
            pltpu.VMEM((128, 128), jnp.float32),
            pltpu.SemaphoreType.DMA((GROUPS * PARTS,)),
        ],
        compiler_params=params,
        name="spread",
    )(rank, rates, totals, local, lines)
    return updated, enclosed


def solution(mesh):
    split = Mesh(mesh.devices.reshape(mesh.shape["az"], -1, 2), ("az",) + RAD)
    placed = (P(None, None, RAD, "az"), P(RAD), P(RAD), P(RAD), P(RAD), P(RAD))
    return jax.shard_map(
        shards,
        mesh=split,
        in_specs=placed,
        out_specs=(P(None, None, RAD, "az"), P(RAD)),
        check_vma=False,
    )
```

```python
import jax
import jax.numpy as jnp
from jax import lax
from jax.experimental import pallas as pl
from jax.experimental.pallas import tpu as pltpu
from jax.sharding import Mesh, PartitionSpec as P

star_mass = 1.0
RAD = ("chip", "core")

ORDER = (0, 1, 3, 2, 4)
RING = 64
GROUPS = 3
ROWS = 96
SPAN = ROWS // GROUPS
HALF = 16
BLOCK = 2 * HALF
PIECES = 2 * RING
PARTS = SPAN // 8
STEP = 32
VMEM_LIMIT = 24 * 1024 * 1024

TILES = ((0, 1, 5), (1, 2, 2))


def iotas():
    lane = lax.broadcasted_iota(jnp.int32, (8, 128), 1)
    line = lax.broadcasted_iota(jnp.int32, (8, 128), 0)
    return lane, line


def windows():
    for side in range(2):
        for layer in range(2):
            for half in range(2):
                yield side, layer, half, BLOCK * (32 * side + 16 * layer + 8 * half) + 31


def pack_kernel(given, fields, packed, cells, lines, shifts, sems, sent):
    lane, line = iotas()
    shift_copy = pltpu.make_async_copy(given, shifts, sems.at[GROUPS * PARTS])
    shift_copy.start()
    copies = {}
    for part, group in sorted(
        ((part, group) for part in range(PARTS) for group in range(GROUPS)),
        key=lambda at: at not in ((0, 0), (PARTS - 1, GROUPS - 1)),
    ):
        rows = pl.ds(SPAN * group + 8 * part, 8)
        copies[part, group] = pltpu.make_async_copy(
            fields.at[:, :, rows, :], cells.at[:, :, rows, :], sems.at[GROUPS * part + group]
        )
        copies[part, group].start()
    arrived = [(0, 0), (PARTS - 1, GROUPS - 1)]
    for at in arrived:
        copies[at].wait()
    shift_copy.wait()
    for side, layer, half, first in windows():
        row = (ROWS - 1) * (1 - side)
        part, odd = shifts[row] & 127, shifts[row] & 128
        tile = jnp.zeros((8, 128), jnp.float32)
        for place, field in enumerate(ORDER):
            low, high = (
                pltpu.roll(jnp.broadcast_to(cells[field, layer, pl.ds(row, 1), pl.ds(at, 128)], (8, 128)), part, 1)
                for at in (0, 128)
            )
            chosen = jnp.where((lane < part) ^ (odd != 0) ^ (half == 1), high, low)
            turned = pltpu.roll(chosen, 16 * (place + 1), 1)
            for bit in (1, 2, 4):
                turned = jnp.where(line & bit == 0, turned, pltpu.roll(turned, 128 - 16 * bit, 1))
            tile = jnp.where(lane >> 4 == place + 1, turned, tile)
        lines[pl.ds(first, 8, stride=BLOCK), :] = tile
    blocks = lines.reshape(RING, BLOCK, 128)
    sending = []

    def send(first, count, low, high):
        part = pl.ds(first, count), pl.ds(low, high - low)
        copy = pltpu.make_async_copy(blocks.at[part[0], part[1], :], packed.at[part[0], part[1], :], sent.at[len(sending)])
        copy.start()
        sending.append(copy)

    for part in range(PARTS):
        for group in range(GROUPS):
            if (part, group) not in arrived:
                copies[part, group].wait()
            taken = {}
            for place, field in enumerate(ORDER):
                for layer in range(2):
                    for half in range(2):
                        first = 16 * BLOCK * part + BLOCK * layer + HALF * half + 5 * group + place
                        taken[first] = cells[
                            field, layer, pl.ds(SPAN * group + 8 * part, 8), pl.ds(128 * half, 128)
                        ]
            for first, value in taken.items():
                lines[pl.ds(first, 8, stride=2 * BLOCK), :] = value
        send(16 * part, 16, 0, 8)
        send(16 * part, 16, 16, 32)
    halves = [cells[0, z, :, pl.ds(128 * h, 128)] for z in range(2) for h in range(2)]
    total = (halves[0] + halves[1]) + (halves[2] + halves[3])
    square = jnp.concatenate([total, jnp.zeros((128 - ROWS, 128), jnp.float32)], axis=0)
    mass = jnp.sum(square.T, axis=0, keepdims=True)
    lines[pl.ds(15, RING, stride=BLOCK), :] = jnp.broadcast_to(mass, (RING, 128))
    send(0, RING, 8, 16)
    for copy in sending:
        copy.wait()


def ends_kernel(steps, lines, moved, twice):
    cells = lines[pl.ds(31, RING, stride=BLOCK), :]
    twice[pl.ds(0, RING), :] = cells
    twice[pl.ds(RING, RING), :] = cells
    shift = steps[3]
    lane = lax.broadcasted_iota(jnp.int32, (RING, 128), 1)
    crossed = (lane & 15) + 16 * (steps[4] & 15) < (shift & 255)
    blocks = shift >> 8
    moved[...] = jnp.where(crossed, twice[pl.ds(RING - 1 - blocks, RING), :], twice[pl.ds(RING - blocks, RING), :])


def join_kernel(tail, ends, begun, moved, rows, sem):
    rows[...] = tail[...]
    lane = lax.broadcasted_iota(jnp.int32, (RING, 128), 1)
    last = pl.ds(7, RING, stride=8)
    rows[last, :] = jnp.where((lane < 16) | (lane >= 96), tail[last, :], ends[...])
    copy = pltpu.make_async_copy(rows.reshape(RING, 8, 128), moved.at[:, pl.ds(24, 8), :], sem)
    copy.start()
    copy.wait()


def shift_kernel(steps, lines, begun, tail, mass, moved, square, sems):
    lane, line = iotas()
    blocks = moved.reshape(RING, BLOCK, 128)

    def copy_of(quarter):
        part = pl.ds(quarter * (RING // 4), RING // 4)
        return pltpu.make_async_copy(
            blocks.at[part, pl.ds(0, 24), :], begun.at[part, pl.ds(0, 24), :], sems.at[quarter]
        )

    whole, part, early = [], [], []
    for group in range(GROUPS):
        shift = steps[group]
        whole.append(shift >> 7)
        part.append(shift & 127)
        early.append(lane < part[group])

    def piece_of(piece, tile, group):
        at = pl.multiple_of(((piece - whole[group]) & (PIECES - 1)) * HALF + 8 * tile, 8)
        return lines[pl.ds(at, 8), :]

    def turned(value, group):
        return pltpu.roll(value, part[group], 1)

    def several(step, state):
        before, edges = state
        edges = list(edges)
        first_piece = step * STEP
        loaded = [
            [[piece_of(first_piece + i, tile, group) for group in TILES[tile][:2]] for tile in range(2)]
            for i in range(STEP)
        ]
        values = []
        for i in range(STEP):
            now, made = [], []
            for tile, (first, second, split) in enumerate(TILES):
                a, b = turned(loaded[i][tile][0], first), turned(loaded[i][tile][1], second)
                pa, pb = before[tile]
                made.append(
                    jnp.where(line < split, jnp.where(early[first], pa, a), jnp.where(early[second], pb, b))
                )
                now.append((a, b))
            before = tuple(now)
            values.append(made)
        for i in range(0, STEP, 2):
            ring = step * (STEP // 2) + i // 2
            for tile in range(2):
                both = jnp.where(lane == 127, values[i + 1][tile], values[i][tile])
                edges[tile] = jnp.where(lane >> 1 == ring, pltpu.roll(both, (2 * ring + 1) & 127, 1), edges[tile])
        for i in range(STEP):
            for tile in range(2):
                if i % 2 == 1 and tile == 1:
                    at = pl.multiple_of((first_piece + i) // 2 * 8, 8)
                    tail[pl.ds(at, 8), :] = values[i][tile]
                else:
                    at = pl.multiple_of((first_piece + i) * HALF + 8 * tile, 8)
                    moved[pl.ds(at, 8), :] = values[i][tile]
        return before, tuple(edges)

    before = tuple(
        tuple(turned(piece_of(PIECES - 1, tile, group), group) for group in TILES[tile][:2]) for tile in range(2)
    )
    zero = jnp.zeros((8, 128), jnp.float32)
    state = before, (zero, zero)
    steps_each = PIECES // STEP // 4
    for quarter in range(4):
        state = lax.fori_loop(steps_each * quarter, steps_each * (quarter + 1), several, state)
        copy_of(quarter).start()
    _, edges = state
    square[...] = jnp.concatenate([edges[0], edges[1], jnp.zeros((112, 128), jnp.float32)], axis=0).T
    left = pltpu.roll(square[pl.ds(0, RING, stride=2), :], 96, 1)
    right = square[pl.ds(1, RING, stride=2), :]
    left = jnp.concatenate([left[RING - 1 :], left[: RING - 1]], axis=0)
    right = jnp.concatenate([right[1:], right[:1]], axis=0)
    tail[pl.ds(7, RING, stride=8), :] = left + right
    parts = lines[pl.ds(15, RING, stride=BLOCK), :]
    mass[...] = jnp.broadcast_to(jnp.sum(parts, axis=0, keepdims=True), (8, 128))

    for quarter in range(4):
        copy_of(quarter).wait()


def spread_kernel(rank, rates, totals, local, lines, updated, enclosed, done, ends, square):
    lane, line = iotas()
    here = rank[0]
    base = jnp.float32(star_mass)
    for other in range(totals.shape[0] // 8):
        base = base + jnp.where(other < here, totals[8 * other], 0.0)
    below = 8 * jnp.maximum(here - 1, 0)
    above = 8 * jnp.minimum(here + 1, totals.shape[0] // 8 - 1)
    outer_pull = (
        totals[below + 4] * (base - totals[below + 3]),
        totals[above + 2] * (base + totals[8 * here] + totals[above + 1]),
    )
    enclosed[...] = local[...] + base

    borders = lines[pl.ds(31, RING, stride=BLOCK), :]
    square[pl.ds(0, RING, stride=2), :] = pltpu.roll(borders, 32, 1)
    square[pl.ds(1, RING - 1, stride=2), :] = lines[pl.ds(BLOCK + 31, RING - 1, stride=BLOCK), :]
    square[pl.ds(127, 1), :] = lines[pl.ds(31, 1), :]
    across = square[...].T
    edges = across[0:8], across[8:16]
    under_edges = tuple(pltpu.roll(value, 1, 0) for value in edges)
    takes = (((line == 1) | (line == 2), (line == 6) | (line == 7)), (None, (line == 3) | (line == 4)))

    def spread(first_rate, row, tile):
        first, second, split = TILES[tile]
        return jnp.where(
            line < split, rates[first_rate + SPAN * first + row], rates[first_rate + SPAN * second + row]
        )

    def pull(row):
        return rates[2 * ROWS + row] * (base + rates[3 * ROWS + row])

    def pulls(row, tile):
        first, second, _ = TILES[tile]
        other = jnp.where(takes[tile][1], pull(SPAN * second + row), 0.0)
        if takes[tile][0] is None:
            return other
        return jnp.where(takes[tile][0], pull(SPAN * first + row), other)

    def source(value, rate):
        return value - rate * pltpu.roll(value, 1, 0)

    def spots():
        return ((tile, layer, half) for tile in range(2) for layer in range(2) for half in range(2))

    def place_of(row, tile, layer, half):
        return pl.multiple_of((2 * row + layer) * BLOCK + HALF * half + 8 * tile, 8)

    def begin(row):
        cells = {spot: lines[pl.ds(place_of(row, *spot), 8), :] for spot in spots()}
        full, partial = [], []
        for tile in range(2):
            az, rad, rate = spread(0, row, tile), spread(ROWS, row, tile), pulls(row, tile)
            keep = 1.0 - 2.0 * (az + rad)
            border = edges[tile] - rate * under_edges[tile]
            for layer in range(2):
                low, high = (source(cells[tile, layer, half], rate) for half in range(2))
                side = pltpu.roll(border, (128 - 4 * row - 2 * layer) & 127, 1)
                low_up, high_up = pltpu.roll(low, 1, 1), pltpu.roll(high, 1, 1)
                low_down, high_down = pltpu.roll(low, 127, 1), pltpu.roll(high, 127, 1)
                low_sum = jnp.where(lane == 0, side, low_up) + jnp.where(lane == 127, high_down, low_down)
                high_sum = jnp.where(lane == 0, low_up, high_up) + jnp.where(lane == 127, side, high_down)
                full += [low, high]
                partial += [keep * low + az * low_sum, keep * high + az * high_sum]
        return full, partial

    def end(row, partial, under, over):
        for tile in range(2):
            rad = spread(ROWS, row, tile)
            for layer in range(2):
                for half in range(2):
                    at = 4 * tile + 2 * layer + half
                    done[pl.ds(place_of(row, tile, layer, half), 8), :] = partial[at] + rad * (under[at] + over[at])

    ends[...] = jnp.zeros(ends.shape, jnp.float32)
    for side, layer, half, first in windows():
        tile = lines[pl.ds(first, 8, stride=BLOCK), :]
        for place in range(5):
            turned = pltpu.roll(pltpu.roll(tile, 112 - 16 * place, 1), 0, 1, stride=16, stride_axis=0)
            cells = jnp.sum(jnp.where(lane >> 4 == line, turned, 0.0), axis=0, keepdims=True)
            ends[pl.ds(8 * (4 * side + 2 * layer + half) + place, 1), :] = cells

    def outer(side):
        rate = jnp.where(takes[0][0], outer_pull[side], 0.0)
        return [source(ends[pl.ds(32 * side + 8 * i, 8), :], rate) for i in range(4)]

    last, last_partial = begin(SPAN - 1)
    full, partial = begin(0)
    turned = [pltpu.roll(value, 5, 0) for value in last]
    under = [jnp.where(line < 5, value, turned[i]) for i, value in enumerate(outer(0))]
    under += [jnp.where(line < 5, turned[i], turned[4 + i]) for i in range(4)]
    turned = [pltpu.roll(value, 3, 0) for value in full]
    over = [jnp.where(line < 3, turned[i], turned[4 + i]) for i in range(4)]
    over += [jnp.where(line < 2, turned[4 + i], pltpu.roll(value, 2, 0)) for i, value in enumerate(outer(1))]
    for i in range(8):
        ends[pl.ds(64 + 8 * i, 8), :] = last[i]
        ends[pl.ds(128 + 8 * i, 8), :] = last_partial[i]
        ends[pl.ds(192 + 8 * i, 8), :] = over[i]

    def kept(first):
        return [ends[pl.ds(first + 8 * i, 8), :] for i in range(8)]

    def rows(step, state):
        under, full, partial = state
        for row in range(30):
            row = 30 * step + row + 1
            over, later = begin(row)
            end(row - 1, partial, under, over)
            under, full, partial = full, over, later
        return under, full, partial

    under, full, partial = lax.fori_loop(0, (SPAN - 2) // 30, rows, (under, full, partial))
    end(SPAN - 2, partial, under, kept(64))
    end(SPAN - 1, kept(128), full, kept(192))
    for place, field in enumerate(ORDER):
        for layer in range(2):
            taken = {}
            for group in range(GROUPS):
                for half in range(2):
                    first = BLOCK * layer + HALF * half + 5 * group + place
                    taken[group, half] = done[pl.ds(first, SPAN, stride=2 * BLOCK), :]
            for (group, half), value in taken.items():
                updated[field, layer, pl.ds(SPAN * group, SPAN), pl.ds(128 * half, 128)] = value


def specs(*kinds):
    return [pl.BlockSpec(memory_space=kind) for kind in kinds]


def shards(fields, shifts, cycle_area, gravity, kappa_az, kappa_rad):
    vmem, smem = pltpu.VMEM, pltpu.SMEM
    params = pltpu.CompilerParams(vmem_limit_bytes=VMEM_LIMIT)
    blocks = jax.ShapeDtypeStruct((RING, BLOCK, 128), jnp.float32)

    def dealt(lines):
        return lax.all_to_all(lines, "az", 0, 0, tiled=True).reshape(RING * BLOCK, 128)

    ranks = lax.axis_size(RAD)
    packed = pl.pallas_call(
        pack_kernel,
        out_shape=blocks,
        in_specs=specs(pltpu.HBM, pltpu.HBM),
        out_specs=specs(pl.ANY)[0],
        scratch_shapes=[
            pltpu.VMEM(fields.shape, jnp.float32),
            pltpu.VMEM((RING * BLOCK, 128), jnp.float32),
            pltpu.SMEM(shifts.shape, jnp.int32),
            pltpu.SemaphoreType.DMA((GROUPS * PARTS + 1,)),
            pltpu.SemaphoreType.DMA((2 * PARTS + 1,)),
        ],
        compiler_params=pltpu.CompilerParams(vmem_limit_bytes=60 * 1024 * 1024),
        name="pack",
    )(shifts, fields)
    whole = dealt(packed)
    place = lax.axis_index("az").astype(jnp.int32)
    mine = lax.dynamic_slice(shifts.reshape(GROUPS, SPAN), (0, place // 2), (GROUPS, 1))[:, 0]
    end = jnp.where(place < RING // 2, shifts[ROWS - 1 :], shifts[:1])
    steps = jnp.concatenate([mine, end, place[None]])
    rates = jnp.concatenate([kappa_az, kappa_rad, gravity, cycle_area])
    steps, rates = lax.optimization_barrier((steps, rates))
    gravity, cycle_area = rates[2 * ROWS : 3 * ROWS], rates[3 * ROWS :]
    ends = pl.pallas_call(
        ends_kernel,
        out_shape=jax.ShapeDtypeStruct((RING, 128), jnp.float32),
        in_specs=specs(smem, vmem),
        out_specs=specs(vmem)[0],
        scratch_shapes=[pltpu.VMEM((2 * RING, 128), jnp.float32)],
        compiler_params=params,
        name="ends",
    )(steps, whole)
    outward = [(q * ranks + i, q * ranks + i + 1) for q in range(RING // 2) for i in range(ranks - 1)]
    inward = [(q * ranks + i + 1, q * ranks + i) for q in range(RING // 2, RING) for i in range(ranks - 1)]
    ends = lax.ppermute(ends, ("az",) + RAD, outward + inward)
    begun, tail, mass = pl.pallas_call(
        shift_kernel,
        out_shape=(
            blocks,
            jax.ShapeDtypeStruct((RING * 8, 128), jnp.float32),
            jax.ShapeDtypeStruct((8, 128), jnp.float32),
        ),
        in_specs=specs(smem, vmem),
        out_specs=specs(pl.ANY, vmem, vmem),
        scratch_shapes=[
            pltpu.VMEM((RING * BLOCK, 128), jnp.float32),
            pltpu.VMEM((128, 128), jnp.float32),
            pltpu.SemaphoreType.DMA((4,)),
        ],
        compiler_params=params,
        name="shift",
    )(steps, whole)
    moved = pl.pallas_call(
        join_kernel,
        out_shape=blocks,
        in_specs=specs(vmem, vmem, pl.ANY),
        out_specs=specs(pl.ANY)[0],
        scratch_shapes=[pltpu.VMEM((RING * 8, 128), jnp.float32), pltpu.SemaphoreType.DMA],
        input_output_aliases={2: 0},
        compiler_params=params,
        name="join",
    )(tail, ends, begun)
    lines = dealt(moved)

    row_mass = cycle_area * mass[0, :ROWS] / (2.0 * RING * 256)
    row = jnp.arange(ROWS)
    inside = jnp.sum(jnp.where(row[None, :] < row[:, None], row_mass[None, :], 0.0), axis=1)
    local = inside + 0.5 * row_mass
    rates = jnp.concatenate([rates[: 3 * ROWS], local])
    kind, at = jnp.arange(8)[:, None], row[None, :]
    picked = jnp.where((kind == 1) & (at == 0) | (kind == 3) & (at == ROWS - 1), 0.5 * row_mass[None, :], 0.0)
    picked = jnp.where((kind == 2) & (at == 0) | (kind == 4) & (at == ROWS - 1), gravity[None, :], picked)
    ends = jnp.sum(jnp.where(kind == 0, row_mass[None, :], picked), axis=1)
    ends, local, rates = lax.optimization_barrier((ends, local, rates))
    totals = lax.all_gather(lax.all_gather(ends, "core"), "chip").reshape(ranks * 8)
    rank = lax.axis_index(RAD).astype(jnp.int32)[None]
    updated, enclosed = pl.pallas_call(
        spread_kernel,
        out_shape=(
            jax.ShapeDtypeStruct(fields.shape, jnp.float32),
            jax.ShapeDtypeStruct(gravity.shape, jnp.float32),
        ),
        in_specs=specs(smem, smem, smem, vmem, vmem),
        out_specs=specs(vmem, vmem),
        scratch_shapes=[
            pltpu.VMEM((RING * BLOCK, 128), jnp.float32),
            pltpu.VMEM((256, 128), jnp.float32),
            pltpu.VMEM((128, 128), jnp.float32),
        ],
        compiler_params=params,
        name="spread",
    )(rank, rates, totals, local, lines)
    return updated, enclosed


def solution(mesh):
    split = Mesh(mesh.devices.reshape(mesh.shape["az"], -1, 2), ("az",) + RAD)
    placed = (P(None, None, RAD, "az"), P(RAD), P(RAD), P(RAD), P(RAD), P(RAD))
    return jax.shard_map(
        shards,
        mesh=split,
        in_specs=placed,
        out_specs=(P(None, None, RAD, "az"), P(RAD)),
        check_vma=False,
    )
```

```python
import jax
import jax.numpy as jnp
from jax import lax
from jax.experimental import pallas as pl
from jax.experimental.pallas import tpu as pltpu
from jax.sharding import Mesh, PartitionSpec as P

star_mass = 1.0
RAD = ("chip", "core")

ORDER = (0, 1, 3, 2, 4)
RING = 64
GROUPS = 3
ROWS = 96
SPAN = ROWS // GROUPS
HALF = 16
BLOCK = 2 * HALF
PIECES = 2 * RING
PARTS = SPAN // 8
STEP = 32
VMEM_LIMIT = 24 * 1024 * 1024

TILES = ((0, 1, 5), (1, 2, 2))


def iotas():
    lane = lax.broadcasted_iota(jnp.int32, (8, 128), 1)
    line = lax.broadcasted_iota(jnp.int32, (8, 128), 0)
    return lane, line


def windows():
    for side in range(2):
        for layer in range(2):
            for half in range(2):
                yield side, layer, half, BLOCK * (32 * side + 16 * layer + 8 * half) + 31


def pack_kernel(given, fields, packed, cells, lines, shifts, sems, sent):
    lane, line = iotas()
    shift_copy = pltpu.make_async_copy(given, shifts, sems.at[GROUPS * PARTS])
    shift_copy.start()
    copies = {}
    for part, group in sorted(
        ((part, group) for part in range(PARTS) for group in range(GROUPS)),
        key=lambda at: at not in ((0, 0), (PARTS - 1, GROUPS - 1)),
    ):
        rows = pl.ds(SPAN * group + 8 * part, 8)
        copies[part, group] = pltpu.make_async_copy(
            fields.at[:, :, rows, :], cells.at[:, :, rows, :], sems.at[GROUPS * part + group]
        )
        copies[part, group].start()
    arrived = [(0, 0), (PARTS - 1, GROUPS - 1)]
    for at in arrived:
        copies[at].wait()
    shift_copy.wait()
    turned = {}
    for side in range(2):
        row = (ROWS - 1) * (1 - side)
        part = shifts[row] & 127
        for layer in range(2):
            for half in range(2):
                tile = jnp.zeros((8, 128), jnp.float32)
                for place, field in enumerate(ORDER):
                    cell = cells[field, layer, pl.ds(row, 1), pl.ds(128 * half, 128)]
                    tile = jnp.where(line == place, jnp.broadcast_to(cell, (8, 128)), tile)
                turned[side, layer, half] = pltpu.roll(tile, part, 1)
    for side, layer, half, first in windows():
        shift = shifts[(ROWS - 1) * (1 - side)]
        swapped = (lane < (shift & 127)) ^ (shift & 128 != 0) ^ (half == 1)
        lines[pl.ds(first, 8, stride=BLOCK), :] = jnp.where(swapped, turned[side, layer, 1], turned[side, layer, 0])
    blocks = lines.reshape(RING, BLOCK, 128)
    sending = []

    def send(first, count, low, high):
        part = pl.ds(first, count), pl.ds(low, high - low)
        copy = pltpu.make_async_copy(blocks.at[part[0], part[1], :], packed.at[part[0], part[1], :], sent.at[len(sending)])
        copy.start()
        sending.append(copy)

    for part in range(PARTS):
        for group in range(GROUPS):
            if (part, group) not in arrived:
                copies[part, group].wait()
            taken = {}
            for place, field in enumerate(ORDER):
                for layer in range(2):
                    for half in range(2):
                        first = 16 * BLOCK * part + BLOCK * layer + HALF * half + 5 * group + place
                        taken[first] = cells[
                            field, layer, pl.ds(SPAN * group + 8 * part, 8), pl.ds(128 * half, 128)
                        ]
            for first, value in taken.items():
                lines[pl.ds(first, 8, stride=2 * BLOCK), :] = value
        send(16 * part, 16, 0, 8)
        send(16 * part, 16, 16, 32)
    halves = [cells[0, z, :, pl.ds(128 * h, 128)] for z in range(2) for h in range(2)]
    total = (halves[0] + halves[1]) + (halves[2] + halves[3])
    square = jnp.concatenate([total, jnp.zeros((128 - ROWS, 128), jnp.float32)], axis=0)
    mass = jnp.sum(square.T, axis=0, keepdims=True)
    lines[pl.ds(15, RING, stride=BLOCK), :] = jnp.broadcast_to(mass, (RING, 128))
    send(0, RING, 8, 16)
    for copy in sending:
        copy.wait()


def ends_kernel(steps, lines, moved, twice):
    cells = lines[pl.ds(31, RING, stride=BLOCK), :]
    twice[pl.ds(0, RING), :] = cells
    twice[pl.ds(RING, RING), :] = cells
    shift = steps[3]
    lane = lax.broadcasted_iota(jnp.int32, (RING, 128), 1)
    crossed = lane + 16 * (steps[4] & 8) < (shift & 255)
    blocks = shift >> 8
    moved[...] = jnp.where(crossed, twice[pl.ds(RING - 1 - blocks, RING), :], twice[pl.ds(RING - blocks, RING), :])


def join_kernel(tail, ends, begun, moved, rows, sem):
    rows[...] = tail[...]
    rows[pl.ds(7, RING, stride=8), :] = ends[...]
    copy = pltpu.make_async_copy(rows.reshape(RING, 8, 128), moved.at[:, pl.ds(24, 8), :], sem)
    copy.start()
    copy.wait()


def shift_kernel(steps, lines, begun, tail, mass, square):
    lane, line = iotas()
    moved = begun.reshape(RING * BLOCK, 128)
    whole, part, early = [], [], []
    for group in range(GROUPS):
        shift = steps[group]
        whole.append(shift >> 7)
        part.append(shift & 127)
        early.append(lane < part[group])

    def piece_of(piece, tile, group):
        at = pl.multiple_of(((piece - whole[group]) & (PIECES - 1)) * HALF + 8 * tile, 8)
        return lines[pl.ds(at, 8), :]

    def turned(value, group):
        return pltpu.roll(value, part[group], 1)

    def several(step, state):
        before, edges = state
        edges = list(edges)
        first_piece = step * STEP
        loaded = [
            [[piece_of(first_piece + i, tile, group) for group in TILES[tile][:2]] for tile in range(2)]
            for i in range(STEP)
        ]
        values = []
        for i in range(STEP):
            now, made = [], []
            for tile, (first, second, split) in enumerate(TILES):
                a, b = turned(loaded[i][tile][0], first), turned(loaded[i][tile][1], second)
                pa, pb = before[tile]
                made.append(
                    jnp.where(line < split, jnp.where(early[first], pa, a), jnp.where(early[second], pb, b))
                )
                now.append((a, b))
            before = tuple(now)
            values.append(made)
        for i in range(0, STEP, 2):
            ring = step * (STEP // 2) + i // 2
            for tile in range(2):
                both = jnp.where(lane == 127, values[i + 1][tile], values[i][tile])
                edges[tile] = jnp.where(lane >> 1 == ring, pltpu.roll(both, (2 * ring + 1) & 127, 1), edges[tile])
        for i in range(STEP):
            for tile in range(2):
                if i % 2 == 1 and tile == 1:
                    at = pl.multiple_of((first_piece + i) // 2 * 8, 8)
                    tail[pl.ds(at, 8), :] = values[i][tile]
                else:
                    at = pl.multiple_of((first_piece + i) * HALF + 8 * tile, 8)
                    moved[pl.ds(at, 8), :] = values[i][tile]
        return before, tuple(edges)

    before = tuple(
        tuple(turned(piece_of(PIECES - 1, tile, group), group) for group in TILES[tile][:2]) for tile in range(2)
    )
    zero = jnp.zeros((8, 128), jnp.float32)
    state = before, (zero, zero)
    steps_each = PIECES // STEP // 4
    for quarter in range(4):
        state = lax.fori_loop(steps_each * quarter, steps_each * (quarter + 1), several, state)
    _, edges = state
    square[...] = jnp.concatenate([edges[0], edges[1], jnp.zeros((112, 128), jnp.float32)], axis=0).T
    left = square[pl.ds(0, RING, stride=2), :]
    right = square[pl.ds(1, RING, stride=2), :]
    left = jnp.concatenate([left[RING - 1 :], left[: RING - 1]], axis=0)
    right = jnp.concatenate([right[1:], right[:1]], axis=0)
    moved[pl.ds(15, RING, stride=BLOCK), :] = left + pltpu.roll(right, 16, 1)
    parts = lines[pl.ds(15, RING, stride=BLOCK), :]
    mass[...] = jnp.broadcast_to(jnp.sum(parts, axis=0, keepdims=True), (8, 128))


def spread_kernel(rank, rates, totals, local, lines, updated, enclosed, done, ends, square):
    lane, line = iotas()
    here = rank[0]
    base = jnp.float32(star_mass)
    for other in range(totals.shape[0] // 8):
        base = base + jnp.where(other < here, totals[8 * other], 0.0)
    below = 8 * jnp.maximum(here - 1, 0)
    above = 8 * jnp.minimum(here + 1, totals.shape[0] // 8 - 1)
    outer_pull = (
        totals[below + 4] * (base - totals[below + 3]),
        totals[above + 2] * (base + totals[8 * here] + totals[above + 1]),
    )
    enclosed[...] = local[...] + base

    borders = lines[pl.ds(15, RING, stride=BLOCK), :]
    square[pl.ds(0, RING, stride=2), :] = borders
    borders = pltpu.roll(borders, 112, 1)
    square[pl.ds(1, RING, stride=2), :] = jnp.concatenate([borders[1:], borders[:1]], axis=0)
    across = square[...].T
    edges = across[0:8], across[8:16]
    under_edges = tuple(pltpu.roll(value, 1, 0) for value in edges)
    takes = (((line == 1) | (line == 2), (line == 6) | (line == 7)), (None, (line == 3) | (line == 4)))

    def spread(first_rate, row, tile):
        first, second, split = TILES[tile]
        return jnp.where(
            line < split, rates[first_rate + SPAN * first + row], rates[first_rate + SPAN * second + row]
        )

    def pull(row):
        return rates[2 * ROWS + row] * (base + rates[3 * ROWS + row])

    def pulls(row, tile):
        first, second, _ = TILES[tile]
        other = jnp.where(takes[tile][1], pull(SPAN * second + row), 0.0)
        if takes[tile][0] is None:
            return other
        return jnp.where(takes[tile][0], pull(SPAN * first + row), other)

    def source(value, rate):
        return value - rate * pltpu.roll(value, 1, 0)

    def spots():
        return ((tile, layer, half) for tile in range(2) for layer in range(2) for half in range(2))

    def place_of(row, tile, layer, half):
        return pl.multiple_of((2 * row + layer) * BLOCK + HALF * half + 8 * tile, 8)

    def begin(row):
        cells = {spot: lines[pl.ds(place_of(row, *spot), 8), :] for spot in spots()}
        full, partial = [], []
        for tile in range(2):
            az, rad, rate = spread(0, row, tile), spread(ROWS, row, tile), pulls(row, tile)
            keep = 1.0 - 2.0 * (az + rad)
            border = edges[tile] - rate * under_edges[tile]
            for layer in range(2):
                low, high = (source(cells[tile, layer, half], rate) for half in range(2))
                side = pltpu.roll(border, (128 - 4 * row - 2 * layer) & 127, 1)
                low_up, high_up = pltpu.roll(low, 1, 1), pltpu.roll(high, 1, 1)
                low_down, high_down = pltpu.roll(low, 127, 1), pltpu.roll(high, 127, 1)
                low_sum = jnp.where(lane == 0, side, low_up) + jnp.where(lane == 127, high_down, low_down)
                high_sum = jnp.where(lane == 0, low_up, high_up) + jnp.where(lane == 127, side, high_down)
                full += [low, high]
                partial += [keep * low + az * low_sum, keep * high + az * high_sum]
        return full, partial

    def end(row, partial, under, over):
        for tile in range(2):
            rad = spread(ROWS, row, tile)
            for layer in range(2):
                for half in range(2):
                    at = 4 * tile + 2 * layer + half
                    done[pl.ds(place_of(row, tile, layer, half), 8), :] = partial[at] + rad * (under[at] + over[at])

    def outer(side):
        rate = jnp.where(takes[0][0], outer_pull[side], 0.0)
        return [
            source(lines[pl.ds(first, 8, stride=BLOCK), :], rate) for at, _, _, first in windows() if at == side
        ]

    last, last_partial = begin(SPAN - 1)
    full, partial = begin(0)
    turned = [pltpu.roll(value, 5, 0) for value in last]
    under = [jnp.where(line < 5, value, turned[i]) for i, value in enumerate(outer(0))]
    under += [jnp.where(line < 5, turned[i], turned[4 + i]) for i in range(4)]
    turned = [pltpu.roll(value, 3, 0) for value in full]
    over = [jnp.where(line < 3, turned[i], turned[4 + i]) for i in range(4)]
    over += [jnp.where(line < 2, turned[4 + i], pltpu.roll(value, 2, 0)) for i, value in enumerate(outer(1))]
    for i in range(8):
        ends[pl.ds(64 + 8 * i, 8), :] = last[i]
        ends[pl.ds(128 + 8 * i, 8), :] = last_partial[i]
        ends[pl.ds(192 + 8 * i, 8), :] = over[i]

    def kept(first):
        return [ends[pl.ds(first + 8 * i, 8), :] for i in range(8)]

    def rows(step, state):
        under, full, partial = state
        for row in range(30):
            row = 30 * step + row + 1
            over, later = begin(row)
            end(row - 1, partial, under, over)
            under, full, partial = full, over, later
        return under, full, partial

    under, full, partial = lax.fori_loop(0, (SPAN - 2) // 30, rows, (under, full, partial))
    end(SPAN - 2, partial, under, kept(64))
    end(SPAN - 1, kept(128), full, kept(192))
    for place, field in enumerate(ORDER):
        for layer in range(2):
            taken = {}
            for group in range(GROUPS):
                for half in range(2):
                    first = BLOCK * layer + HALF * half + 5 * group + place
                    taken[group, half] = done[pl.ds(first, SPAN, stride=2 * BLOCK), :]
            for (group, half), value in taken.items():
                updated[field, layer, pl.ds(SPAN * group, SPAN), pl.ds(128 * half, 128)] = value


def specs(*kinds):
    return [pl.BlockSpec(memory_space=kind) for kind in kinds]


def shards(fields, shifts, cycle_area, gravity, kappa_az, kappa_rad):
    vmem, smem = pltpu.VMEM, pltpu.SMEM
    params = pltpu.CompilerParams(vmem_limit_bytes=VMEM_LIMIT)
    blocks = jax.ShapeDtypeStruct((RING, BLOCK, 128), jnp.float32)

    def dealt(lines):
        return lax.all_to_all(lines, "az", 0, 0, tiled=True).reshape(RING * BLOCK, 128)

    ranks = lax.axis_size(RAD)
    packed = pl.pallas_call(
        pack_kernel,
        out_shape=blocks,
        in_specs=specs(pltpu.HBM, pltpu.HBM),
        out_specs=specs(pl.ANY)[0],
        scratch_shapes=[
            pltpu.VMEM(fields.shape, jnp.float32),
            pltpu.VMEM((RING * BLOCK, 128), jnp.float32),
            pltpu.SMEM(shifts.shape, jnp.int32),
            pltpu.SemaphoreType.DMA((GROUPS * PARTS + 1,)),
            pltpu.SemaphoreType.DMA((2 * PARTS + 1,)),
        ],
        compiler_params=pltpu.CompilerParams(vmem_limit_bytes=60 * 1024 * 1024),
        name="pack",
    )(shifts, fields)
    whole = dealt(packed)
    place = lax.axis_index("az").astype(jnp.int32)
    mine = lax.dynamic_slice(shifts.reshape(GROUPS, SPAN), (0, place // 2), (GROUPS, 1))[:, 0]
    end = jnp.where(place < RING // 2, shifts[ROWS - 1 :], shifts[:1])
    steps = jnp.concatenate([mine, end, place[None]])
    rates = jnp.concatenate([kappa_az, kappa_rad, gravity, cycle_area])
    steps, rates = lax.optimization_barrier((steps, rates))
    gravity, cycle_area = rates[2 * ROWS : 3 * ROWS], rates[3 * ROWS :]
    ends = pl.pallas_call(
        ends_kernel,
        out_shape=jax.ShapeDtypeStruct((RING, 128), jnp.float32),
        in_specs=specs(smem, vmem),
        out_specs=specs(vmem)[0],
        scratch_shapes=[pltpu.VMEM((2 * RING, 128), jnp.float32)],
        compiler_params=params,
        name="ends",
    )(steps, whole)
    outward = [(q * ranks + i, q * ranks + i + 1) for q in range(RING // 2) for i in range(ranks - 1)]
    inward = [(q * ranks + i + 1, q * ranks + i) for q in range(RING // 2, RING) for i in range(ranks - 1)]
    ends = lax.ppermute(ends, ("az",) + RAD, outward + inward)
    begun, tail, mass = pl.pallas_call(
        shift_kernel,
        out_shape=(
            blocks,
            jax.ShapeDtypeStruct((RING * 8, 128), jnp.float32),
            jax.ShapeDtypeStruct((8, 128), jnp.float32),
        ),
        in_specs=specs(smem, vmem),
        out_specs=specs(vmem, vmem, vmem),
        scratch_shapes=[pltpu.VMEM((128, 128), jnp.float32)],
        compiler_params=params,
        name="shift",
    )(steps, whole)
    moved = pl.pallas_call(
        join_kernel,
        out_shape=blocks,
        in_specs=specs(vmem, vmem, pl.ANY),
        out_specs=specs(pl.ANY)[0],
        scratch_shapes=[pltpu.VMEM((RING * 8, 128), jnp.float32), pltpu.SemaphoreType.DMA],
        input_output_aliases={2: 0},
        compiler_params=params,
        name="join",
    )(tail, ends, begun)
    lines = dealt(moved)

    row_mass = cycle_area * mass[0, :ROWS] / (2.0 * RING * 256)
    row = jnp.arange(ROWS)
    inside = jnp.sum(jnp.where(row[None, :] < row[:, None], row_mass[None, :], 0.0), axis=1)
    local = inside + 0.5 * row_mass
    rates = jnp.concatenate([rates[: 3 * ROWS], local])
    kind, at = jnp.arange(8)[:, None], row[None, :]
    picked = jnp.where((kind == 1) & (at == 0) | (kind == 3) & (at == ROWS - 1), 0.5 * row_mass[None, :], 0.0)
    picked = jnp.where((kind == 2) & (at == 0) | (kind == 4) & (at == ROWS - 1), gravity[None, :], picked)
    ends = jnp.sum(jnp.where(kind == 0, row_mass[None, :], picked), axis=1)
    ends, local, rates = lax.optimization_barrier((ends, local, rates))
    totals = lax.all_gather(lax.all_gather(ends, "core"), "chip").reshape(ranks * 8)
    rank = lax.axis_index(RAD).astype(jnp.int32)[None]
    updated, enclosed = pl.pallas_call(
        spread_kernel,
        out_shape=(
            jax.ShapeDtypeStruct(fields.shape, jnp.float32),
            jax.ShapeDtypeStruct(gravity.shape, jnp.float32),
        ),
        in_specs=specs(smem, smem, smem, vmem, vmem),
        out_specs=specs(vmem, vmem),
        scratch_shapes=[
            pltpu.VMEM((RING * BLOCK, 128), jnp.float32),
            pltpu.VMEM((256, 128), jnp.float32),
            pltpu.VMEM((128, 128), jnp.float32),
        ],
        compiler_params=params,
        name="spread",
    )(rank, rates, totals, local, lines)
    return updated, enclosed


def solution(mesh):
    split = Mesh(mesh.devices.reshape(mesh.shape["az"], -1, 2), ("az",) + RAD)
    placed = (P(None, None, RAD, "az"), P(RAD), P(RAD), P(RAD), P(RAD), P(RAD))
    return jax.shard_map(
        shards,
        mesh=split,
        in_specs=placed,
        out_specs=(P(None, None, RAD, "az"), P(RAD)),
        check_vma=False,
    )
```

```python
import jax
import jax.numpy as jnp
from jax import lax
from jax.experimental import pallas as pl
from jax.experimental.pallas import tpu as pltpu
from jax.sharding import Mesh, PartitionSpec as P

star_mass = 1.0
RAD = ("chip", "core")

ORDER = (0, 1, 3, 2, 4)
RING = 64
GROUPS = 3
ROWS = 96
SPAN = ROWS // GROUPS
HALF = 16
BLOCK = 2 * HALF
PIECES = 2 * RING
PARTS = SPAN // 8
STEP = 32
VMEM_LIMIT = 24 * 1024 * 1024

TILES = ((0, 1, 5), (1, 2, 2))


def iotas():
    lane = lax.broadcasted_iota(jnp.int32, (8, 128), 1)
    line = lax.broadcasted_iota(jnp.int32, (8, 128), 0)
    return lane, line


def windows():
    for side in range(2):
        for layer in range(2):
            for half in range(2):
                yield side, layer, half, BLOCK * (32 * side + 16 * layer + 8 * half) + 31


def pack_kernel(given, fields, packed, cells, lines, shifts, sems, sent):
    lane, line = iotas()
    shift_copy = pltpu.make_async_copy(given, shifts, sems.at[GROUPS * PARTS])
    shift_copy.start()
    copies = {}
    for part, group in sorted(
        ((part, group) for part in range(PARTS) for group in range(GROUPS)),
        key=lambda at: at not in ((0, 0), (PARTS - 1, GROUPS - 1)),
    ):
        rows = pl.ds(SPAN * group + 8 * part, 8)
        copies[part, group] = pltpu.make_async_copy(
            fields.at[:, :, rows, :], cells.at[:, :, rows, :], sems.at[GROUPS * part + group]
        )
        copies[part, group].start()
    arrived = [(0, 0), (PARTS - 1, GROUPS - 1)]
    for at in arrived:
        copies[at].wait()
    shift_copy.wait()
    turned = {}
    for side in range(2):
        row = (ROWS - 1) * (1 - side)
        part = shifts[row] & 127
        for layer in range(2):
            for half in range(2):
                tile = jnp.zeros((8, 128), jnp.float32)
                for place, field in enumerate(ORDER):
                    cell = cells[field, layer, pl.ds(row, 1), pl.ds(128 * half, 128)]
                    tile = jnp.where(line == place, jnp.broadcast_to(cell, (8, 128)), tile)
                turned[side, layer, half] = pltpu.roll(tile, part, 1)
    for side, layer, half, first in windows():
        shift = shifts[(ROWS - 1) * (1 - side)]
        swapped = (lane < (shift & 127)) ^ (shift & 128 != 0) ^ (half == 1)
        lines[pl.ds(first, 8, stride=BLOCK), :] = jnp.where(swapped, turned[side, layer, 1], turned[side, layer, 0])
    blocks = lines.reshape(RING, BLOCK, 128)
    sending = []

    def send(first, count, low, high):
        part = pl.ds(first, count), pl.ds(low, high - low)
        copy = pltpu.make_async_copy(blocks.at[part[0], part[1], :], packed.at[part[0], part[1], :], sent.at[len(sending)])
        copy.start()
        sending.append(copy)

    for part in range(PARTS):
        for group in range(GROUPS):
            if (part, group) not in arrived:
                copies[part, group].wait()
            taken = {}
            for place, field in enumerate(ORDER):
                for layer in range(2):
                    for half in range(2):
                        first = 16 * BLOCK * part + BLOCK * layer + HALF * half + 5 * group + place
                        taken[first] = cells[
                            field, layer, pl.ds(SPAN * group + 8 * part, 8), pl.ds(128 * half, 128)
                        ]
            for first, value in taken.items():
                lines[pl.ds(first, 8, stride=2 * BLOCK), :] = value
        send(16 * part, 16, 0, 8)
        send(16 * part, 16, 16, 32)
    halves = [cells[0, z, :, pl.ds(128 * h, 128)] for z in range(2) for h in range(2)]
    total = (halves[0] + halves[1]) + (halves[2] + halves[3])
    square = jnp.concatenate([total, jnp.zeros((128 - ROWS, 128), jnp.float32)], axis=0)
    mass = jnp.sum(square.T, axis=0, keepdims=True)
    lines[pl.ds(15, RING, stride=BLOCK), :] = jnp.broadcast_to(mass, (RING, 128))
    send(0, RING, 8, 16)
    for copy in sending:
        copy.wait()


def join_kernel(steps, near, tail, ends, begun, moved, rows, twice, sem):
    twice[pl.ds(0, RING), :] = ends[...]
    twice[pl.ds(RING, RING), :] = ends[...]
    rows[...] = tail[...]
    lane = lax.broadcasted_iota(jnp.int32, (RING, 128), 1)
    crossed = lane + 16 * (steps[3] & 8) < (near[0] & 255)
    blocks = near[0] >> 8
    rows[pl.ds(7, RING, stride=8), :] = jnp.where(
        crossed, twice[pl.ds(RING - 1 - blocks, RING), :], twice[pl.ds(RING - blocks, RING), :]
    )
    copy = pltpu.make_async_copy(rows.reshape(RING, 8, 128), moved.at[:, pl.ds(24, 8), :], sem)
    copy.start()
    copy.wait()


def shift_kernel(steps, lines, begun, tail, mass, square):
    lane, line = iotas()
    moved = begun.reshape(RING * BLOCK, 128)
    whole, part, early = [], [], []
    for group in range(GROUPS):
        shift = steps[group]
        whole.append(shift >> 7)
        part.append(shift & 127)
        early.append(lane < part[group])

    def piece_of(piece, tile, group):
        at = pl.multiple_of(((piece - whole[group]) & (PIECES - 1)) * HALF + 8 * tile, 8)
        return lines[pl.ds(at, 8), :]

    def turned(value, group):
        return pltpu.roll(value, part[group], 1)

    def several(step, state):
        before, edges = state
        edges = list(edges)
        first_piece = step * STEP
        loaded = [
            [[piece_of(first_piece + i, tile, group) for group in TILES[tile][:2]] for tile in range(2)]
            for i in range(STEP)
        ]
        values = []
        for i in range(STEP):
            now, made = [], []
            for tile, (first, second, split) in enumerate(TILES):
                a, b = turned(loaded[i][tile][0], first), turned(loaded[i][tile][1], second)
                pa, pb = before[tile]
                made.append(
                    jnp.where(line < split, jnp.where(early[first], pa, a), jnp.where(early[second], pb, b))
                )
                now.append((a, b))
            before = tuple(now)
            values.append(made)
        for i in range(0, STEP, 2):
            ring = step * (STEP // 2) + i // 2
            for tile in range(2):
                both = jnp.where(lane == 127, values[i + 1][tile], values[i][tile])
                edges[tile] = jnp.where(lane >> 1 == ring, pltpu.roll(both, (2 * ring + 1) & 127, 1), edges[tile])
        for i in range(STEP):
            for tile in range(2):
                if i % 2 == 1 and tile == 1:
                    at = pl.multiple_of((first_piece + i) // 2 * 8, 8)
                    tail[pl.ds(at, 8), :] = values[i][tile]
                else:
                    at = pl.multiple_of((first_piece + i) * HALF + 8 * tile, 8)
                    moved[pl.ds(at, 8), :] = values[i][tile]
        return before, tuple(edges)

    before = tuple(
        tuple(turned(piece_of(PIECES - 1, tile, group), group) for group in TILES[tile][:2]) for tile in range(2)
    )
    zero = jnp.zeros((8, 128), jnp.float32)
    state = before, (zero, zero)
    steps_each = PIECES // STEP // 4
    for quarter in range(4):
        state = lax.fori_loop(steps_each * quarter, steps_each * (quarter + 1), several, state)
    _, edges = state
    square[...] = jnp.concatenate([edges[0], edges[1], jnp.zeros((112, 128), jnp.float32)], axis=0).T
    left = square[pl.ds(0, RING, stride=2), :]
    right = square[pl.ds(1, RING, stride=2), :]
    left = jnp.concatenate([left[RING - 1 :], left[: RING - 1]], axis=0)
    right = jnp.concatenate([right[1:], right[:1]], axis=0)
    moved[pl.ds(15, RING, stride=BLOCK), :] = left + pltpu.roll(right, 16, 1)
    parts = lines[pl.ds(15, RING, stride=BLOCK), :]
    mass[...] = jnp.broadcast_to(jnp.sum(parts, axis=0, keepdims=True), (8, 128))


def spread_kernel(rank, rates, totals, local, lines, updated, enclosed, done, ends, square):
    lane, line = iotas()
    here = rank[0]
    base = jnp.float32(star_mass)
    for other in range(totals.shape[0] // 8):
        base = base + jnp.where(other < here, totals[8 * other], 0.0)
    below = 8 * jnp.maximum(here - 1, 0)
    above = 8 * jnp.minimum(here + 1, totals.shape[0] // 8 - 1)
    outer_pull = (
        totals[below + 4] * (base - totals[below + 3]),
        totals[above + 2] * (base + totals[8 * here] + totals[above + 1]),
    )
    enclosed[...] = local[...] + base

    borders = lines[pl.ds(15, RING, stride=BLOCK), :]
    square[pl.ds(0, RING, stride=2), :] = borders
    borders = pltpu.roll(borders, 112, 1)
    square[pl.ds(1, RING, stride=2), :] = jnp.concatenate([borders[1:], borders[:1]], axis=0)
    across = square[...].T
    edges = across[0:8], across[8:16]
    under_edges = tuple(pltpu.roll(value, 1, 0) for value in edges)
    takes = (((line == 1) | (line == 2), (line == 6) | (line == 7)), (None, (line == 3) | (line == 4)))

    def spread(first_rate, row, tile):
        first, second, split = TILES[tile]
        return jnp.where(
            line < split, rates[first_rate + SPAN * first + row], rates[first_rate + SPAN * second + row]
        )

    def pull(row):
        return rates[2 * ROWS + row] * (base + rates[3 * ROWS + row])

    def pulls(row, tile):
        first, second, _ = TILES[tile]
        other = jnp.where(takes[tile][1], pull(SPAN * second + row), 0.0)
        if takes[tile][0] is None:
            return other
        return jnp.where(takes[tile][0], pull(SPAN * first + row), other)

    def source(value, rate):
        return value - rate * pltpu.roll(value, 1, 0)

    def spots():
        return ((tile, layer, half) for tile in range(2) for layer in range(2) for half in range(2))

    def place_of(row, tile, layer, half):
        return pl.multiple_of((2 * row + layer) * BLOCK + HALF * half + 8 * tile, 8)

    def begin(row):
        cells = {spot: lines[pl.ds(place_of(row, *spot), 8), :] for spot in spots()}
        full, partial = [], []
        for tile in range(2):
            az, rad, rate = spread(0, row, tile), spread(ROWS, row, tile), pulls(row, tile)
            keep = 1.0 - 2.0 * (az + rad)
            border = edges[tile] - rate * under_edges[tile]
            for layer in range(2):
                low, high = (source(cells[tile, layer, half], rate) for half in range(2))
                side = pltpu.roll(border, (128 - 4 * row - 2 * layer) & 127, 1)
                low_up, high_up = pltpu.roll(low, 1, 1), pltpu.roll(high, 1, 1)
                low_down, high_down = pltpu.roll(low, 127, 1), pltpu.roll(high, 127, 1)
                low_sum = jnp.where(lane == 0, side, low_up) + jnp.where(lane == 127, high_down, low_down)
                high_sum = jnp.where(lane == 0, low_up, high_up) + jnp.where(lane == 127, side, high_down)
                full += [low, high]
                partial += [keep * low + az * low_sum, keep * high + az * high_sum]
        return full, partial

    def end(row, partial, under, over):
        for tile in range(2):
            rad = spread(ROWS, row, tile)
            for layer in range(2):
                for half in range(2):
                    at = 4 * tile + 2 * layer + half
                    done[pl.ds(place_of(row, tile, layer, half), 8), :] = partial[at] + rad * (under[at] + over[at])

    def outer(side):
        rate = jnp.where(takes[0][0], outer_pull[side], 0.0)
        return [
            source(lines[pl.ds(first, 8, stride=BLOCK), :], rate) for at, _, _, first in windows() if at == side
        ]

    last, last_partial = begin(SPAN - 1)
    full, partial = begin(0)
    turned = [pltpu.roll(value, 5, 0) for value in last]
    under = [jnp.where(line < 5, value, turned[i]) for i, value in enumerate(outer(0))]
    under += [jnp.where(line < 5, turned[i], turned[4 + i]) for i in range(4)]
    turned = [pltpu.roll(value, 3, 0) for value in full]
    over = [jnp.where(line < 3, turned[i], turned[4 + i]) for i in range(4)]
    over += [jnp.where(line < 2, turned[4 + i], pltpu.roll(value, 2, 0)) for i, value in enumerate(outer(1))]
    for i in range(8):
        ends[pl.ds(64 + 8 * i, 8), :] = last[i]
        ends[pl.ds(128 + 8 * i, 8), :] = last_partial[i]
        ends[pl.ds(192 + 8 * i, 8), :] = over[i]

    def kept(first):
        return [ends[pl.ds(first + 8 * i, 8), :] for i in range(8)]

    def rows(step, state):
        under, full, partial = state
        for row in range(30):
            row = 30 * step + row + 1
            over, later = begin(row)
            end(row - 1, partial, under, over)
            under, full, partial = full, over, later
        return under, full, partial

    under, full, partial = lax.fori_loop(0, (SPAN - 2) // 30, rows, (under, full, partial))
    end(SPAN - 2, partial, under, kept(64))
    end(SPAN - 1, kept(128), full, kept(192))
    for place, field in enumerate(ORDER):
        for layer in range(2):
            taken = {}
            for group in range(GROUPS):
                for half in range(2):
                    first = BLOCK * layer + HALF * half + 5 * group + place
                    taken[group, half] = done[pl.ds(first, SPAN, stride=2 * BLOCK), :]
            for (group, half), value in taken.items():
                updated[field, layer, pl.ds(SPAN * group, SPAN), pl.ds(128 * half, 128)] = value


def specs(*kinds):
    return [pl.BlockSpec(memory_space=kind) for kind in kinds]


def shards(fields, shifts, cycle_area, gravity, kappa_az, kappa_rad):
    vmem, smem = pltpu.VMEM, pltpu.SMEM
    params = pltpu.CompilerParams(vmem_limit_bytes=VMEM_LIMIT)
    blocks = jax.ShapeDtypeStruct((RING, BLOCK, 128), jnp.float32)

    def dealt(lines):
        return lax.all_to_all(lines, "az", 0, 0, tiled=True).reshape(RING * BLOCK, 128)

    ranks = lax.axis_size(RAD)
    packed = pl.pallas_call(
        pack_kernel,
        out_shape=blocks,
        in_specs=specs(pltpu.HBM, pltpu.HBM),
        out_specs=specs(pl.ANY)[0],
        scratch_shapes=[
            pltpu.VMEM(fields.shape, jnp.float32),
            pltpu.VMEM((RING * BLOCK, 128), jnp.float32),
            pltpu.SMEM(shifts.shape, jnp.int32),
            pltpu.SemaphoreType.DMA((GROUPS * PARTS + 1,)),
            pltpu.SemaphoreType.DMA((2 * PARTS + 1,)),
        ],
        compiler_params=pltpu.CompilerParams(vmem_limit_bytes=60 * 1024 * 1024),
        name="pack",
    )(shifts, fields)
    whole = dealt(packed)
    place = lax.axis_index("az").astype(jnp.int32)
    mine = lax.dynamic_slice(shifts.reshape(GROUPS, SPAN), (0, place // 2), (GROUPS, 1))[:, 0]
    end = jnp.where(place < RING // 2, shifts[ROWS - 1 :], shifts[:1])
    steps = jnp.concatenate([mine, place[None]])
    rates = jnp.concatenate([kappa_az, kappa_rad, gravity, cycle_area])
    steps, rates = lax.optimization_barrier((steps, rates))
    gravity, cycle_area = rates[2 * ROWS : 3 * ROWS], rates[3 * ROWS :]
    outward = [(q * ranks + i, q * ranks + i + 1) for q in range(RING // 2) for i in range(ranks - 1)]
    inward = [(q * ranks + i + 1, q * ranks + i) for q in range(RING // 2, RING) for i in range(ranks - 1)]
    near = lax.ppermute(end, ("az",) + RAD, outward + inward)
    ends = lax.ppermute(whole.reshape(RING, BLOCK, 128)[:, BLOCK - 1], ("az",) + RAD, outward + inward)
    begun, tail, mass = pl.pallas_call(
        shift_kernel,
        out_shape=(
            blocks,
            jax.ShapeDtypeStruct((RING * 8, 128), jnp.float32),
            jax.ShapeDtypeStruct((8, 128), jnp.float32),
        ),
        in_specs=specs(smem, vmem),
        out_specs=specs(vmem, vmem, vmem),
        scratch_shapes=[pltpu.VMEM((128, 128), jnp.float32)],
        compiler_params=params,
        name="shift",
    )(steps, whole)
    moved = pl.pallas_call(
        join_kernel,
        out_shape=blocks,
        in_specs=specs(smem, smem, vmem, vmem, pl.ANY),
        out_specs=specs(pl.ANY)[0],
        scratch_shapes=[
            pltpu.VMEM((RING * 8, 128), jnp.float32),
            pltpu.VMEM((2 * RING, 128), jnp.float32),
            pltpu.SemaphoreType.DMA,
        ],
        input_output_aliases={4: 0},
        compiler_params=params,
        name="join",
    )(steps, near, tail, ends, begun)
    lines = dealt(moved)

    row_mass = cycle_area * mass[0, :ROWS] / (2.0 * RING * 256)
    row = jnp.arange(ROWS)
    inside = jnp.sum(jnp.where(row[None, :] < row[:, None], row_mass[None, :], 0.0), axis=1)
    local = inside + 0.5 * row_mass
    rates = jnp.concatenate([rates[: 3 * ROWS], local])
    kind, at = jnp.arange(8)[:, None], row[None, :]
    picked = jnp.where((kind == 1) & (at == 0) | (kind == 3) & (at == ROWS - 1), 0.5 * row_mass[None, :], 0.0)
    picked = jnp.where((kind == 2) & (at == 0) | (kind == 4) & (at == ROWS - 1), gravity[None, :], picked)
    ends = jnp.sum(jnp.where(kind == 0, row_mass[None, :], picked), axis=1)
    ends, local, rates = lax.optimization_barrier((ends, local, rates))
    totals = lax.all_gather(lax.all_gather(ends, "core"), "chip").reshape(ranks * 8)
    rank = lax.axis_index(RAD).astype(jnp.int32)[None]
    updated, enclosed = pl.pallas_call(
        spread_kernel,
        out_shape=(
            jax.ShapeDtypeStruct(fields.shape, jnp.float32),
            jax.ShapeDtypeStruct(gravity.shape, jnp.float32),
        ),
        in_specs=specs(smem, smem, smem, vmem, vmem),
        out_specs=specs(vmem, vmem),
        scratch_shapes=[
            pltpu.VMEM((RING * BLOCK, 128), jnp.float32),
            pltpu.VMEM((256, 128), jnp.float32),
            pltpu.VMEM((128, 128), jnp.float32),
        ],
        compiler_params=params,
        name="spread",
    )(rank, rates, totals, local, lines)
    return updated, enclosed


def solution(mesh):
    split = Mesh(mesh.devices.reshape(mesh.shape["az"], -1, 2), ("az",) + RAD)
    placed = (P(None, None, RAD, "az"), P(RAD), P(RAD), P(RAD), P(RAD), P(RAD))
    return jax.shard_map(
        shards,
        mesh=split,
        in_specs=placed,
        out_specs=(P(None, None, RAD, "az"), P(RAD)),
        check_vma=False,
    )
```

```python
import jax
import jax.numpy as jnp
from jax import lax
from jax.experimental import pallas as pl
from jax.experimental.pallas import tpu as pltpu
from jax.sharding import Mesh, PartitionSpec as P

star_mass = 1.0
RAD = ("chip", "core")

ORDER = (0, 1, 3, 2, 4)
RING = 64
GROUPS = 3
ROWS = 96
SPAN = ROWS // GROUPS
HALF = 16
BLOCK = 2 * HALF
PIECES = 2 * RING
PARTS = SPAN // 8
STEP = 32
VMEM_LIMIT = 24 * 1024 * 1024

TILES = ((0, 1, 5), (1, 2, 2))


def iotas():
    lane = lax.broadcasted_iota(jnp.int32, (8, 128), 1)
    line = lax.broadcasted_iota(jnp.int32, (8, 128), 0)
    return lane, line


def windows():
    for side in range(2):
        for layer in range(2):
            for half in range(2):
                yield side, layer, half, BLOCK * (32 * side + 16 * layer + 8 * half) + 31


def pack_kernel(given, fields, packed, cells, lines, shifts, sems, sent):
    lane, line = iotas()
    shift_copy = pltpu.make_async_copy(given, shifts, sems.at[GROUPS * PARTS])
    shift_copy.start()
    copies = {}
    for part, group in sorted(
        ((part, group) for part in range(PARTS) for group in range(GROUPS)),
        key=lambda at: at not in ((0, 0), (PARTS - 1, GROUPS - 1)),
    ):
        rows = pl.ds(SPAN * group + 8 * part, 8)
        copies[part, group] = pltpu.make_async_copy(
            fields.at[:, :, rows, :], cells.at[:, :, rows, :], sems.at[GROUPS * part + group]
        )
        copies[part, group].start()
    arrived = [(0, 0), (PARTS - 1, GROUPS - 1)]
    for at in arrived:
        copies[at].wait()
    shift_copy.wait()
    turned = {}
    for side in range(2):
        row = (ROWS - 1) * (1 - side)
        part = shifts[row] & 127
        for layer in range(2):
            for half in range(2):
                tile = jnp.zeros((8, 128), jnp.float32)
                for place, field in enumerate(ORDER):
                    cell = cells[field, layer, pl.ds(row, 1), pl.ds(128 * half, 128)]
                    tile = jnp.where(line == place, jnp.broadcast_to(cell, (8, 128)), tile)
                turned[side, layer, half] = pltpu.roll(tile, part, 1)
    for side, layer, half, first in windows():
        shift = shifts[(ROWS - 1) * (1 - side)]
        swapped = (lane < (shift & 127)) ^ (shift & 128 != 0) ^ (half == 1)
        lines[pl.ds(first, 8, stride=BLOCK), :] = jnp.where(swapped, turned[side, layer, 1], turned[side, layer, 0])
    blocks = lines.reshape(RING, BLOCK, 128)
    sending = []

    def send(first, count, low, high):
        part = pl.ds(first, count), pl.ds(low, high - low)
        copy = pltpu.make_async_copy(blocks.at[part[0], part[1], :], packed.at[part[0], part[1], :], sent.at[len(sending)])
        copy.start()
        sending.append(copy)

    for part in range(PARTS):
        for group in range(GROUPS):
            if (part, group) not in arrived:
                copies[part, group].wait()
            taken = {}
            for place, field in enumerate(ORDER):
                for layer in range(2):
                    for half in range(2):
                        first = 16 * BLOCK * part + BLOCK * layer + HALF * half + 5 * group + place
                        taken[first] = cells[
                            field, layer, pl.ds(SPAN * group + 8 * part, 8), pl.ds(128 * half, 128)
                        ]
            for first, value in taken.items():
                lines[pl.ds(first, 8, stride=2 * BLOCK), :] = value
        send(16 * part, 16, 0, 8)
        send(16 * part, 16, 16, 32)
    halves = [cells[0, z, :, pl.ds(128 * h, 128)] for z in range(2) for h in range(2)]
    total = (halves[0] + halves[1]) + (halves[2] + halves[3])
    square = jnp.concatenate([total, jnp.zeros((128 - ROWS, 128), jnp.float32)], axis=0)
    mass = jnp.sum(square.T, axis=0, keepdims=True)
    lines[pl.ds(15, RING, stride=BLOCK), :] = jnp.broadcast_to(mass, (RING, 128))
    send(0, RING, 8, 16)
    for copy in sending:
        copy.wait()


def ends_kernel(steps, lines, moved, twice):
    cells = lines[pl.ds(31, RING, stride=BLOCK), :]
    twice[pl.ds(0, RING), :] = cells
    twice[pl.ds(RING, RING), :] = cells
    shift = steps[3]
    lane = lax.broadcasted_iota(jnp.int32, (RING, 128), 1)
    crossed = lane + 16 * (steps[4] & 8) < (shift & 255)
    blocks = shift >> 8
    moved[...] = jnp.where(crossed, twice[pl.ds(RING - 1 - blocks, RING), :], twice[pl.ds(RING - blocks, RING), :])


def join_kernel(brim, tail, ends, begun, moved, rows, sems):
    edges = pltpu.make_async_copy(brim.reshape(RING, 8, 128), moved.at[:, pl.ds(8, 8), :], sems.at[0])
    edges.start()
    rows[...] = tail[...]
    rows[pl.ds(7, RING, stride=8), :] = ends[...]
    last = pltpu.make_async_copy(rows.reshape(RING, 8, 128), moved.at[:, pl.ds(24, 8), :], sems.at[1])
    last.start()
    edges.wait()
    last.wait()


def shift_kernel(steps, lines, begun, brim, tail, mass, moved, square, sems):
    lane, line = iotas()
    blocks = moved.reshape(RING, BLOCK, 128)

    def copies_of(quarter):
        part = pl.ds(quarter * (RING // 4), RING // 4)
        for half in range(2):
            rows = pl.ds(HALF * half, 8)
            yield pltpu.make_async_copy(
                blocks.at[part, rows, :], begun.at[part, rows, :], sems.at[2 * quarter + half]
            )

    whole, part, early = [], [], []
    for group in range(GROUPS):
        shift = steps[group]
        whole.append(shift >> 7)
        part.append(shift & 127)
        early.append(lane < part[group])

    def piece_of(piece, tile, group):
        at = pl.multiple_of(((piece - whole[group]) & (PIECES - 1)) * HALF + 8 * tile, 8)
        return lines[pl.ds(at, 8), :]

    def turned(value, group):
        return pltpu.roll(value, part[group], 1)

    def several(step, state):
        before, edges = state
        edges = list(edges)
        first_piece = step * STEP
        loaded = [
            [[piece_of(first_piece + i, tile, group) for group in TILES[tile][:2]] for tile in range(2)]
            for i in range(STEP)
        ]
        values = []
        for i in range(STEP):
            now, made = [], []
            for tile, (first, second, split) in enumerate(TILES):
                a, b = turned(loaded[i][tile][0], first), turned(loaded[i][tile][1], second)
                pa, pb = before[tile]
                made.append(
                    jnp.where(line < split, jnp.where(early[first], pa, a), jnp.where(early[second], pb, b))
                )
                now.append((a, b))
            before = tuple(now)
            values.append(made)
        for i in range(0, STEP, 2):
            ring = step * (STEP // 2) + i // 2
            for tile in range(2):
                both = jnp.where(lane == 127, values[i + 1][tile], values[i][tile])
                edges[tile] = jnp.where(lane >> 1 == ring, pltpu.roll(both, (2 * ring + 1) & 127, 1), edges[tile])
        for i in range(STEP):
            for tile in range(2):
                if tile == 1:
                    at = pl.multiple_of((first_piece + i) // 2 * 8, 8)
                    (brim, tail)[i % 2][pl.ds(at, 8), :] = values[i][tile]
                else:
                    at = pl.multiple_of((first_piece + i) * HALF, 8)
                    moved[pl.ds(at, 8), :] = values[i][tile]
        return before, tuple(edges)

    before = tuple(
        tuple(turned(piece_of(PIECES - 1, tile, group), group) for group in TILES[tile][:2]) for tile in range(2)
    )
    zero = jnp.zeros((8, 128), jnp.float32)
    state = before, (zero, zero)
    steps_each = PIECES // STEP // 4
    for quarter in range(4):
        state = lax.fori_loop(steps_each * quarter, steps_each * (quarter + 1), several, state)
        for copy in copies_of(quarter):
            copy.start()
    _, edges = state
    square[...] = jnp.concatenate([edges[0], edges[1], jnp.zeros((112, 128), jnp.float32)], axis=0).T
    left = square[pl.ds(0, RING, stride=2), :]
    right = square[pl.ds(1, RING, stride=2), :]
    left = jnp.concatenate([left[RING - 1 :], left[: RING - 1]], axis=0)
    right = jnp.concatenate([right[1:], right[:1]], axis=0)
    brim[pl.ds(7, RING, stride=8), :] = left + pltpu.roll(right, 16, 1)
    parts = lines[pl.ds(15, RING, stride=BLOCK), :]
    mass[...] = jnp.broadcast_to(jnp.sum(parts, axis=0, keepdims=True), (8, 128))
    for quarter in range(4):
        for copy in copies_of(quarter):
            copy.wait()


def spread_kernel(rank, rates, totals, local, lines, updated, enclosed, done, ends, square):
    lane, line = iotas()
    here = rank[0]
    base = jnp.float32(star_mass)
    for other in range(totals.shape[0] // 8):
        base = base + jnp.where(other < here, totals[8 * other], 0.0)
    below = 8 * jnp.maximum(here - 1, 0)
    above = 8 * jnp.minimum(here + 1, totals.shape[0] // 8 - 1)
    outer_pull = (
        totals[below + 4] * (base - totals[below + 3]),
        totals[above + 2] * (base + totals[8 * here] + totals[above + 1]),
    )
    enclosed[...] = local[...] + base

    borders = lines[pl.ds(15, RING, stride=BLOCK), :]
    square[pl.ds(0, RING, stride=2), :] = borders
    borders = pltpu.roll(borders, 112, 1)
    square[pl.ds(1, RING, stride=2), :] = jnp.concatenate([borders[1:], borders[:1]], axis=0)
    across = square[...].T
    edges = across[0:8], across[8:16]
    under_edges = tuple(pltpu.roll(value, 1, 0) for value in edges)
    takes = (((line == 1) | (line == 2), (line == 6) | (line == 7)), (None, (line == 3) | (line == 4)))

    def spread(first_rate, row, tile):
        first, second, split = TILES[tile]
        return jnp.where(
            line < split, rates[first_rate + SPAN * first + row], rates[first_rate + SPAN * second + row]
        )

    def pull(row):
        return rates[2 * ROWS + row] * (base + rates[3 * ROWS + row])

    def pulls(row, tile):
        first, second, _ = TILES[tile]
        other = jnp.where(takes[tile][1], pull(SPAN * second + row), 0.0)
        if takes[tile][0] is None:
            return other
        return jnp.where(takes[tile][0], pull(SPAN * first + row), other)

    def source(value, rate):
        return value - rate * pltpu.roll(value, 1, 0)

    def spots():
        return ((tile, layer, half) for tile in range(2) for layer in range(2) for half in range(2))

    def place_of(row, tile, layer, half):
        return pl.multiple_of((2 * row + layer) * BLOCK + HALF * half + 8 * tile, 8)

    def begin(row):
        cells = {spot: lines[pl.ds(place_of(row, *spot), 8), :] for spot in spots()}
        full, partial = [], []
        for tile in range(2):
            az, rad, rate = spread(0, row, tile), spread(ROWS, row, tile), pulls(row, tile)
            keep = 1.0 - 2.0 * (az + rad)
            border = edges[tile] - rate * under_edges[tile]
            for layer in range(2):
                low, high = (source(cells[tile, layer, half], rate) for half in range(2))
                side = pltpu.roll(border, (128 - 4 * row - 2 * layer) & 127, 1)
                low_up, high_up = pltpu.roll(low, 1, 1), pltpu.roll(high, 1, 1)
                low_down, high_down = pltpu.roll(low, 127, 1), pltpu.roll(high, 127, 1)
                low_sum = jnp.where(lane == 0, side, low_up) + jnp.where(lane == 127, high_down, low_down)
                high_sum = jnp.where(lane == 0, low_up, high_up) + jnp.where(lane == 127, side, high_down)
                full += [low, high]
                partial += [keep * low + az * low_sum, keep * high + az * high_sum]
        return full, partial

    def end(row, partial, under, over):
        for tile in range(2):
            rad = spread(ROWS, row, tile)
            for layer in range(2):
                for half in range(2):
                    at = 4 * tile + 2 * layer + half
                    done[pl.ds(place_of(row, tile, layer, half), 8), :] = partial[at] + rad * (under[at] + over[at])

    def outer(side):
        rate = jnp.where(takes[0][0], outer_pull[side], 0.0)
        return [
            source(lines[pl.ds(first, 8, stride=BLOCK), :], rate) for at, _, _, first in windows() if at == side
        ]

    last, last_partial = begin(SPAN - 1)
    full, partial = begin(0)
    turned = [pltpu.roll(value, 5, 0) for value in last]
    under = [jnp.where(line < 5, value, turned[i]) for i, value in enumerate(outer(0))]
    under += [jnp.where(line < 5, turned[i], turned[4 + i]) for i in range(4)]
    turned = [pltpu.roll(value, 3, 0) for value in full]
    over = [jnp.where(line < 3, turned[i], turned[4 + i]) for i in range(4)]
    over += [jnp.where(line < 2, turned[4 + i], pltpu.roll(value, 2, 0)) for i, value in enumerate(outer(1))]
    for i in range(8):
        ends[pl.ds(64 + 8 * i, 8), :] = last[i]
        ends[pl.ds(128 + 8 * i, 8), :] = last_partial[i]
        ends[pl.ds(192 + 8 * i, 8), :] = over[i]

    def kept(first):
        return [ends[pl.ds(first + 8 * i, 8), :] for i in range(8)]

    def rows(step, state):
        under, full, partial = state
        for row in range(30):
            row = 30 * step + row + 1
            over, later = begin(row)
            end(row - 1, partial, under, over)
            under, full, partial = full, over, later
        return under, full, partial

    under, full, partial = lax.fori_loop(0, (SPAN - 2) // 30, rows, (under, full, partial))
    end(SPAN - 2, partial, under, kept(64))
    end(SPAN - 1, kept(128), full, kept(192))
    for place, field in enumerate(ORDER):
        for layer in range(2):
            taken = {}
            for group in range(GROUPS):
                for half in range(2):
                    first = BLOCK * layer + HALF * half + 5 * group + place
                    taken[group, half] = done[pl.ds(first, SPAN, stride=2 * BLOCK), :]
            for (group, half), value in taken.items():
                updated[field, layer, pl.ds(SPAN * group, SPAN), pl.ds(128 * half, 128)] = value


def specs(*kinds):
    return [pl.BlockSpec(memory_space=kind) for kind in kinds]


def shards(fields, shifts, cycle_area, gravity, kappa_az, kappa_rad):
    vmem, smem = pltpu.VMEM, pltpu.SMEM
    params = pltpu.CompilerParams(vmem_limit_bytes=VMEM_LIMIT)
    blocks = jax.ShapeDtypeStruct((RING, BLOCK, 128), jnp.float32)

    def dealt(lines):
        return lax.all_to_all(lines, "az", 0, 0, tiled=True).reshape(RING * BLOCK, 128)

    ranks = lax.axis_size(RAD)
    packed = pl.pallas_call(
        pack_kernel,
        out_shape=blocks,
        in_specs=specs(pltpu.HBM, pltpu.HBM),
        out_specs=specs(pl.ANY)[0],
        scratch_shapes=[
            pltpu.VMEM(fields.shape, jnp.float32),
            pltpu.VMEM((RING * BLOCK, 128), jnp.float32),
            pltpu.SMEM(shifts.shape, jnp.int32),
            pltpu.SemaphoreType.DMA((GROUPS * PARTS + 1,)),
            pltpu.SemaphoreType.DMA((2 * PARTS + 1,)),
        ],
        compiler_params=pltpu.CompilerParams(vmem_limit_bytes=60 * 1024 * 1024),
        name="pack",
    )(shifts, fields)
    whole = dealt(packed)
    place = lax.axis_index("az").astype(jnp.int32)
    mine = lax.dynamic_slice(shifts.reshape(GROUPS, SPAN), (0, place // 2), (GROUPS, 1))[:, 0]
    end = jnp.where(place < RING // 2, shifts[ROWS - 1 :], shifts[:1])
    steps = jnp.concatenate([mine, end, place[None]])
    rates = jnp.concatenate([kappa_az, kappa_rad, gravity, cycle_area])
    steps, rates = lax.optimization_barrier((steps, rates))
    gravity, cycle_area = rates[2 * ROWS : 3 * ROWS], rates[3 * ROWS :]
    ends = pl.pallas_call(
        ends_kernel,
        out_shape=jax.ShapeDtypeStruct((RING, 128), jnp.float32),
        in_specs=specs(smem, vmem),
        out_specs=specs(vmem)[0],
        scratch_shapes=[pltpu.VMEM((2 * RING, 128), jnp.float32)],
        compiler_params=params,
        name="ends",
    )(steps, whole)
    outward = [(q * ranks + i, q * ranks + i + 1) for q in range(RING // 2) for i in range(ranks - 1)]
    inward = [(q * ranks + i + 1, q * ranks + i) for q in range(RING // 2, RING) for i in range(ranks - 1)]
    ends = lax.ppermute(ends, ("az",) + RAD, outward + inward)
    begun, brim, tail, mass = pl.pallas_call(
        shift_kernel,
        out_shape=(
            blocks,
            jax.ShapeDtypeStruct((RING * 8, 128), jnp.float32),
            jax.ShapeDtypeStruct((RING * 8, 128), jnp.float32),
            jax.ShapeDtypeStruct((8, 128), jnp.float32),
        ),
        in_specs=specs(smem, vmem),
        out_specs=specs(pl.ANY, vmem, vmem, vmem),
        scratch_shapes=[
            pltpu.VMEM((RING * BLOCK, 128), jnp.float32),
            pltpu.VMEM((128, 128), jnp.float32),
            pltpu.SemaphoreType.DMA((8,)),
        ],
        compiler_params=params,
        name="shift",
    )(steps, whole)
    moved = pl.pallas_call(
        join_kernel,
        out_shape=blocks,
        in_specs=specs(vmem, vmem, vmem, pl.ANY),
        out_specs=specs(pl.ANY)[0],
        scratch_shapes=[pltpu.VMEM((RING * 8, 128), jnp.float32), pltpu.SemaphoreType.DMA((2,))],
        input_output_aliases={3: 0},
        compiler_params=params,
        name="join",
    )(brim, tail, ends, begun)
    lines = dealt(moved)

    row_mass = cycle_area * mass[0, :ROWS] / (2.0 * RING * 256)
    row = jnp.arange(ROWS)
    inside = jnp.sum(jnp.where(row[None, :] < row[:, None], row_mass[None, :], 0.0), axis=1)
    local = inside + 0.5 * row_mass
    rates = jnp.concatenate([rates[: 3 * ROWS], local])
    kind, at = jnp.arange(8)[:, None], row[None, :]
    picked = jnp.where((kind == 1) & (at == 0) | (kind == 3) & (at == ROWS - 1), 0.5 * row_mass[None, :], 0.0)
    picked = jnp.where((kind == 2) & (at == 0) | (kind == 4) & (at == ROWS - 1), gravity[None, :], picked)
    ends = jnp.sum(jnp.where(kind == 0, row_mass[None, :], picked), axis=1)
    ends, local, rates = lax.optimization_barrier((ends, local, rates))
    totals = lax.all_gather(lax.all_gather(ends, "core"), "chip").reshape(ranks * 8)
    rank = lax.axis_index(RAD).astype(jnp.int32)[None]
    updated, enclosed = pl.pallas_call(
        spread_kernel,
        out_shape=(
            jax.ShapeDtypeStruct(fields.shape, jnp.float32),
            jax.ShapeDtypeStruct(gravity.shape, jnp.float32),
        ),
        in_specs=specs(smem, smem, smem, vmem, vmem),
        out_specs=specs(vmem, vmem),
        scratch_shapes=[
            pltpu.VMEM((RING * BLOCK, 128), jnp.float32),
            pltpu.VMEM((256, 128), jnp.float32),
            pltpu.VMEM((128, 128), jnp.float32),
        ],
        compiler_params=params,
        name="spread",
    )(rank, rates, totals, local, lines)
    return updated, enclosed


def solution(mesh):
    split = Mesh(mesh.devices.reshape(mesh.shape["az"], -1, 2), ("az",) + RAD)
    placed = (P(None, None, RAD, "az"), P(RAD), P(RAD), P(RAD), P(RAD), P(RAD))
    return jax.shard_map(
        shards,
        mesh=split,
        in_specs=placed,
        out_specs=(P(None, None, RAD, "az"), P(RAD)),
        check_vma=False,
    )
```

```python
import jax
import jax.numpy as jnp
from jax import lax
from jax.experimental import pallas as pl
from jax.experimental.pallas import tpu as pltpu
from jax.sharding import Mesh, PartitionSpec as P

star_mass = 1.0
RAD = ("chip", "core")

ORDER = (0, 1, 3, 2, 4)
RING = 64
GROUPS = 3
ROWS = 96
SPAN = ROWS // GROUPS
HALF = 16
BLOCK = 2 * HALF
PIECES = 2 * RING
PARTS = SPAN // 8
STEP = 32
VMEM_LIMIT = 24 * 1024 * 1024

TILES = ((0, 1, 5), (1, 2, 2))


def iotas():
    lane = lax.broadcasted_iota(jnp.int32, (8, 128), 1)
    line = lax.broadcasted_iota(jnp.int32, (8, 128), 0)
    return lane, line


def windows():
    for side in range(2):
        for layer in range(2):
            for half in range(2):
                yield side, layer, half, BLOCK * (32 * side + 16 * layer + 8 * half) + 31


def pack_kernel(given, fields, packed, cells, lines, shifts, sems, sent):
    lane, line = iotas()
    shift_copy = pltpu.make_async_copy(given, shifts, sems.at[GROUPS * PARTS])
    shift_copy.start()
    copies = {}
    for part, group in sorted(
        ((part, group) for part in range(PARTS) for group in range(GROUPS)),
        key=lambda at: at not in ((0, 0), (PARTS - 1, GROUPS - 1)),
    ):
        rows = pl.ds(SPAN * group + 8 * part, 8)
        copies[part, group] = pltpu.make_async_copy(
            fields.at[:, :, rows, :], cells.at[:, :, rows, :], sems.at[GROUPS * part + group]
        )
        copies[part, group].start()
    arrived = [(0, 0), (PARTS - 1, GROUPS - 1)]
    for at in arrived:
        copies[at].wait()
    shift_copy.wait()
    turned = {}
    for side in range(2):
        row = (ROWS - 1) * (1 - side)
        part = shifts[row] & 127
        for layer in range(2):
            for half in range(2):
                tile = jnp.zeros((8, 128), jnp.float32)
                for place, field in enumerate(ORDER):
                    cell = cells[field, layer, pl.ds(row, 1), pl.ds(128 * half, 128)]
                    tile = jnp.where(line == place, jnp.broadcast_to(cell, (8, 128)), tile)
                turned[side, layer, half] = pltpu.roll(tile, part, 1)
    for side, layer, half, first in windows():
        shift = shifts[(ROWS - 1) * (1 - side)]
        swapped = (lane < (shift & 127)) ^ (shift & 128 != 0) ^ (half == 1)
        lines[pl.ds(first, 8, stride=BLOCK), :] = jnp.where(swapped, turned[side, layer, 1], turned[side, layer, 0])
    blocks = lines.reshape(RING, BLOCK, 128)
    sending = []

    def send(first, count, low, high):
        part = pl.ds(first, count), pl.ds(low, high - low)
        copy = pltpu.make_async_copy(blocks.at[part[0], part[1], :], packed.at[part[0], part[1], :], sent.at[len(sending)])
        copy.start()
        sending.append(copy)

    for part in range(PARTS):
        for group in range(GROUPS):
            if (part, group) not in arrived:
                copies[part, group].wait()
            taken = {}
            for place, field in enumerate(ORDER):
                for layer in range(2):
                    for half in range(2):
                        first = 16 * BLOCK * part + BLOCK * layer + HALF * half + 5 * group + place
                        taken[first] = cells[
                            field, layer, pl.ds(SPAN * group + 8 * part, 8), pl.ds(128 * half, 128)
                        ]
            for first, value in taken.items():
                lines[pl.ds(first, 8, stride=2 * BLOCK), :] = value
        send(16 * part, 16, 0, 8)
        send(16 * part, 16, 16, 32)
    halves = [cells[0, z, :, pl.ds(128 * h, 128)] for z in range(2) for h in range(2)]
    total = (halves[0] + halves[1]) + (halves[2] + halves[3])
    square = jnp.concatenate([total, jnp.zeros((128 - ROWS, 128), jnp.float32)], axis=0)
    mass = jnp.sum(square.T, axis=0, keepdims=True)
    lines[pl.ds(15, RING, stride=BLOCK), :] = jnp.broadcast_to(mass, (RING, 128))
    send(0, RING, 8, 16)
    for copy in sending:
        copy.wait()


def ends_kernel(steps, lines, moved, twice):
    cells = lines[pl.ds(31, RING, stride=BLOCK), :]
    twice[pl.ds(0, RING), :] = cells
    twice[pl.ds(RING, RING), :] = cells
    shift = steps[3]
    lane = lax.broadcasted_iota(jnp.int32, (RING, 128), 1)
    crossed = lane + 16 * (steps[4] & 8) < (shift & 255)
    blocks = shift >> 8
    moved[...] = jnp.where(crossed, twice[pl.ds(RING - 1 - blocks, RING), :], twice[pl.ds(RING - blocks, RING), :])


def join_kernel(tail, ends, begun, moved, rows, sem):
    rows[...] = tail[...]
    rows[pl.ds(7, RING, stride=8), :] = ends[...]
    copy = pltpu.make_async_copy(rows.reshape(RING, 8, 128), moved.at[:, pl.ds(24, 8), :], sem)
    copy.start()
    copy.wait()


def shift_kernel(steps, lines, begun, tail, mass, square):
    lane, line = iotas()
    moved = begun.reshape(RING * BLOCK, 128)
    whole, part, early = [], [], []
    for group in range(GROUPS):
        shift = steps[group]
        whole.append(shift >> 7)
        part.append(shift & 127)
        early.append(lane < part[group])

    def piece_of(piece, tile, group):
        at = pl.multiple_of(((piece - whole[group]) & (PIECES - 1)) * HALF + 8 * tile, 8)
        return lines[pl.ds(at, 8), :]

    def turned(value, group):
        return pltpu.roll(value, part[group], 1)

    def several(step, state):
        before, edges = state
        edges = list(edges)
        first_piece = step * STEP
        loaded = [
            [[piece_of(first_piece + i, tile, group) for group in TILES[tile][:2]] for tile in range(2)]
            for i in range(STEP)
        ]
        values = []
        for i in range(STEP):
            now, made = [], []
            for tile, (first, second, split) in enumerate(TILES):
                a, b = turned(loaded[i][tile][0], first), turned(loaded[i][tile][1], second)
                pa, pb = before[tile]
                made.append(
                    jnp.where(line < split, jnp.where(early[first], pa, a), jnp.where(early[second], pb, b))
                )
                now.append((a, b))
            before = tuple(now)
            values.append(made)
        for i in range(0, STEP, 2):
            ring = step * (STEP // 2) + i // 2
            for tile in range(2):
                both = jnp.where(lane == 127, values[i + 1][tile], values[i][tile])
                edges[tile] = jnp.where(lane >> 1 == ring, pltpu.roll(both, (2 * ring + 1) & 127, 1), edges[tile])
        for i in range(STEP):
            for tile in range(2):
                if i % 2 == 1 and tile == 1:
                    at = pl.multiple_of((first_piece + i) // 2 * 8, 8)
                    tail[pl.ds(at, 8), :] = values[i][tile]
                else:
                    at = pl.multiple_of((first_piece + i) * HALF + 8 * tile, 8)
                    moved[pl.ds(at, 8), :] = values[i][tile]
        return before, tuple(edges)

    before = tuple(
        tuple(turned(piece_of(PIECES - 1, tile, group), group) for group in TILES[tile][:2]) for tile in range(2)
    )
    zero = jnp.zeros((8, 128), jnp.float32)
    state = before, (zero, zero)
    steps_each = PIECES // STEP // 4
    for quarter in range(4):
        state = lax.fori_loop(steps_each * quarter, steps_each * (quarter + 1), several, state)
    _, edges = state
    square[...] = jnp.concatenate([edges[0], edges[1], jnp.zeros((112, 128), jnp.float32)], axis=0).T
    left = square[pl.ds(0, RING, stride=2), :]
    right = square[pl.ds(1, RING, stride=2), :]
    left = jnp.concatenate([left[RING - 1 :], left[: RING - 1]], axis=0)
    right = jnp.concatenate([right[1:], right[:1]], axis=0)
    moved[pl.ds(15, RING, stride=BLOCK), :] = left + pltpu.roll(right, 16, 1)
    parts = lines[pl.ds(15, RING, stride=BLOCK), :]
    mass[...] = jnp.broadcast_to(jnp.sum(parts, axis=0, keepdims=True), (8, 128))


def spread_kernel(rank, rates, totals, local, lines, updated, enclosed, done, ends, square):
    lane, line = iotas()
    here = rank[0]
    base = jnp.float32(star_mass)
    for other in range(totals.shape[0] // 8):
        base = base + jnp.where(other < here, totals[8 * other], 0.0)
    below = 8 * jnp.maximum(here - 1, 0)
    above = 8 * jnp.minimum(here + 1, totals.shape[0] // 8 - 1)
    outer_pull = (
        totals[below + 4] * (base - totals[below + 3]),
        totals[above + 2] * (base + totals[8 * here] + totals[above + 1]),
    )
    enclosed[...] = local[...] + base

    borders = lines[pl.ds(15, RING, stride=BLOCK), :]
    square[pl.ds(0, RING, stride=2), :] = borders
    borders = pltpu.roll(borders, 112, 1)
    square[pl.ds(1, RING, stride=2), :] = jnp.concatenate([borders[1:], borders[:1]], axis=0)
    across = square[...].T
    edges = across[0:8], across[8:16]
    under_edges = tuple(pltpu.roll(value, 1, 0) for value in edges)
    takes = (((line == 1) | (line == 2), (line == 6) | (line == 7)), (None, (line == 3) | (line == 4)))

    def spread(first_rate, row, tile):
        first, second, split = TILES[tile]
        return jnp.where(
            line < split, rates[first_rate + SPAN * first + row], rates[first_rate + SPAN * second + row]
        )

    def pull(row):
        return rates[2 * ROWS + row] * (base + rates[3 * ROWS + row])

    def pulls(row, tile):
        first, second, _ = TILES[tile]
        other = jnp.where(takes[tile][1], pull(SPAN * second + row), 0.0)
        if takes[tile][0] is None:
            return other
        return jnp.where(takes[tile][0], pull(SPAN * first + row), other)

    def source(value, rate):
        return value - rate * pltpu.roll(value, 1, 0)

    def spots():
        return ((tile, layer, half) for tile in range(2) for layer in range(2) for half in range(2))

    def place_of(row, tile, layer, half):
        return pl.multiple_of((2 * row + layer) * BLOCK + HALF * half + 8 * tile, 8)

    def begin(row):
        cells = {spot: lines[pl.ds(place_of(row, *spot), 8), :] for spot in spots()}
        full, partial, rads = [], [], []
        for tile in range(2):
            az, rad, rate = spread(0, row, tile), spread(ROWS, row, tile), pulls(row, tile)
            keep = 1.0 - 2.0 * (az + rad)
            rads.append(rad)
            border = edges[tile] - rate * under_edges[tile]
            for layer in range(2):
                low, high = (source(cells[tile, layer, half], rate) for half in range(2))
                side = pltpu.roll(border, (128 - 4 * row - 2 * layer) & 127, 1)
                low_up, high_up = pltpu.roll(low, 1, 1), pltpu.roll(high, 1, 1)
                low_down, high_down = pltpu.roll(low, 127, 1), pltpu.roll(high, 127, 1)
                low_sum = jnp.where(lane == 0, side, low_up) + jnp.where(lane == 127, high_down, low_down)
                high_sum = jnp.where(lane == 0, low_up, high_up) + jnp.where(lane == 127, side, high_down)
                full += [low, high]
                partial += [keep * low + az * low_sum, keep * high + az * high_sum]
        return full, partial, rads

    def end(row, partial, under, over, rads):
        for tile in range(2):
            rad = rads[tile]
            for layer in range(2):
                for half in range(2):
                    at = 4 * tile + 2 * layer + half
                    done[pl.ds(place_of(row, tile, layer, half), 8), :] = partial[at] + rad * (under[at] + over[at])

    def outer(side):
        rate = jnp.where(takes[0][0], outer_pull[side], 0.0)
        return [
            source(lines[pl.ds(first, 8, stride=BLOCK), :], rate) for at, _, _, first in windows() if at == side
        ]

    last, last_partial, last_rads = begin(SPAN - 1)
    full, partial, rads = begin(0)
    turned = [pltpu.roll(value, 5, 0) for value in last]
    under = [jnp.where(line < 5, value, turned[i]) for i, value in enumerate(outer(0))]
    under += [jnp.where(line < 5, turned[i], turned[4 + i]) for i in range(4)]
    turned = [pltpu.roll(value, 3, 0) for value in full]
    over = [jnp.where(line < 3, turned[i], turned[4 + i]) for i in range(4)]
    over += [jnp.where(line < 2, turned[4 + i], pltpu.roll(value, 2, 0)) for i, value in enumerate(outer(1))]
    for i in range(8):
        ends[pl.ds(64 + 8 * i, 8), :] = last[i]
        ends[pl.ds(128 + 8 * i, 8), :] = last_partial[i]
        ends[pl.ds(192 + 8 * i, 8), :] = over[i]

    def kept(first):
        return [ends[pl.ds(first + 8 * i, 8), :] for i in range(8)]

    def rows(step, state):
        under, full, partial, rads = state
        for row in range(30):
            row = 30 * step + row + 1
            over, later, coming = begin(row)
            end(row - 1, partial, under, over, rads)
            under, full, partial, rads = full, over, later, coming
        return under, full, partial, rads

    under, full, partial, rads = lax.fori_loop(0, (SPAN - 2) // 30, rows, (under, full, partial, rads))
    end(SPAN - 2, partial, under, kept(64), rads)
    end(SPAN - 1, kept(128), full, kept(192), last_rads)
    for place, field in enumerate(ORDER):
        for layer in range(2):
            taken = {}
            for group in range(GROUPS):
                for half in range(2):
                    first = BLOCK * layer + HALF * half + 5 * group + place
                    taken[group, half] = done[pl.ds(first, SPAN, stride=2 * BLOCK), :]
            for (group, half), value in taken.items():
                updated[field, layer, pl.ds(SPAN * group, SPAN), pl.ds(128 * half, 128)] = value


def specs(*kinds):
    return [pl.BlockSpec(memory_space=kind) for kind in kinds]


def shards(fields, shifts, cycle_area, gravity, kappa_az, kappa_rad):
    vmem, smem = pltpu.VMEM, pltpu.SMEM
    params = pltpu.CompilerParams(vmem_limit_bytes=VMEM_LIMIT)
    blocks = jax.ShapeDtypeStruct((RING, BLOCK, 128), jnp.float32)

    def dealt(lines):
        return lax.all_to_all(lines, "az", 0, 0, tiled=True).reshape(RING * BLOCK, 128)

    ranks = lax.axis_size(RAD)
    packed = pl.pallas_call(
        pack_kernel,
        out_shape=blocks,
        in_specs=specs(pltpu.HBM, pltpu.HBM),
        out_specs=specs(pl.ANY)[0],
        scratch_shapes=[
            pltpu.VMEM(fields.shape, jnp.float32),
            pltpu.VMEM((RING * BLOCK, 128), jnp.float32),
            pltpu.SMEM(shifts.shape, jnp.int32),
            pltpu.SemaphoreType.DMA((GROUPS * PARTS + 1,)),
            pltpu.SemaphoreType.DMA((2 * PARTS + 1,)),
        ],
        compiler_params=pltpu.CompilerParams(vmem_limit_bytes=60 * 1024 * 1024),
        name="pack",
    )(shifts, fields)
    whole = dealt(packed)
    place = lax.axis_index("az").astype(jnp.int32)
    mine = lax.dynamic_slice(shifts.reshape(GROUPS, SPAN), (0, place // 2), (GROUPS, 1))[:, 0]
    end = jnp.where(place < RING // 2, shifts[ROWS - 1 :], shifts[:1])
    steps = jnp.concatenate([mine, end, place[None]])
    rates = jnp.concatenate([kappa_az, kappa_rad, gravity, cycle_area])
    steps, rates = lax.optimization_barrier((steps, rates))
    gravity, cycle_area = rates[2 * ROWS : 3 * ROWS], rates[3 * ROWS :]
    ends = pl.pallas_call(
        ends_kernel,
        out_shape=jax.ShapeDtypeStruct((RING, 128), jnp.float32),
        in_specs=specs(smem, vmem),
        out_specs=specs(vmem)[0],
        scratch_shapes=[pltpu.VMEM((2 * RING, 128), jnp.float32)],
        compiler_params=params,
        name="ends",
    )(steps, whole)
    outward = [(q * ranks + i, q * ranks + i + 1) for q in range(RING // 2) for i in range(ranks - 1)]
    inward = [(q * ranks + i + 1, q * ranks + i) for q in range(RING // 2, RING) for i in range(ranks - 1)]
    ends = lax.ppermute(ends, ("az",) + RAD, outward + inward)
    begun, tail, mass = pl.pallas_call(
        shift_kernel,
        out_shape=(
            blocks,
            jax.ShapeDtypeStruct((RING * 8, 128), jnp.float32),
            jax.ShapeDtypeStruct((8, 128), jnp.float32),
        ),
        in_specs=specs(smem, vmem),
        out_specs=specs(vmem, vmem, vmem),
        scratch_shapes=[pltpu.VMEM((128, 128), jnp.float32)],
        compiler_params=params,
        name="shift",
    )(steps, whole)
    moved = pl.pallas_call(
        join_kernel,
        out_shape=blocks,
        in_specs=specs(vmem, vmem, pl.ANY),
        out_specs=specs(pl.ANY)[0],
        scratch_shapes=[pltpu.VMEM((RING * 8, 128), jnp.float32), pltpu.SemaphoreType.DMA],
        input_output_aliases={2: 0},
        compiler_params=params,
        name="join",
    )(tail, ends, begun)
    lines = dealt(moved)

    row_mass = cycle_area * mass[0, :ROWS] / (2.0 * RING * 256)
    row = jnp.arange(ROWS)
    inside = jnp.sum(jnp.where(row[None, :] < row[:, None], row_mass[None, :], 0.0), axis=1)
    local = inside + 0.5 * row_mass
    rates = jnp.concatenate([rates[: 3 * ROWS], local])
    kind, at = jnp.arange(8)[:, None], row[None, :]
    picked = jnp.where((kind == 1) & (at == 0) | (kind == 3) & (at == ROWS - 1), 0.5 * row_mass[None, :], 0.0)
    picked = jnp.where((kind == 2) & (at == 0) | (kind == 4) & (at == ROWS - 1), gravity[None, :], picked)
    ends = jnp.sum(jnp.where(kind == 0, row_mass[None, :], picked), axis=1)
    ends, local, rates = lax.optimization_barrier((ends, local, rates))
    totals = lax.all_gather(lax.all_gather(ends, "core"), "chip").reshape(ranks * 8)
    rank = lax.axis_index(RAD).astype(jnp.int32)[None]
    updated, enclosed = pl.pallas_call(
        spread_kernel,
        out_shape=(
            jax.ShapeDtypeStruct(fields.shape, jnp.float32),
            jax.ShapeDtypeStruct(gravity.shape, jnp.float32),
        ),
        in_specs=specs(smem, smem, smem, vmem, vmem),
        out_specs=specs(vmem, vmem),
        scratch_shapes=[
            pltpu.VMEM((RING * BLOCK, 128), jnp.float32),
            pltpu.VMEM((256, 128), jnp.float32),
            pltpu.VMEM((128, 128), jnp.float32),
        ],
        compiler_params=params,
        name="spread",
    )(rank, rates, totals, local, lines)
    return updated, enclosed


def solution(mesh):
    split = Mesh(mesh.devices.reshape(mesh.shape["az"], -1, 2), ("az",) + RAD)
    placed = (P(None, None, RAD, "az"), P(RAD), P(RAD), P(RAD), P(RAD), P(RAD))
    return jax.shard_map(
        shards,
        mesh=split,
        in_specs=placed,
        out_specs=(P(None, None, RAD, "az"), P(RAD)),
        check_vma=False,
    )
```

```python
import jax
import jax.numpy as jnp
from jax import lax
from jax.experimental import pallas as pl
from jax.experimental.pallas import tpu as pltpu
from jax.sharding import Mesh, PartitionSpec as P

star_mass = 1.0
RAD = ("chip", "core")

ORDER = (0, 1, 3, 2, 4)
RING = 64
GROUPS = 3
ROWS = 96
SPAN = ROWS // GROUPS
HALF = 16
BLOCK = 2 * HALF
PIECES = 2 * RING
PARTS = SPAN // 8
STEP = 32
VMEM_LIMIT = 24 * 1024 * 1024

TILES = ((0, 1, 5), (1, 2, 2))


def iotas():
    lane = lax.broadcasted_iota(jnp.int32, (8, 128), 1)
    line = lax.broadcasted_iota(jnp.int32, (8, 128), 0)
    return lane, line


def windows():
    for side in range(2):
        for layer in range(2):
            for half in range(2):
                yield side, layer, half, BLOCK * (32 * side + 16 * layer + 8 * half) + 31


def pack_kernel(given, fields, packed, cells, lines, shifts, sems, sent):
    lane, line = iotas()
    shift_copy = pltpu.make_async_copy(given, shifts, sems.at[GROUPS * PARTS])
    shift_copy.start()
    density = pltpu.make_async_copy(fields.at[0], cells.at[0], sems.at[GROUPS * PARTS + 1])
    density.start()
    copies = {}
    for part, group in sorted(
        ((part, group) for part in range(PARTS) for group in range(GROUPS)),
        key=lambda at: at not in ((0, 0), (PARTS - 1, GROUPS - 1)),
    ):
        rows = pl.ds(SPAN * group + 8 * part, 8)
        copies[part, group] = pltpu.make_async_copy(
            fields.at[pl.ds(1, 4), :, rows, :], cells.at[pl.ds(1, 4), :, rows, :], sems.at[GROUPS * part + group]
        )
        copies[part, group].start()
    density.wait()
    halves = [cells[0, z, :, pl.ds(128 * h, 128)] for z in range(2) for h in range(2)]
    total = (halves[0] + halves[1]) + (halves[2] + halves[3])
    square = jnp.concatenate([total, jnp.zeros((128 - ROWS, 128), jnp.float32)], axis=0)
    mass = jnp.sum(square.T, axis=0, keepdims=True)
    lines[pl.ds(15, RING, stride=BLOCK), :] = jnp.broadcast_to(mass, (RING, 128))
    arrived = [(0, 0), (PARTS - 1, GROUPS - 1)]
    for at in arrived:
        copies[at].wait()
    shift_copy.wait()
    turned = {}
    for side in range(2):
        row = (ROWS - 1) * (1 - side)
        part = shifts[row] & 127
        for layer in range(2):
            for half in range(2):
                tile = jnp.zeros((8, 128), jnp.float32)
                for place, field in enumerate(ORDER):
                    cell = cells[field, layer, pl.ds(row, 1), pl.ds(128 * half, 128)]
                    tile = jnp.where(line == place, jnp.broadcast_to(cell, (8, 128)), tile)
                turned[side, layer, half] = pltpu.roll(tile, part, 1)
    for side, layer, half, first in windows():
        shift = shifts[(ROWS - 1) * (1 - side)]
        swapped = (lane < (shift & 127)) ^ (shift & 128 != 0) ^ (half == 1)
        lines[pl.ds(first, 8, stride=BLOCK), :] = jnp.where(swapped, turned[side, layer, 1], turned[side, layer, 0])
    blocks = lines.reshape(RING, BLOCK, 128)
    sending = []

    def send(first, count, low, high):
        part = pl.ds(first, count), pl.ds(low, high - low)
        copy = pltpu.make_async_copy(blocks.at[part[0], part[1], :], packed.at[part[0], part[1], :], sent.at[len(sending)])
        copy.start()
        sending.append(copy)

    for part in range(PARTS):
        for group in range(GROUPS):
            if (part, group) not in arrived:
                copies[part, group].wait()
            taken = {}
            for place, field in enumerate(ORDER):
                for layer in range(2):
                    for half in range(2):
                        first = 16 * BLOCK * part + BLOCK * layer + HALF * half + 5 * group + place
                        taken[first] = cells[
                            field, layer, pl.ds(SPAN * group + 8 * part, 8), pl.ds(128 * half, 128)
                        ]
            for first, value in taken.items():
                lines[pl.ds(first, 8, stride=2 * BLOCK), :] = value
        send(16 * part, 16, 0, 32)
    for copy in sending:
        copy.wait()


def ends_kernel(steps, lines, moved, twice):
    cells = lines[pl.ds(31, RING, stride=BLOCK), :]
    twice[pl.ds(0, RING), :] = cells
    twice[pl.ds(RING, RING), :] = cells
    shift = steps[3]
    lane = lax.broadcasted_iota(jnp.int32, (RING, 128), 1)
    crossed = lane + 16 * (steps[4] & 8) < (shift & 255)
    blocks = shift >> 8
    moved[...] = jnp.where(crossed, twice[pl.ds(RING - 1 - blocks, RING), :], twice[pl.ds(RING - blocks, RING), :])


def join_kernel(tail, ends, begun, moved, rows, sem):
    rows[...] = tail[...]
    rows[pl.ds(7, RING, stride=8), :] = ends[...]
    copy = pltpu.make_async_copy(rows.reshape(RING, 8, 128), moved.at[:, pl.ds(24, 8), :], sem)
    copy.start()
    copy.wait()


def shift_kernel(steps, lines, begun, tail, mass, square):
    lane, line = iotas()
    moved = begun.reshape(RING * BLOCK, 128)
    whole, part, early = [], [], []
    for group in range(GROUPS):
        shift = steps[group]
        whole.append(shift >> 7)
        part.append(shift & 127)
        early.append(lane < part[group])

    def piece_of(piece, tile, group):
        at = pl.multiple_of(((piece - whole[group]) & (PIECES - 1)) * HALF + 8 * tile, 8)
        return lines[pl.ds(at, 8), :]

    def turned(value, group):
        return pltpu.roll(value, part[group], 1)

    def several(step, state):
        before, edges = state
        edges = list(edges)
        first_piece = step * STEP
        loaded = [
            [[piece_of(first_piece + i, tile, group) for group in TILES[tile][:2]] for tile in range(2)]
            for i in range(STEP)
        ]
        values = []
        for i in range(STEP):
            now, made = [], []
            for tile, (first, second, split) in enumerate(TILES):
                a, b = turned(loaded[i][tile][0], first), turned(loaded[i][tile][1], second)
                pa, pb = before[tile]
                made.append(
                    jnp.where(line < split, jnp.where(early[first], pa, a), jnp.where(early[second], pb, b))
                )
                now.append((a, b))
            before = tuple(now)
            values.append(made)
        for i in range(0, STEP, 2):
            ring = step * (STEP // 2) + i // 2
            for tile in range(2):
                both = jnp.where(lane == 127, values[i + 1][tile], values[i][tile])
                edges[tile] = jnp.where(lane >> 1 == ring, pltpu.roll(both, (2 * ring + 1) & 127, 1), edges[tile])
        for i in range(STEP):
            for tile in range(2):
                if i % 2 == 1 and tile == 1:
                    at = pl.multiple_of((first_piece + i) // 2 * 8, 8)
                    tail[pl.ds(at, 8), :] = values[i][tile]
                else:
                    at = pl.multiple_of((first_piece + i) * HALF + 8 * tile, 8)
                    moved[pl.ds(at, 8), :] = values[i][tile]
        return before, tuple(edges)

    before = tuple(
        tuple(turned(piece_of(PIECES - 1, tile, group), group) for group in TILES[tile][:2]) for tile in range(2)
    )
    zero = jnp.zeros((8, 128), jnp.float32)
    state = before, (zero, zero)
    steps_each = PIECES // STEP // 4
    for quarter in range(4):
        state = lax.fori_loop(steps_each * quarter, steps_each * (quarter + 1), several, state)
    _, edges = state
    square[...] = jnp.concatenate([edges[0], edges[1], jnp.zeros((112, 128), jnp.float32)], axis=0).T
    left = square[pl.ds(0, RING, stride=2), :]
    right = square[pl.ds(1, RING, stride=2), :]
    left = jnp.concatenate([left[RING - 1 :], left[: RING - 1]], axis=0)
    right = jnp.concatenate([right[1:], right[:1]], axis=0)
    moved[pl.ds(15, RING, stride=BLOCK), :] = left + pltpu.roll(right, 16, 1)
    parts = lines[pl.ds(15, RING, stride=BLOCK), :]
    mass[...] = jnp.broadcast_to(jnp.sum(parts, axis=0, keepdims=True), (8, 128))


def spread_kernel(rank, rates, totals, local, lines, updated, enclosed, done, ends, square):
    lane, line = iotas()
    here = rank[0]
    base = jnp.float32(star_mass)
    for other in range(totals.shape[0] // 8):
        base = base + jnp.where(other < here, totals[8 * other], 0.0)
    below = 8 * jnp.maximum(here - 1, 0)
    above = 8 * jnp.minimum(here + 1, totals.shape[0] // 8 - 1)
    outer_pull = (
        totals[below + 4] * (base - totals[below + 3]),
        totals[above + 2] * (base + totals[8 * here] + totals[above + 1]),
    )
    enclosed[...] = local[...] + base

    borders = lines[pl.ds(15, RING, stride=BLOCK), :]
    square[pl.ds(0, RING, stride=2), :] = borders
    borders = pltpu.roll(borders, 112, 1)
    square[pl.ds(1, RING, stride=2), :] = jnp.concatenate([borders[1:], borders[:1]], axis=0)
    across = square[...].T
    edges = across[0:8], across[8:16]
    under_edges = tuple(pltpu.roll(value, 1, 0) for value in edges)
    takes = (((line == 1) | (line == 2), (line == 6) | (line == 7)), (None, (line == 3) | (line == 4)))

    def spread(first_rate, row, tile):
        first, second, split = TILES[tile]
        return jnp.where(
            line < split, rates[first_rate + SPAN * first + row], rates[first_rate + SPAN * second + row]
        )

    def pull(row):
        return rates[2 * ROWS + row] * (base + rates[3 * ROWS + row])

    def pulls(row, tile):
        first, second, _ = TILES[tile]
        other = jnp.where(takes[tile][1], pull(SPAN * second + row), 0.0)
        if takes[tile][0] is None:
            return other
        return jnp.where(takes[tile][0], pull(SPAN * first + row), other)

    def source(value, rate):
        return value - rate * pltpu.roll(value, 1, 0)

    def spots():
        return ((tile, layer, half) for tile in range(2) for layer in range(2) for half in range(2))

    def place_of(row, tile, layer, half):
        return pl.multiple_of((2 * row + layer) * BLOCK + HALF * half + 8 * tile, 8)

    def begin(row):
        cells = {spot: lines[pl.ds(place_of(row, *spot), 8), :] for spot in spots()}
        full, partial = [], []
        for tile in range(2):
            az, rad, rate = spread(0, row, tile), spread(ROWS, row, tile), pulls(row, tile)
            keep = 1.0 - 2.0 * (az + rad)
            border = edges[tile] - rate * under_edges[tile]
            for layer in range(2):
                low, high = (source(cells[tile, layer, half], rate) for half in range(2))
                side = pltpu.roll(border, (128 - 4 * row - 2 * layer) & 127, 1)
                low_up, high_up = pltpu.roll(low, 1, 1), pltpu.roll(high, 1, 1)
                low_down, high_down = pltpu.roll(low, 127, 1), pltpu.roll(high, 127, 1)
                low_sum = jnp.where(lane == 0, side, low_up) + jnp.where(lane == 127, high_down, low_down)
                high_sum = jnp.where(lane == 0, low_up, high_up) + jnp.where(lane == 127, side, high_down)
                full += [low, high]
                partial += [keep * low + az * low_sum, keep * high + az * high_sum]
        return full, partial

    def end(row, partial, under, over):
        for tile in range(2):
            rad = spread(ROWS, row, tile)
            for layer in range(2):
                for half in range(2):
                    at = 4 * tile + 2 * layer + half
                    done[pl.ds(place_of(row, tile, layer, half), 8), :] = partial[at] + rad * (under[at] + over[at])

    def outer(side):
        rate = jnp.where(takes[0][0], outer_pull[side], 0.0)
        return [
            source(lines[pl.ds(first, 8, stride=BLOCK), :], rate) for at, _, _, first in windows() if at == side
        ]

    last, last_partial = begin(SPAN - 1)
    full, partial = begin(0)
    turned = [pltpu.roll(value, 5, 0) for value in last]
    under = [jnp.where(line < 5, value, turned[i]) for i, value in enumerate(outer(0))]
    under += [jnp.where(line < 5, turned[i], turned[4 + i]) for i in range(4)]
    turned = [pltpu.roll(value, 3, 0) for value in full]
    over = [jnp.where(line < 3, turned[i], turned[4 + i]) for i in range(4)]
    over += [jnp.where(line < 2, turned[4 + i], pltpu.roll(value, 2, 0)) for i, value in enumerate(outer(1))]
    for i in range(8):
        ends[pl.ds(64 + 8 * i, 8), :] = last[i]
        ends[pl.ds(128 + 8 * i, 8), :] = last_partial[i]
        ends[pl.ds(192 + 8 * i, 8), :] = over[i]

    def kept(first):
        return [ends[pl.ds(first + 8 * i, 8), :] for i in range(8)]

    def rows(step, state):
        under, full, partial = state
        for row in range(30):
            row = 30 * step + row + 1
            over, later = begin(row)
            end(row - 1, partial, under, over)
            under, full, partial = full, over, later
        return under, full, partial

    under, full, partial = lax.fori_loop(0, (SPAN - 2) // 30, rows, (under, full, partial))
    end(SPAN - 2, partial, under, kept(64))
    end(SPAN - 1, kept(128), full, kept(192))
    for place, field in enumerate(ORDER):
        for layer in range(2):
            taken = {}
            for group in range(GROUPS):
                for half in range(2):
                    first = BLOCK * layer + HALF * half + 5 * group + place
                    taken[group, half] = done[pl.ds(first, SPAN, stride=2 * BLOCK), :]
            for (group, half), value in taken.items():
                updated[field, layer, pl.ds(SPAN * group, SPAN), pl.ds(128 * half, 128)] = value


def specs(*kinds):
    return [pl.BlockSpec(memory_space=kind) for kind in kinds]


def shards(fields, shifts, cycle_area, gravity, kappa_az, kappa_rad):
    vmem, smem = pltpu.VMEM, pltpu.SMEM
    params = pltpu.CompilerParams(vmem_limit_bytes=VMEM_LIMIT)
    blocks = jax.ShapeDtypeStruct((RING, BLOCK, 128), jnp.float32)

    def dealt(lines):
        return lax.all_to_all(lines, "az", 0, 0, tiled=True).reshape(RING * BLOCK, 128)

    ranks = lax.axis_size(RAD)
    packed = pl.pallas_call(
        pack_kernel,
        out_shape=blocks,
        in_specs=specs(pltpu.HBM, pltpu.HBM),
        out_specs=specs(pl.ANY)[0],
        scratch_shapes=[
            pltpu.VMEM(fields.shape, jnp.float32),
            pltpu.VMEM((RING * BLOCK, 128), jnp.float32),
            pltpu.SMEM(shifts.shape, jnp.int32),
            pltpu.SemaphoreType.DMA((GROUPS * PARTS + 2,)),
            pltpu.SemaphoreType.DMA((PARTS,)),
        ],
        compiler_params=pltpu.CompilerParams(vmem_limit_bytes=60 * 1024 * 1024),
        name="pack",
    )(shifts, fields)
    whole = dealt(packed)
    place = lax.axis_index("az").astype(jnp.int32)
    mine = lax.dynamic_slice(shifts.reshape(GROUPS, SPAN), (0, place // 2), (GROUPS, 1))[:, 0]
    end = jnp.where(place < RING // 2, shifts[ROWS - 1 :], shifts[:1])
    steps = jnp.concatenate([mine, end, place[None]])
    rates = jnp.concatenate([kappa_az, kappa_rad, gravity, cycle_area])
    steps, rates = lax.optimization_barrier((steps, rates))
    gravity, cycle_area = rates[2 * ROWS : 3 * ROWS], rates[3 * ROWS :]
    ends = pl.pallas_call(
        ends_kernel,
        out_shape=jax.ShapeDtypeStruct((RING, 128), jnp.float32),
        in_specs=specs(smem, vmem),
        out_specs=specs(vmem)[0],
        scratch_shapes=[pltpu.VMEM((2 * RING, 128), jnp.float32)],
        compiler_params=params,
        name="ends",
    )(steps, whole)
    outward = [(q * ranks + i, q * ranks + i + 1) for q in range(RING // 2) for i in range(ranks - 1)]
    inward = [(q * ranks + i + 1, q * ranks + i) for q in range(RING // 2, RING) for i in range(ranks - 1)]
    ends = lax.ppermute(ends, ("az",) + RAD, outward + inward)
    begun, tail, mass = pl.pallas_call(
        shift_kernel,
        out_shape=(
            blocks,
            jax.ShapeDtypeStruct((RING * 8, 128), jnp.float32),
            jax.ShapeDtypeStruct((8, 128), jnp.float32),
        ),
        in_specs=specs(smem, vmem),
        out_specs=specs(vmem, vmem, vmem),
        scratch_shapes=[pltpu.VMEM((128, 128), jnp.float32)],
        compiler_params=params,
        name="shift",
    )(steps, whole)
    moved = pl.pallas_call(
        join_kernel,
        out_shape=blocks,
        in_specs=specs(vmem, vmem, pl.ANY),
        out_specs=specs(pl.ANY)[0],
        scratch_shapes=[pltpu.VMEM((RING * 8, 128), jnp.float32), pltpu.SemaphoreType.DMA],
        input_output_aliases={2: 0},
        compiler_params=params,
        name="join",
    )(tail, ends, begun)
    lines = dealt(moved)

    row_mass = cycle_area * mass[0, :ROWS] / (2.0 * RING * 256)
    row = jnp.arange(ROWS)
    inside = jnp.sum(jnp.where(row[None, :] < row[:, None], row_mass[None, :], 0.0), axis=1)
    local = inside + 0.5 * row_mass
    rates = jnp.concatenate([rates[: 3 * ROWS], local])
    kind, at = jnp.arange(8)[:, None], row[None, :]
    picked = jnp.where((kind == 1) & (at == 0) | (kind == 3) & (at == ROWS - 1), 0.5 * row_mass[None, :], 0.0)
    picked = jnp.where((kind == 2) & (at == 0) | (kind == 4) & (at == ROWS - 1), gravity[None, :], picked)
    ends = jnp.sum(jnp.where(kind == 0, row_mass[None, :], picked), axis=1)
    ends, local, rates = lax.optimization_barrier((ends, local, rates))
    totals = lax.all_gather(lax.all_gather(ends, "core"), "chip").reshape(ranks * 8)
    rank = lax.axis_index(RAD).astype(jnp.int32)[None]
    updated, enclosed = pl.pallas_call(
        spread_kernel,
        out_shape=(
            jax.ShapeDtypeStruct(fields.shape, jnp.float32),
            jax.ShapeDtypeStruct(gravity.shape, jnp.float32),
        ),
        in_specs=specs(smem, smem, smem, vmem, vmem),
        out_specs=specs(vmem, vmem),
        scratch_shapes=[
            pltpu.VMEM((RING * BLOCK, 128), jnp.float32),
            pltpu.VMEM((256, 128), jnp.float32),
            pltpu.VMEM((128, 128), jnp.float32),
        ],
        compiler_params=params,
        name="spread",
    )(rank, rates, totals, local, lines)
    return updated, enclosed


def solution(mesh):
    split = Mesh(mesh.devices.reshape(mesh.shape["az"], -1, 2), ("az",) + RAD)
    placed = (P(None, None, RAD, "az"), P(RAD), P(RAD), P(RAD), P(RAD), P(RAD))
    return jax.shard_map(
        shards,
        mesh=split,
        in_specs=placed,
        out_specs=(P(None, None, RAD, "az"), P(RAD)),
        check_vma=False,
    )
```
